32 devices in a mesh: member: 2 (over x), patch: 8 (over z, y), feat: 2 (over core).
Axes of the slice: x: 2, y: 2, z: 4, core: 2. Of those that a mesh axis runs over, the one named last changes fastest.
Arguments:
- node_latent: bfloat16 [10240, 512], P(('member', 'patch')), parts along dimension 0, may hold values from -6 to 6
- edge_latent: bfloat16 [65536, 512], P(('member', 'patch')), parts along dimension 0, may hold values from -6 to 6
- edge_senders: int32 [65536], P(('member', 'patch')), parts along dimension 0, may hold values from 0 to 1151
- edge_receivers: int32 [65536], P(('member', 'patch')), parts along dimension 0, may hold values from 0 to 1151
- halo_rows: int32 [32, 128], P(('member', 'patch')), parts along dimension 0, may hold values from 0 to 639
- coarse_rows: int32 [512], P(('member', 'patch')), parts along dimension 0, may hold values from 0 to 639
- edge_counts: int32 [16], P(('member', 'patch')), parts along dimension 0, may hold values from 1024 to 4096, as said below
- edge_w1: bfloat16 [1536, 512], P(None, 'feat'), may hold values from -0.15625 to 0.15625
- edge_w2: bfloat16 [512, 512], P('feat'), may hold values from -0.25 to 0.25
- edge_gain: bfloat16 [512], replicated, may hold values from 0.099609375 to 1.8984375
- node_w1: bfloat16 [1024, 512], P(None, 'feat'), may hold values from -0.1875 to 0.1875
- node_w2: bfloat16 [512, 512], P('feat'), may hold values from -0.25 to 0.25
- node_gain: bfloat16 [512], replicated, may hold values from 0.099609375 to 1.8984375
Outputs:
- nodes_out: bfloat16 [10240, 512], P(('member', 'patch'), 'feat'), parts along dimension 0
- edges_out: bfloat16 [65536, 512], P(('member', 'patch'), 'feat'), parts along dimension 0
The draws below stay inside these ranges and needn't reach their ends.
There are 2 independent parts, one for each index of `member`. The reference program is written for one: setup_inputs(seed, part) draws one part's arguments, and reference() takes and returns one part's arrays. A program takes and returns all parts, laid end to end along the dimension named above; an argument that names none is the same for every part. Nothing has to cross between parts.
Inputs may be any that keep to these rules, and one draw needn't show every extreme that they name: `edge_counts`: every patch has at least 1024 live edges; at least one patch is full in every draw.
All inputs are finite; a program needn't handle non-finite values.
Results may differ from the reference program's by a relative error of at most 0.0055.
Values may be sent and summed in bfloat16 or wider, within the bound.
No kernel may reach another device: no remote copies, remote signals or barrier semaphores. Data moves between devices by JAX's collectives and lax.ppermute only.
A program may use at most 128 MiB of HBM per device.

```python
from functools import partial
import jax
import jax.numpy as jnp
from jax import lax

D = 512
HID = 512
NODE_DEV = 640
EDGE_DEV = 4096
HALO = 128
COARSE_DEV = 32
NODES = 5120
EDGES = 32768
COARSE = 256
TABLE = 1152
N_PATCH = 8


def draw_edge_counts(key, part):
    key = jax.random.fold_in(key, 7)
    first_key, second_key = jax.random.split(key)
    counts = jax.random.randint(first_key, (N_PATCH,), EDGE_DEV // 4, EDGE_DEV + 1)
    full_patch = jax.random.randint(second_key, (), 0, N_PATCH)
    return jnp.where(jnp.arange(N_PATCH) == full_patch, EDGE_DEV, counts).astype(jnp.int32)


def with_ends(entries, stream_key, least, largest):
    extent = entries.shape
    index_at = [jax.random.randint(jax.random.fold_in(stream_key, axis), (), 0, extent[axis]) for axis in range(len(extent))]
    entries = entries.at[tuple(index_at)].set(least)
    longest = extent.index(max(extent))
    index_at[longest] = (index_at[longest] + 1) % extent[longest]
    return entries.at[tuple(index_at)].set(largest)


def shard_levels(stream_key, extent, pieces, low, top_value):
    def one(position, parts):
        draws = jax.random.uniform(jax.random.fold_in(jax.random.fold_in(stream_key, 6), position), (parts,), jnp.float32, low / len(pieces), top_value / len(pieces))
        return jnp.repeat(jnp.exp(draws), extent[position] // parts).reshape((-1,) + (1,) * (len(extent) - position - 1))

    factor_of = one(*pieces[0])
    for cut in pieces[1:]:
        factor_of = factor_of * one(*cut)
    return factor_of


def noise(key, shape, spread, reach, cuts=(), held_as=jnp.bfloat16):
    gain = shard_levels(key, shape, cuts, -0.22, 0.18) if cuts else 1.0
    drawn = jax.random.normal(key, shape, jnp.float32) * spread * gain
    return jnp.minimum(jnp.maximum(drawn, -reach), reach).astype(held_as)


def setup_inputs(seed: int = 0, part: int = 0) -> dict:
    key_of = jax.random.split(jax.random.key(seed), 14)
    part_keys = jax.random.split(jax.random.fold_in(key_of[13], part), 14)
    node_latent = noise(part_keys[0], (NODES, D), 1.0, 6.0, ((0, 8),))
    edge_latent = noise(part_keys[1], (EDGES, D), 1.0, 6.0, ((0, 8),))
    edge_senders = with_ends(jax.random.randint(part_keys[2], (EDGES,), 0, TABLE), jax.random.fold_in(part_keys[2], 1), 0, TABLE - 1).astype(jnp.int32)
    edge_receivers = with_ends(jax.random.randint(part_keys[3], (EDGES,), 0, TABLE), jax.random.fold_in(part_keys[3], 1), 0, TABLE - 1).astype(jnp.int32)
    halo_rows = with_ends(jax.random.randint(part_keys[4], (2 * N_PATCH, HALO), 0, NODE_DEV), jax.random.fold_in(part_keys[4], 1), 0, NODE_DEV - 1).astype(jnp.int32)
    coarse_rows = with_ends(jax.random.randint(part_keys[5], (COARSE,), 0, NODE_DEV), jax.random.fold_in(part_keys[5], 1), 0, NODE_DEV - 1).astype(jnp.int32)
    edge_counts = draw_edge_counts(jax.random.fold_in(jax.random.fold_in(key_of[13], part), 71), part)
    edge_w1 = noise(key_of[7], (3 * D, HID), (3 * D) ** -0.5, 0.15625, ((1, 2),))
    edge_w2 = noise(key_of[8], (HID, D), HID ** -0.5, 0.25, ((0, 2),))
    edge_gain = jnp.clip(1.0 + 0.18 * jax.random.normal(key_of[9], (D,), jnp.float32), 0.099609375, 1.8984375).astype(jnp.bfloat16)
    node_w1 = noise(key_of[10], (2 * D, HID), (2 * D) ** -0.5, 0.1875, ((1, 2),))
    node_w2 = noise(key_of[11], (HID, D), HID ** -0.5, 0.25, ((0, 2),))
    node_gain = jnp.clip(1.0 + 0.18 * jax.random.normal(key_of[12], (D,), jnp.float32), 0.099609375, 1.8984375).astype(jnp.bfloat16)
    return {"node_latent": node_latent, "edge_latent": edge_latent, "edge_senders": edge_senders, "edge_receivers": edge_receivers, "halo_rows": halo_rows, "coarse_rows": coarse_rows, "edge_counts": edge_counts, "edge_w1": edge_w1, "edge_w2": edge_w2, "edge_gain": edge_gain, "node_w1": node_w1, "node_w2": node_w2, "node_gain": node_gain}


EPSILON = 1e-05

def normalize(values, gain_vector):
    center = lax.optimization_barrier(jnp.mean(values, axis=1, keepdims=True))
    square = lax.optimization_barrier(jnp.mean(values * values, axis=1, keepdims=True))
    return (values - center) * lax.rsqrt(square - center * center + EPSILON) * gain_vector.astype(jnp.float32)

def pick_rows(matrix, indices):
    return matrix[indices]

def add_back(local_rows, upper_rows, upper_values, lower_rows, lower_values, coarse_index, coarse_values):
    return local_rows.at[upper_rows].add(upper_values).at[lower_rows].add(lower_values).at[coarse_index].add(coarse_values)

def edge_patch(operands, edge_w1, edge_w2, edge_gain):
    lookup, latent, senders, receivers, live_limit = operands
    stacked = jnp.concatenate([latent, lookup[senders], lookup[receivers]], axis=1)
    hidden = jax.nn.silu(jnp.dot(stacked, edge_w1, preferred_element_type=jnp.float32)).astype(jnp.bfloat16)
    update = normalize(jnp.dot(hidden, edge_w2, preferred_element_type=jnp.float32), edge_gain)
    live_rows = jnp.arange(EDGE_DEV) < live_limit
    before = latent.astype(jnp.float32)
    fresh_edges = jnp.where(live_rows[:, None], before + update, before).astype(jnp.bfloat16)
    message = jnp.where(live_rows[:, None], fresh_edges, jnp.zeros_like(fresh_edges)).astype(jnp.float32)
    target = jnp.where(live_rows, receivers, TABLE)
    summed = jax.ops.segment_sum(message, target, num_segments=TABLE + 1)[:TABLE]
    return (fresh_edges, summed)

def reference(node_latent, edge_latent, edge_senders, edge_receivers, halo_rows, coarse_rows, edge_counts, edge_w1, edge_w2, edge_gain, node_w1, node_w2, node_gain):
    node_blocks = node_latent.reshape(N_PATCH, NODE_DEV, D)
    halo_lists = halo_rows.reshape(N_PATCH, 2, HALO)
    coarse_picks = coarse_rows.reshape(N_PATCH, COARSE_DEV)
    upward = jax.vmap(pick_rows)(node_blocks, halo_lists[:, 0])
    downward = jax.vmap(pick_rows)(node_blocks, halo_lists[:, 1])
    coarse_all = jax.vmap(pick_rows)(node_blocks, coarse_picks).reshape(COARSE, D)
    blank_rim = jnp.zeros((1, HALO, D), jnp.bfloat16)
    from_lower = jnp.concatenate([blank_rim, upward[:-1]], axis=0)
    from_upper = jnp.concatenate([downward[1:], blank_rim], axis=0)
    shared = jnp.broadcast_to(coarse_all[None], (N_PATCH, COARSE, D))
    tables = jnp.concatenate([node_blocks, from_lower, from_upper, shared], axis=1)
    per_patch = partial(edge_patch, edge_w1=edge_w1, edge_w2=edge_w2, edge_gain=edge_gain)
    fresh_edges, summed = lax.map(per_patch, (tables, edge_latent.reshape(N_PATCH, EDGE_DEV, D), edge_senders.reshape(N_PATCH, EDGE_DEV), edge_receivers.reshape(N_PATCH, EDGE_DEV), edge_counts))
    local_rows = summed[:, :NODE_DEV]
    sec_lower = summed[:, NODE_DEV:NODE_DEV + HALO]
    sec_upper = summed[:, NODE_DEV + HALO:NODE_DEV + 2 * HALO]
    coarse_back = lax.optimization_barrier(jnp.sum(summed[:, NODE_DEV + 2 * HALO:], axis=0)).reshape(N_PATCH, COARSE_DEV, D)
    empty_rim = jnp.zeros((1, HALO, D), summed.dtype)
    back_up = jnp.concatenate([sec_lower[1:], empty_rim], axis=0)
    back_down = jnp.concatenate([empty_rim, sec_upper[:-1]], axis=0)
    gathered = jax.vmap(add_back)(local_rows, halo_lists[:, 0], back_up, halo_lists[:, 1], back_down, coarse_picks, coarse_back).reshape(NODES, D)
    message_sum = gathered.astype(jnp.bfloat16)
    stacked = jnp.concatenate([node_latent, message_sum], axis=1)
    hidden = jax.nn.silu(jnp.dot(stacked, node_w1, preferred_element_type=jnp.float32)).astype(jnp.bfloat16)
    update = normalize(jnp.dot(hidden, node_w2, preferred_element_type=jnp.float32), node_gain)
    nodes_out = (node_latent.astype(jnp.float32) + update).astype(jnp.bfloat16)
    return (nodes_out, fresh_edges.reshape(EDGES, D))
```

```python
import functools

import jax
import jax.numpy as jnp
from jax import lax
from jax.experimental import pallas as pl
from jax.experimental.pallas import tpu as pltpu
from jax.sharding import PartitionSpec as P

EPSILON = 1e-05
F32 = jnp.float32
BF16 = jnp.bfloat16
MIB = 1024 * 1024
FEAT_SWAP = [(0, 1), (1, 0)]


def silu(v):
    return 0.5 * v * (1.0 + jnp.tanh(0.5 * v))


def dot(a, b):
    return jnp.dot(a, b, preferred_element_type=F32)


def layer_norm(pre, gain):
    width = pre.shape[1]
    center = jnp.sum(pre, axis=1, keepdims=True) / width
    square = jnp.sum(pre * pre, axis=1, keepdims=True) / width
    return (pre - center) * lax.rsqrt(square - center * center + EPSILON) * gain


def one_hot_rows(index_row, first, count):
    entries = index_row.shape[1]
    column = jnp.transpose(jnp.broadcast_to(index_row, (128, entries))) - first
    lanes = lax.broadcasted_iota(jnp.int32, (entries, 128), 1)
    return jnp.concatenate(
        [(column == lanes + 128 * j).astype(F32).astype(BF16) for j in range(count // 128)], axis=1
    )


def one_hot_columns(index_row, first, count):
    entries = index_row.shape[1]
    rows = lax.broadcasted_iota(jnp.int32, (count, entries), 0) + first
    return (rows == jnp.broadcast_to(index_row, (count, entries))).astype(F32).astype(BF16)


def lend_kernel(feat_ref, node_ref, halo_ref, coarse_ref, out_ref):
    node_count = node_ref.shape[0]
    halo = jnp.where(feat_ref[0] == 0, halo_ref[0:1, :], halo_ref[1:2, :])
    index_row = jnp.concatenate([halo, coarse_ref[...]], axis=1)
    picks = one_hot_columns(index_row, 0, node_count)
    out_ref[...] = lax.dot_general(
        picks, node_ref[...], (((0,), (0,)), ((), ())), preferred_element_type=F32
    ).astype(BF16)


def local_kernel(
    feat_ref, node_ref, lent_ref, wa_ref, wb_ref, latent_ref, index_ref, out_ref, table, local_slots, coarse
):
    node_count, width = node_ref.shape
    half = wa_ref.shape[1]
    halves = ((wa_ref, 0), (wb_ref, half))

    @pl.when(pl.program_id(0) == 0)
    def _():
        for side in range(2):
            base = side * local_slots
            rows = slice((side + 1) * width, (side + 2) * width)
            for weight, col in halves:
                cols = slice(col, col + half)
                table[base : base + node_count, cols] = dot(node_ref[...], weight[rows, :]).astype(BF16)
                table[base + node_count : base + node_count + coarse, cols] = dot(
                    lent_ref[lent_ref.shape[0] - coarse :, :], weight[rows, :]
                ).astype(BF16)
            table[base + node_count + coarse : base + local_slots, :] = jnp.zeros(
                (local_slots - node_count - coarse, 2 * half), BF16
            )

    picks = jnp.concatenate(
        [one_hot_rows(index_ref[side : side + 1, :], 0, local_slots) for side in range(2)], axis=1
    )
    for weight, col in halves:
        cols = slice(col, col + half)
        out_ref[:, cols] = dot(latent_ref[...], weight[:width, :]) + dot(picks, table[:, cols])


def edge_kernel(
    feat_ref,
    limit_ref,
    pre_ref,
    latent_ref,
    index_ref,
    mine_ref,
    theirs_ref,
    wa_ref,
    wb_ref,
    va_ref,
    vb_ref,
    gain_ref,
    out_mine_ref,
    out_other_ref,
    group_mine_ref,
    group_other_ref,
    local_ref,
    table,
    sums,
    local_slots,
):
    step = pl.program_id(0)
    steps = pl.num_programs(0)
    block, width = latent_ref.shape
    half = wa_ref.shape[1]
    group = mine_ref.shape[0]
    used = local_ref.shape[0]
    feat = feat_ref[0]

    @pl.when(step == 0)
    def _():
        for side in range(2):
            rows = slice((side + 1) * width, (side + 2) * width)
            for weight, col in ((wa_ref, 0), (wb_ref, half)):
                cols = slice(col, col + half)
                base = side * 2 * group
                at_mine = pl.multiple_of(base + feat * group, group)
                at_theirs = pl.multiple_of(base + (1 - feat) * group, group)
                table[pl.ds(at_mine, group), cols] = dot(mine_ref[...], weight[rows, :]).astype(BF16)
                table[pl.ds(at_theirs, group), cols] = dot(theirs_ref[...], weight[rows, :]).astype(BF16)
        sums[...] = jnp.zeros_like(sums)
        local_ref[...] = jnp.zeros_like(local_ref)

    picks = jnp.concatenate(
        [one_hot_rows(index_ref[side : side + 1, :], local_slots, 2 * group) for side in range(2)], axis=1
    )
    hidden = silu(pre_ref[...] + dot(picks, table[...])).astype(BF16)
    pre = dot(hidden[:, :half], va_ref[...]) + dot(hidden[:, half:], vb_ref[...])
    update = layer_norm(pre, gain_ref[...].astype(F32))
    before = latent_ref[...]
    row = lax.broadcasted_iota(jnp.int32, (block, 1), 0) + (feat * steps + step) * block
    fresh = jnp.where(row < limit_ref[0], before.astype(F32) + update, before.astype(F32)).astype(BF16)
    low, high = fresh[:, : width // 2], fresh[:, width // 2 :]
    out_mine_ref[...] = jnp.where(feat == 0, low, high)
    out_other_ref[...] = jnp.where(feat == 0, high, low)
    receivers = index_ref[1:2, :]
    local_ref[...] += dot(one_hot_columns(receivers, 0, used), fresh)
    sums[...] += dot(one_hot_columns(receivers, local_slots, 2 * group), fresh)

    @pl.when(step == steps - 1)
    def _():
        group_mine_ref[...] = sums[pl.ds(pl.multiple_of(feat * group, group), group), :]
        group_other_ref[...] = sums[pl.ds(pl.multiple_of((1 - feat) * group, group), group), :].astype(BF16)


def merge_kernel(mine_ref, theirs_ref, *out_refs):
    at = 0
    for out_ref in out_refs:
        rows = out_ref.shape[0]
        part = slice(at, at + rows)
        out_ref[...] = (mine_ref[part, :] + theirs_ref[part, :].astype(F32)).astype(BF16)
        at += rows


def place_kernel(feat_ref, block_ref, whole_ref, out_ref):
    out_ref[...] = block_ref[...]


def node_kernel(
    feat_ref,
    node_ref,
    halo_ref,
    coarse_ref,
    own_ref,
    partner_ref,
    mine_ref,
    theirs_ref,
    wa_ref,
    wb_ref,
    va_ref,
    vb_ref,
    gain_ref,
    out_ref,
):
    node_count, width = node_ref.shape
    half = wa_ref.shape[1]
    group = mine_ref.shape[0]
    coarse = coarse_ref.shape[1]
    feat = feat_ref[0]
    low, high = halo_ref[0:1, :], halo_ref[1:2, :]
    coarse_row = coarse_ref[...]
    repeat = (group - low.shape[1]) // coarse
    index_row = jnp.concatenate(
        [jnp.where(feat == 0, low, high)]
        + [coarse_row] * repeat
        + [jnp.where(feat == 0, high, low)]
        + [coarse_row] * (repeat + 2),
        axis=1,
    )
    returned = jnp.concatenate(
        [mine_ref[...], theirs_ref[...], own_ref[node_count:, :].astype(BF16), partner_ref[node_count:, :]], axis=0
    )
    received = (
        own_ref[:node_count, :]
        + partner_ref[:node_count, :].astype(F32)
        + dot(one_hot_columns(index_row, 0, node_count), returned)
    ).astype(BF16)
    total = None
    for weight, second in ((wa_ref, va_ref), (wb_ref, vb_ref)):
        pre = dot(node_ref[...], weight[:width, :]) + dot(received, weight[width:, :])
        part = dot(silu(pre).astype(BF16), second[...])
        total = part if total is None else total + part
    update = layer_norm(total, gain_ref[...].astype(F32))
    fresh = (node_ref[...].astype(F32) + update).astype(BF16)
    out_ref[...] = jnp.where(feat == 0, fresh[:, : width // 2], fresh[:, width // 2 :])


def whole(shape):
    return pl.BlockSpec(shape, lambda *_: (0,) * len(shape))


def call(kernel, grid, scalars, in_specs, out_specs, out_shape, operands, flops, scratch=(), aliases=None):
    return pl.pallas_call(
        kernel,
        grid_spec=pltpu.PrefetchScalarGridSpec(
            num_scalar_prefetch=len(scalars),
            grid=grid,
            in_specs=in_specs,
            out_specs=out_specs,
            scratch_shapes=list(scratch),
        ),
        out_shape=out_shape,
        input_output_aliases=aliases or {},
        cost_estimate=pl.CostEstimate(flops=flops, bytes_accessed=4 * MIB, transcendentals=0),
        compiler_params=pltpu.CompilerParams(vmem_limit_bytes=40 * MIB),
    )(*scalars, *operands)


def hops(count, distance, wrap):
    pairs = []
    for patch in range(count):
        for feat, step in ((0, distance), (1, -distance)):
            target = patch + step
            if wrap or 0 <= target < count:
                pairs.append((2 * patch + feat, 2 * (target % count) + feat))
    return pairs


def exchange_pairs(count):
    middle = count // 2
    pairs = [hops(count, 1, False)] + [hops(count, k, True) for k in range(2, middle)]
    last = [(2 * patch, 2 * ((patch + middle) % count)) for patch in range(count)]
    return pairs + [last + [(1, 2 * count - 1), (2 * count - 1, 1)]]


def relative_slots(rows, patch, patches, node_count, halo, coarse, local_slots, group):
    at = rows - (node_count + 2 * halo)
    owner, entry = at // coarse, at % coarse
    below = (patch - owner) % patches
    middle = patches // 2
    first, second = local_slots, local_slots + group
    ends = ((patch == 0) & (owner == patches - 1)) | ((patch == patches - 1) & (owner == 0))
    place = jnp.where(
        below <= middle,
        first + halo + coarse * (below - 1),
        second + halo + coarse * (patches - below - 1),
    )
    place = jnp.where(ends, second + halo + coarse * (middle - 1), place)
    place = jnp.where(below == 0, node_count, place) + entry
    place = jnp.where(rows < node_count + 2 * halo, second + rows - (node_count + halo), place)
    place = jnp.where(rows < node_count + halo, first + rows - node_count, place)
    return jnp.where(rows < node_count, rows, place)


def on_device(
    node_latent,
    edge_latent,
    edge_senders,
    edge_receivers,
    halo_rows,
    coarse_rows,
    edge_counts,
    edge_w1,
    edge_w2,
    edge_gain,
    node_w1,
    node_w2,
    node_gain,
):
    node_count, width = node_latent.shape
    half = width // 2
    edge_count = edge_latent.shape[0]
    halo, coarse = halo_rows.shape[1], coarse_rows.shape[0]
    patches = lax.axis_size("patch")
    feat = lax.axis_index("feat")
    patch = lax.axis_index("patch")
    both = ("patch", "feat")
    group = halo + coarse * (patches // 2)
    used = node_count + coarse
    local_slots = -(-used // 256) * 256
    share = edge_count // 2
    block = 512
    steps = share // block
    feat_scalar = feat.astype(jnp.int32).reshape(1)
    coarse_row = coarse_rows.reshape(1, coarse)
    edge_gain, node_gain = edge_gain.reshape(1, width), node_gain.reshape(1, width)

    def shape(rows, columns, kind):
        return jax.ShapeDtypeStruct((rows, columns), kind)

    lent = call(
        lend_kernel,
        (1,),
        (feat_scalar,),
        [whole((node_count, width)), whole((2, halo)), whole((1, coarse))],
        whole((halo + coarse, width)),
        shape(halo + coarse, width, BF16),
        (node_latent, halo_rows, coarse_row),
        2 * node_count * (halo + coarse) * width,
    )
    pairs = exchange_pairs(patches)
    arrived = [lax.ppermute(lent, both, pairs[0])]
    for some in pairs[1:]:
        arrived.append(lax.ppermute(lent[halo:], both, some))
    table_mine = jnp.concatenate(arrived, axis=0)
    table_theirs = lax.ppermute(table_mine, "feat", FEAT_SWAP)

    edge_w1_b = lax.ppermute(edge_w1, "feat", FEAT_SWAP)
    edge_w2_b = lax.ppermute(edge_w2, "feat", FEAT_SWAP)
    node_w1_b = lax.ppermute(node_w1, "feat", FEAT_SWAP)
    node_w2_b = lax.ppermute(node_w2, "feat", FEAT_SWAP)

    live = jnp.arange(edge_count) < edge_counts[0]
    slots = jnp.stack(
        [
            jnp.where(
                live,
                relative_slots(rows, patch, patches, node_count, halo, coarse, local_slots, group),
                -1,
            )
            for rows in (edge_senders, edge_receivers)
        ]
    )

    my_rows = lambda i, f, *_: (f[0] * steps + i, 0)
    other_rows = lambda i, f, *_: ((1 - f[0]) * steps + i, 0)
    my_slots = lambda i, f, *_: (0, f[0] * steps + i)
    step_rows = lambda i, *_: (i, 0)

    pre = call(
        functools.partial(local_kernel, local_slots=local_slots, coarse=coarse),
        (steps,),
        (feat_scalar,),
        [
            whole((node_count, width)),
            whole((halo + coarse, width)),
            whole((3 * width, half)),
            whole((3 * width, half)),
            pl.BlockSpec((block, width), my_rows),
            pl.BlockSpec((2, block), my_slots),
        ],
        pl.BlockSpec((block, width), step_rows),
        shape(share, width, F32),
        (node_latent, lent, edge_w1, edge_w1_b, edge_latent, slots),
        2 * width * width * share + 4 * used * width * width + 4 * share * local_slots * width,
        scratch=[pltpu.VMEM((2 * local_slots, width), BF16)],
    )

    edges, edges_other, group_mine, group_other, local_sums = call(
        functools.partial(edge_kernel, local_slots=local_slots),
        (steps,),
        (feat_scalar, edge_counts),
        [
            pl.BlockSpec((block, width), step_rows),
            pl.BlockSpec((block, width), my_rows),
            pl.BlockSpec((2, block), my_slots),
            whole((group, width)),
            whole((group, width)),
            whole((3 * width, half)),
            whole((3 * width, half)),
            whole((half, width)),
            whole((half, width)),
            whole((1, width)),
        ],
        [
            pl.BlockSpec((block, half), my_rows),
            pl.BlockSpec((block, half), step_rows),
            whole((group, width)),
            whole((group, width)),
            whole((used, width)),
        ],
        [
            shape(edge_count, half, BF16),
            shape(share, half, BF16),
            shape(group, width, F32),
            shape(group, width, BF16),
            shape(used, width, F32),
        ],
        (pre, edge_latent, slots, table_mine, table_theirs, edge_w1, edge_w1_b, edge_w2, edge_w2_b, edge_gain),
        2 * share * width * (width + 6 * group + used) + 8 * group * width * width,
        scratch=[pltpu.VMEM((4 * group, width), BF16), pltpu.VMEM((2 * group, width), F32)],
    )

    group_theirs = lax.ppermute(group_other, "feat", FEAT_SWAP)
    sizes = [halo + coarse] + [coarse] * (len(pairs) - 1)
    outgoing = call(
        merge_kernel,
        (1,),
        (),
        [whole((group, width))] * 2,
        [whole((rows, width)) for rows in sizes],
        [shape(rows, width, BF16) for rows in sizes],
        (group_mine, group_theirs),
        group * width,
    )
    back = [
        lax.ppermute(part, both, [(target, source) for source, target in some])
        for part, some in zip(outgoing, pairs)
    ]
    back_mine = jnp.concatenate(back, axis=0)
    back_theirs = lax.ppermute(back_mine, "feat", FEAT_SWAP)
    local_theirs = lax.ppermute(local_sums.astype(BF16), "feat", FEAT_SWAP)
    edges_theirs = lax.ppermute(edges_other, "feat", FEAT_SWAP)
    edges_out = call(
        place_kernel,
        (steps,),
        (feat_scalar,),
        [pl.BlockSpec((block, half), step_rows), pl.BlockSpec(memory_space=pl.ANY)],
        pl.BlockSpec((block, half), other_rows),
        shape(edge_count, half, BF16),
        (edges_theirs, edges),
        share * half,
        aliases={2: 0},
    )
    nodes_out = call(
        node_kernel,
        (1,),
        (feat_scalar,),
        [
            whole((node_count, width)),
            whole((2, halo)),
            whole((1, coarse)),
            whole((used, width)),
            whole((used, width)),
            whole((group, width)),
            whole((group, width)),
            whole((2 * width, half)),
            whole((2 * width, half)),
            whole((half, width)),
            whole((half, width)),
            whole((1, width)),
        ],
        whole((node_count, half)),
        shape(node_count, half, BF16),
        (
            node_latent,
            halo_rows,
            coarse_row,
            local_sums,
            local_theirs,
            back_mine,
            back_theirs,
            node_w1,
            node_w1_b,
            node_w2,
            node_w2_b,
            node_gain,
        ),
        2 * node_count * width * (3 * width + 2 * group),
    )
    return nodes_out, edges_out


def solution(mesh):
    placed = (
        P(("member", "patch"), None),
        P(("member", "patch"), None),
        P(("member", "patch")),
        P(("member", "patch")),
        P(("member", "patch"), None),
        P(("member", "patch")),
        P(("member", "patch")),
        P(None, "feat"),
        P("feat", None),
        P(),
        P(None, "feat"),
        P("feat", None),
        P(),
    )
    return jax.shard_map(
        on_device,
        mesh=mesh,
        in_specs=placed,
        out_specs=(P(("member", "patch"), "feat"), P(("member", "patch"), "feat")),
        check_vma=False,
    )
```

```python
import functools

import jax
import jax.numpy as jnp
from jax import lax
from jax.experimental import pallas as pl
from jax.experimental.pallas import tpu as pltpu
from jax.sharding import PartitionSpec as P

EPSILON = 1e-05
F32 = jnp.float32
BF16 = jnp.bfloat16
MIB = 1024 * 1024
LIMIT = 28
FEAT_SWAP = [(0, 1), (1, 0)]


def silu(v):
    return 0.5 * v * (1.0 + jnp.tanh(0.5 * v))


def dot(a, b):
    return jnp.dot(a, b, preferred_element_type=F32)


def layer_norm(pre, gain):
    width = pre.shape[1]
    center = jnp.sum(pre, axis=1, keepdims=True) / width
    square = jnp.sum(pre * pre, axis=1, keepdims=True) / width
    return (pre - center) * lax.rsqrt(square - center * center + EPSILON) * gain


def one_hot_rows(index, first, count):
    lanes = lax.broadcasted_iota(jnp.int32, (128, 128), 1)
    blocks = []
    for j in range(index.shape[0]):
        column = jnp.transpose(jnp.broadcast_to(index[j : j + 1, :], (128, 128))) - first
        blocks.append(
            jnp.concatenate(
                [(column == lanes + at).astype(F32).astype(BF16) for at in range(0, count, 128)], axis=1
            )
        )
    return jnp.concatenate(blocks, axis=0)


def one_hot_columns(index_row, first, count):
    entries = index_row.shape[1]
    rows = lax.broadcasted_iota(jnp.int32, (count, entries), 0) + first
    return (rows == jnp.broadcast_to(index_row, (count, entries))).astype(F32).astype(BF16)


def flat_row(index):
    return jnp.concatenate([index[j : j + 1, :] for j in range(index.shape[0])], axis=1)


def load_all(pairs, sems):
    copies = [pltpu.make_async_copy(source, target, sems.at[i]) for i, (source, target) in enumerate(pairs)]
    for copy in copies:
        copy.start()
    return copies


class Layout:
    def __init__(self, patches, node_count, halo, coarse):
        self.patches, self.node_count, self.halo, self.coarse = patches, node_count, halo, coarse
        self.group = halo + coarse * (patches // 2)
        self.used = node_count + coarse
        self.local_slots = -(-self.used // 256) * 256

    def slots(self, rows, patch, live):
        node_count, halo, coarse, group = self.node_count, self.halo, self.coarse, self.group
        at = rows - (node_count + 2 * halo)
        owner, entry = lax.shift_right_arithmetic(at, coarse.bit_length() - 1), at & (coarse - 1)
        distance = patch ^ owner
        odd = patch & 1
        place = self.local_slots + (distance & 1) * group + halo + coarse * lax.shift_right_arithmetic(distance, 1)
        place = jnp.where(distance == 0, node_count, place)
        place = jnp.where(distance == 1, self.local_slots + halo, place) + entry
        lower = self.local_slots + (1 - odd) * group - node_count + rows
        upper = self.local_slots + odd * group - (node_count + halo) + rows
        lower = jnp.where(patch == 0, -1, lower)
        upper = jnp.where(patch == self.patches - 1, -1, upper)
        place = jnp.where(rows < node_count + 2 * halo, upper, place)
        place = jnp.where(rows < node_count + halo, lower, place)
        place = jnp.where(rows < node_count, rows, place)
        return jnp.where(live, place, -1)

    def edge_slots(self, index_ref, step, where_ref, edges_per_core, block):
        feat, patch, limit = where_ref[0], where_ref[1], where_ref[2]
        count = block // 128
        start = feat * (edges_per_core // 128) + step * count
        rows = index_ref[pl.ds(start, count), :]
        shape = (count, 128)
        edge = (
            lax.broadcasted_iota(jnp.int32, shape, 0) * 128 + lax.broadcasted_iota(jnp.int32, shape, 1) + start * 128
        )
        return self.slots(rows, patch, edge < limit)


def lend_kernel(where_ref, node_ref, halo_ref, coarse_ref, out_ref, node, halo, coarse, sems):
    for copy in load_all(((node_ref, node), (halo_ref, halo), (coarse_ref, coarse)), sems):
        copy.wait()
    node_count = node.shape[0]
    lists = halo[...]
    which = (where_ref[0] + where_ref[1]) & 1
    index_row = jnp.concatenate(
        [jnp.where(which == 0, lists[0:1], lists[1:2]), coarse[...].reshape(1, -1)], axis=1
    )
    picks = one_hot_columns(index_row, 0, node_count)
    out_ref[...] = lax.dot_general(
        picks, node[...], (((0,), (0,)), ((), ())), preferred_element_type=F32
    ).astype(BF16)


def local_kernel(
    where_ref, node_ref, wa_ref, lent_ref, wb_ref, latent_ref, send_ref, recv_ref, out_ref, table, node, wa, sems, layout, share
):
    step = pl.program_id(0)
    node_count, width = node.shape
    half = wa.shape[1]
    block = latent_ref.shape[0]
    local_slots, used = layout.local_slots, layout.used

    @pl.when(step == 0)
    def _():
        for copy in load_all(((node_ref, node), (wa_ref, wa)), sems):
            copy.wait()
        rows_in = jnp.concatenate([node[...], lent_ref[lent_ref.shape[0] - layout.coarse :, :]], axis=0)
        for side in range(2):
            base = side * local_slots
            rows = slice((side + 1) * width, (side + 2) * width)
            for weight, col in ((wa, 0), (wb_ref, half)):
                table[base : base + used, col : col + half] = dot(rows_in, weight[rows, :]).astype(BF16)
            table[base + used : base + local_slots, :] = jnp.zeros((local_slots - used, 2 * half), BF16)

    picks = jnp.concatenate(
        [
            one_hot_rows(layout.edge_slots(index_ref, step, where_ref, share, block), 0, local_slots)
            for index_ref in (send_ref, recv_ref)
        ],
        axis=1,
    )
    for weight, col in ((wa, 0), (wb_ref, half)):
        cols = slice(col, col + half)
        out_ref[:, cols] = dot(latent_ref[...], weight[:width, :]) + dot(picks, table[:, cols])


def edge_kernel(
    where_ref,
    pre_ref,
    latent_ref,
    send_ref,
    recv_ref,
    mine_ref,
    theirs_ref,
    wa_ref,
    wb_ref,
    va_ref,
    vb_ref,
    gain_ref,
    fresh_ref,
    out_mine_ref,
    out_other_ref,
    group_mine_ref,
    group_other_ref,
    table,
    sums,
    wa,
    va,
    sems,
    layout,
    share,
):
    step = pl.program_id(0)
    steps = pl.num_programs(0)
    block, width = latent_ref.shape
    half = wa.shape[1]
    group = layout.group
    feat = where_ref[0]

    @pl.when(step == 0)
    def _():
        for copy in load_all(((wa_ref, wa), (va_ref, va)), sems):
            copy.wait()
        for side in range(2):
            rows = slice((side + 1) * width, (side + 2) * width)
            for weight, col in ((wa, 0), (wb_ref, half)):
                cols = slice(col, col + half)
                base = side * 2 * group
                at_mine = pl.multiple_of(base + feat * group, group)
                at_theirs = pl.multiple_of(base + (1 - feat) * group, group)
                table[pl.ds(at_mine, group), cols] = dot(mine_ref[...], weight[rows, :]).astype(BF16)
                table[pl.ds(at_theirs, group), cols] = dot(theirs_ref[...], weight[rows, :]).astype(BF16)
        sums[...] = jnp.zeros_like(sums)

    senders, receivers = [
        layout.edge_slots(index_ref, step, where_ref, share, block) for index_ref in (send_ref, recv_ref)
    ]
    picks = jnp.concatenate(
        [one_hot_rows(index, layout.local_slots, 2 * group) for index in (senders, receivers)], axis=1
    )
    hidden = silu(pre_ref[...] + dot(picks, table[...])).astype(BF16)
    pre = dot(hidden[:, :half], va[...]) + dot(hidden[:, half:], vb_ref[...])
    update = layer_norm(pre, gain_ref[...].astype(F32).reshape(1, width))
    before = latent_ref[...]
    row = lax.broadcasted_iota(jnp.int32, (block, 1), 0) + (feat * steps + step) * block
    fresh = jnp.where(row < where_ref[2], before.astype(F32) + update, before.astype(F32)).astype(BF16)
    fresh_ref[...] = fresh
    low, high = fresh[:, : width // 2], fresh[:, width // 2 :]
    out_mine_ref[...] = jnp.where(feat == 0, low, high)
    out_other_ref[...] = jnp.where(feat == 0, high, low)
    sums[...] += dot(one_hot_columns(flat_row(receivers), layout.local_slots, 2 * group), fresh)

    @pl.when(step == steps - 1)
    def _():
        group_mine_ref[...] = sums[pl.ds(pl.multiple_of(feat * group, group), group), :]
        group_other_ref[...] = sums[pl.ds(pl.multiple_of((1 - feat) * group, group), group), :].astype(BF16)


def merge_kernel(mine_ref, theirs_ref, *out_refs):
    at = 0
    for out_ref in out_refs:
        rows = out_ref.shape[0]
        part = slice(at, at + rows)
        out_ref[...] = (mine_ref[part, :] + theirs_ref[part, :].astype(F32)).astype(BF16)
        at += rows


def local_sums_kernel(
    where_ref, fresh_ref, recv_ref, node_ref, wa_ref, wb_ref, sums_ref, pre_ref, node, wa, sems, layout, share
):
    step = pl.program_id(0)
    node_count, width = node.shape
    half = wa.shape[1]
    used = sums_ref.shape[0]
    block = fresh_ref.shape[0]

    @pl.when(step == 0)
    def _():
        load_all(((node_ref, node), (wa_ref.at[pl.ds(0, width), :], wa)), sems)
        sums_ref[...] = jnp.zeros_like(sums_ref)

    receivers = layout.edge_slots(recv_ref, step, where_ref, share, block)
    sums_ref[...] += dot(one_hot_columns(flat_row(receivers), 0, used), fresh_ref[...])

    @pl.when(step == pl.num_programs(0) - 1)
    def _():
        pltpu.make_async_copy(node_ref, node, sems.at[0]).wait()
        pltpu.make_async_copy(wa_ref.at[pl.ds(0, width), :], wa, sems.at[1]).wait()
        pre_ref[:, :half] = dot(node[...], wa[...])
        pre_ref[:, half:] = dot(node[...], wb_ref[...])


def receive_kernel(where_ref, sums_ref, halo_ref, coarse_ref, *refs):
    *parts, own_ref, rounded_ref = refs
    node_count = own_ref.shape[0]
    coarse = coarse_ref.shape[0]
    lists = halo_ref[...]
    which = (where_ref[0] + where_ref[1]) & 1
    coarse_row = coarse_ref[...].reshape(1, coarse)
    index_row = jnp.concatenate(
        [jnp.where(which == 0, lists[0:1], lists[1:2])] + [coarse_row] * (len(parts) + 1), axis=1
    )
    returned = jnp.concatenate([part[...] for part in parts] + [sums_ref[node_count:, :].astype(BF16)], axis=0)
    own = sums_ref[:node_count, :] + dot(one_hot_columns(index_row, 0, node_count), returned)
    own_ref[...] = own
    rounded_ref[...] = own.astype(BF16)


def node_kernel(
    where_ref,
    node_ref,
    own_ref,
    partner_ref,
    pre_ref,
    wa_ref,
    wb_ref,
    va_ref,
    vb_ref,
    gain_ref,
    edges_in_ref,
    edges_ref,
    out_ref,
    edges_out_ref,
    sems,
):
    node_count, width = node_ref.shape
    half = wa_ref.shape[1]
    share = edges_ref.shape[0]
    feat = where_ref[0]
    copy = pltpu.make_async_copy(
        edges_ref, edges_out_ref.at[pl.ds(pl.multiple_of((1 - feat) * share, share), share), :], sems.at[0]
    )
    copy.start()
    received = (own_ref[...] + partner_ref[...].astype(F32)).astype(BF16)
    total = None
    for weight, second, col in ((wa_ref, va_ref, 0), (wb_ref, vb_ref, half)):
        pre = pre_ref[:, col : col + half] + dot(received, weight[...])
        part = dot(silu(pre).astype(BF16), second[...])
        total = part if total is None else total + part
    update = layer_norm(total, gain_ref[...].astype(F32).reshape(1, width))
    fresh = (node_ref[...].astype(F32) + update).astype(BF16)
    out_ref[...] = jnp.where(feat == 0, fresh[:, : width // 2], fresh[:, width // 2 :])
    copy.wait()


def whole(shape):
    return pl.BlockSpec(shape, lambda *_: (0,) * len(shape))


def in_hbm(array):
    return pltpu.with_memory_space_constraint(array, pltpu.HBM)


def call(kernel, grid, where, in_specs, out_specs, out_shape, operands, flops, limit, scratch=(), aliases=None):
    return pl.pallas_call(
        kernel,
        grid_spec=pltpu.PrefetchScalarGridSpec(
            num_scalar_prefetch=len(where),
            grid=grid,
            in_specs=in_specs,
            out_specs=out_specs,
            scratch_shapes=list(scratch),
        ),
        out_shape=out_shape,
        input_output_aliases=aliases or {},
        cost_estimate=pl.CostEstimate(flops=flops, bytes_accessed=4 * MIB, transcendentals=0),
        compiler_params=pltpu.CompilerParams(vmem_limit_bytes=limit * MIB),
    )(*where, *operands)


def exchange_pairs(count):
    across = [(p + 1 if p % 2 else p - 1) % count for p in range(count)]
    rounds = [([p ^ 1 for p in range(count)], across)]
    for distance in range(2, count, 2):
        rounds.append(([p ^ distance for p in range(count)], [p ^ (distance + 1) for p in range(count)]))
    return [
        [(2 * p + feat, 2 * targets[p] + feat) for p in range(count) for feat, targets in enumerate(some)]
        for some in rounds
    ]


def on_device(
    node_latent,
    edge_latent,
    edge_senders,
    edge_receivers,
    halo_rows,
    coarse_rows,
    edge_counts,
    edge_w1,
    edge_w2,
    edge_gain,
    node_w1,
    node_w2,
    node_gain,
):
    node_count, width = node_latent.shape
    half = width // 2
    edge_count = edge_latent.shape[0]
    halo, coarse = halo_rows.shape[1], coarse_rows.shape[0]
    patches = lax.axis_size("patch")
    both = ("patch", "feat")
    layout = Layout(patches, node_count, halo, coarse)
    group, used, local_slots = layout.group, layout.used, layout.local_slots
    share = edge_count // 2
    block = 512
    steps = share // block
    where = (
        jnp.stack(
            [
                lax.axis_index("feat").astype(jnp.int32),
                lax.axis_index("patch").astype(jnp.int32),
                edge_counts[0],
            ]
        ),
    )
    anywhere = pl.BlockSpec(memory_space=pl.ANY)
    dma = pltpu.SemaphoreType.DMA
    index_rows = edge_count // 128

    def shape(rows, columns, kind):
        return jax.ShapeDtypeStruct((rows, columns), kind)

    def swap(values):
        return lax.ppermute(values, "feat", FEAT_SWAP)

    edge_w1_b, edge_w2_b, node_w1_b, node_w2_b = [swap(w) for w in (edge_w1, edge_w2, node_w1, node_w2)]
    node_latent, edge_latent, halo_rows, coarse_rows, edge_w1, edge_w2, node_w1, node_w2, edge_gain, node_gain = [
        in_hbm(array)
        for array in (
            node_latent,
            edge_latent,
            halo_rows,
            coarse_rows,
            edge_w1,
            edge_w2,
            node_w1,
            node_w2,
            edge_gain,
            node_gain,
        )
    ]
    senders, receivers = [in_hbm(rows.reshape(index_rows, 128)) for rows in (edge_senders, edge_receivers)]

    lent = call(
        lend_kernel,
        (1,),
        where,
        [anywhere] * 3,
        whole((halo + coarse, width)),
        shape(halo + coarse, width, BF16),
        (node_latent, halo_rows, coarse_rows),
        2 * node_count * (halo + coarse) * width,
        8,
        scratch=[
            pltpu.VMEM((node_count, width), BF16),
            pltpu.VMEM((2, halo), jnp.int32),
            pltpu.VMEM((coarse,), jnp.int32),
            dma((3,)),
        ],
    )
    pairs = exchange_pairs(patches)
    arrived = [lax.ppermute(lent, both, pairs[0])]
    for some in pairs[1:]:
        arrived.append(lax.ppermute(lent[halo:], both, some))
    table_mine = jnp.concatenate(arrived, axis=0)
    table_theirs = swap(table_mine)

    my_rows = lambda i, where: (where[0] * steps + i, 0)
    step_rows = lambda i, where: (i, 0)

    pre = call(
        functools.partial(local_kernel, layout=layout, share=share),
        (steps,),
        where,
        [
            anywhere,
            anywhere,
            whole((halo + coarse, width)),
            whole((3 * width, half)),
            pl.BlockSpec((block, width), my_rows),
            whole((index_rows, 128)),
            whole((index_rows, 128)),
        ],
        pl.BlockSpec((block, width), step_rows),
        shape(share, width, F32),
        (node_latent, edge_w1, lent, edge_w1_b, edge_latent, senders, receivers),
        2 * width * width * share + 4 * used * width * width + 4 * share * local_slots * width,
        LIMIT,
        scratch=[
            pltpu.VMEM((2 * local_slots, width), BF16),
            pltpu.VMEM((node_count, width), BF16),
            pltpu.VMEM((3 * width, half), BF16),
            dma((2,)),
        ],
    )

    fresh, edges, edges_other, group_mine, group_other = call(
        functools.partial(edge_kernel, layout=layout, share=share),
        (steps,),
        where,
        [
            pl.BlockSpec((block, width), step_rows),
            pl.BlockSpec((block, width), my_rows),
            whole((index_rows, 128)),
            whole((index_rows, 128)),
            whole((group, width)),
            whole((group, width)),
            anywhere,
            whole((3 * width, half)),
            anywhere,
            whole((half, width)),
            whole((width,)),
        ],
        [
            pl.BlockSpec((block, width), step_rows),
            pl.BlockSpec((block, half), my_rows),
            pl.BlockSpec((block, half), step_rows),
            whole((group, width)),
            whole((group, width)),
        ],
        [
            shape(share, width, BF16),
            shape(edge_count, half, BF16),
            shape(share, half, BF16),
            shape(group, width, F32),
            shape(group, width, BF16),
        ],
        (
            pre,
            edge_latent,
            senders,
            receivers,
            table_mine,
            table_theirs,
            edge_w1,
            edge_w1_b,
            edge_w2,
            edge_w2_b,
            edge_gain,
        ),
        2 * share * width * (width + 6 * group) + 8 * group * width * width,
        LIMIT,
        scratch=[
            pltpu.VMEM((4 * group, width), BF16),
            pltpu.VMEM((2 * group, width), F32),
            pltpu.VMEM((3 * width, half), BF16),
            pltpu.VMEM((half, width), BF16),
            dma((2,)),
        ],
    )

    group_theirs = swap(group_other)
    sizes = [halo + coarse] + [coarse] * (len(pairs) - 1)
    outgoing = call(
        merge_kernel,
        (1,),
        (),
        [whole((group, width))] * 2,
        [whole((rows, width)) for rows in sizes],
        [shape(rows, width, BF16) for rows in sizes],
        (group_mine, group_theirs),
        group * width,
        8,
    )
    *outgoing, edges_other, fresh = lax.optimization_barrier((*outgoing, edges_other, fresh))
    back = [lax.ppermute(part, both, some) for part, some in zip(outgoing, pairs)]
    edges_theirs = swap(edges_other)
    local_sums, node_pre = call(
        functools.partial(local_sums_kernel, layout=layout, share=share),
        (steps,),
        where,
        [
            pl.BlockSpec((block, width), step_rows),
            whole((index_rows, 128)),
            anywhere,
            anywhere,
            whole((width, half)),
        ],
        [whole((used, width)), whole((node_count, width))],
        [shape(used, width, F32), shape(node_count, width, F32)],
        (fresh, receivers, node_latent, node_w1, node_w1_b),
        2 * share * width * used + 2 * node_count * width * width,
        16,
        scratch=[
            pltpu.VMEM((node_count, width), BF16),
            pltpu.VMEM((width, half), BF16),
            dma((2,)),
        ],
    )
    own, rounded = call(
        receive_kernel,
        (1,),
        where,
        [whole((used, width)), whole((2, halo)), whole((coarse,))] + [whole((rows, width)) for rows in sizes],
        [whole((node_count, width))] * 2,
        [shape(node_count, width, F32), shape(node_count, width, BF16)],
        (local_sums, halo_rows, coarse_rows, *back),
        2 * node_count * width * (group + coarse),
        16,
    )
    partner = swap(rounded)
    upper_half = pl.BlockSpec((width, half), lambda *_: (1, 0))
    nodes_out, edges_out = call(
        node_kernel,
        (1,),
        where,
        [
            whole((node_count, width)),
            whole((node_count, width)),
            whole((node_count, width)),
            whole((node_count, width)),
            upper_half,
            upper_half,
            whole((half, width)),
            whole((half, width)),
            whole((width,)),
            anywhere,
            anywhere,
        ],
        [whole((node_count, half)), anywhere],
        [shape(node_count, half, BF16), shape(edge_count, half, BF16)],
        (
            node_latent,
            own,
            partner,
            node_pre,
            node_w1,
            node_w1_b,
            node_w2,
            node_w2_b,
            node_gain,
            edges,
            edges_theirs,
        ),
        4 * node_count * width * width,
        16,
        scratch=[dma((1,))],
        aliases={10: 1},
    )
    return nodes_out, edges_out


def solution(mesh):
    placed = (
        P(("member", "patch"), None),
        P(("member", "patch"), None),
        P(("member", "patch")),
        P(("member", "patch")),
        P(("member", "patch"), None),
        P(("member", "patch")),
        P(("member", "patch")),
        P(None, "feat"),
        P("feat", None),
        P(),
        P(None, "feat"),
        P("feat", None),
        P(),
    )
    return jax.shard_map(
        on_device,
        mesh=mesh,
        in_specs=placed,
        out_specs=(P(("member", "patch"), "feat"), P(("member", "patch"), "feat")),
        check_vma=False,
    )
```

```python
import functools

import jax
import jax.numpy as jnp
from jax import lax
from jax.experimental import pallas as pl
from jax.experimental.pallas import tpu as pltpu
from jax.sharding import PartitionSpec as P

EPSILON = 1e-05
F32 = jnp.float32
BF16 = jnp.bfloat16
MIB = 1024 * 1024
LIMIT = 30
DEAD = -1
NOWHERE = -2
FEAT_SWAP = [(0, 1), (1, 0)]


def silu_of_double(half_v):
    return half_v + half_v * jnp.tanh(half_v)


def dot(a, b):
    return jnp.dot(a, b, preferred_element_type=F32)


def layer_norm(pre, gain, keep=None):
    width = pre.shape[1]
    center = jnp.sum(pre, axis=1, keepdims=True) * (1.0 / width)
    square = jnp.sum(pre * pre, axis=1, keepdims=True) * (1.0 / width)
    scale = lax.rsqrt(square - center * center + EPSILON)
    if keep is not None:
        scale = jnp.where(keep, scale, 0.0)
    return (pre - center) * scale * gain


def index_columns(index):
    return [
        jnp.transpose(jnp.broadcast_to(index[j : j + 1, :], (128, 128))) for j in range(index.shape[0])
    ]


def one_hot_rows(columns, first, count):
    lanes = lax.broadcasted_iota(jnp.int32, (128, 128), 1) + first
    return jnp.concatenate(
        [
            jnp.concatenate(
                [(column == lanes + at).astype(F32).astype(BF16) for at in range(0, count, 128)], axis=1
            )
            for column in columns
        ],
        axis=0,
    )


def one_hot_columns(index_row, first, count):
    entries = index_row.shape[1]
    rows = lax.broadcasted_iota(jnp.int32, (count, entries), 0) + first
    return (rows == jnp.broadcast_to(index_row, (count, entries))).astype(F32).astype(BF16)


def flat_row(index):
    return jnp.concatenate([index[j : j + 1, :] for j in range(index.shape[0])], axis=1)


def copies(pairs, sems):
    made = [pltpu.make_async_copy(source, target, sems.at[i]) for i, (source, target) in enumerate(pairs)]
    for copy in made:
        copy.start()
    return made


class Layout:
    def __init__(self, patches, node_count, halo, coarse):
        self.patches, self.node_count, self.halo, self.coarse = patches, node_count, halo, coarse
        self.group = halo + coarse * (patches // 2)
        self.used = node_count + coarse
        self.local_slots = -(-self.used // 256) * 256

    def slots(self, rows, patch):
        node_count, halo, coarse, group = self.node_count, self.halo, self.coarse, self.group
        at = rows - (node_count + 2 * halo)
        owner, entry = lax.shift_right_arithmetic(at, coarse.bit_length() - 1), at & (coarse - 1)
        distance = patch ^ owner
        odd = patch & 1
        place = self.local_slots + (distance & 1) * group + halo + coarse * lax.shift_right_arithmetic(distance, 1)
        place = jnp.where(distance == 0, node_count, place)
        place = jnp.where(distance == 1, self.local_slots + halo, place) + entry
        lower = self.local_slots + (1 - odd) * group - node_count + rows
        upper = self.local_slots + odd * group - (node_count + halo) + rows
        lower = jnp.where(patch == 0, NOWHERE, lower)
        upper = jnp.where(patch == self.patches - 1, NOWHERE, upper)
        place = jnp.where(rows < node_count + 2 * halo, upper, place)
        place = jnp.where(rows < node_count + halo, lower, place)
        return jnp.where(rows < node_count, rows, place)


def lent_list(lists):
    which = (lax.axis_index("feat") + lax.axis_index("patch")) & 1
    return jnp.where(which == 0, lists[0:1], lists[1:2])


def lend_kernel(node_ref, halo_ref, coarse_ref, lent_ref, node, halo, coarse, sems):
    for copy in copies(((halo_ref, halo), (coarse_ref, coarse), (node_ref, node)), sems):
        copy.wait()
    index_row = jnp.concatenate([lent_list(halo[...]), coarse[...].reshape(1, -1)], axis=1)
    lent_ref[...] = lax.dot_general(
        one_hot_columns(index_row, 0, node.shape[0]),
        node[...],
        (((0,), (0,)), ((), ())),
        preferred_element_type=F32,
    ).astype(BF16)


def local_kernel(
    node,
    lent_ref,
    wb_ref,
    limit,
    latent_hbm,
    send_hbm,
    recv_hbm,
    wa_hbm,
    *refs,
    layout,
    block,
):
    count = (len(refs) - 8) // 2
    more_hbm, refs = refs[:count], refs[count:]
    pre_ref, latent, send, recv, wa, *more = refs[: 5 + count]
    table, sems, block_sems = refs[5 + count :]
    share, width = latent.shape
    half = wa.shape[1]
    feat, patch = lax.axis_index("feat"), lax.axis_index("patch")
    local_slots, used = layout.local_slots, layout.used
    rows128 = share // 128
    mine = pl.ds(pl.multiple_of(feat * rows128, rows128), rows128)
    first = copies(
        (
            (wa_hbm, wa),
            (send_hbm.at[mine, :], send),
            (recv_hbm.at[mine, :], recv),
        ),
        sems,
    )
    blocks = copies(
        [
            (
                latent_hbm.at[pl.ds(pl.multiple_of(feat * share + at, block), block), :],
                latent.at[pl.ds(at, block), :],
            )
            for at in range(0, share, block)
        ],
        block_sems,
    )
    rest = copies(list(zip(more_hbm, more)), sems.at[pl.ds(3, count)])
    for copy in first:
        copy.wait()
    rows_in = jnp.concatenate([node[...], lent_ref[lent_ref.shape[0] - layout.coarse :, :]], axis=0)
    for side in range(2):
        base = side * local_slots
        rows = slice((side + 1) * width, (side + 2) * width)
        for weight, col in ((wa, 0), (wb_ref, half)):
            table[base : base + used, col : col + half] = dot(rows_in, weight[rows, :]).astype(BF16)
        table[base + used : base + local_slots, :] = jnp.zeros((local_slots - used, 2 * half), BF16)
    shape = (rows128, 128)
    edge = lax.broadcasted_iota(jnp.int32, shape, 0) * 128 + lax.broadcasted_iota(jnp.int32, shape, 1) + feat * share
    live = edge < limit[0]
    for index in (send, recv):
        index[...] = jnp.where(live, layout.slots(index[...], patch), DEAD)
    for i, copy in enumerate(blocks):
        part = slice(i * block, (i + 1) * block)
        some = slice(i * block // 128, (i + 1) * block // 128)
        picks = jnp.concatenate(
            [one_hot_rows(index_columns(index[some, :]), 0, local_slots) for index in (send, recv)], axis=1
        )
        copy.wait()
        for weight, col in ((wa, 0), (wb_ref, half)):
            cols = slice(col, col + half)
            pre_ref[part, cols] = 0.5 * (dot(latent[part, :], weight[:width, :]) + dot(picks, table[:, cols]))
    for copy in rest:
        copy.wait()


def edge_kernel(
    pre_ref,
    latent_ref,
    send_ref,
    recv_ref,
    mine_ref,
    theirs_ref,
    wa_ref,
    wb_ref,
    va_ref,
    vb_ref,
    gain_ref,
    out_mine_ref,
    out_other_ref,
    group_mine_ref,
    group_other_ref,
    table,
    sums,
    layout,
    block,
):
    share, width = latent_ref.shape
    half = wa_ref.shape[1]
    group = layout.group
    feat = lax.axis_index("feat")
    for side in range(2):
        rows = slice((side + 1) * width, (side + 2) * width)
        for weight, col in ((wa_ref, 0), (wb_ref, half)):
            cols = slice(col, col + half)
            base = side * 2 * group
            for source, owner in ((mine_ref, feat), (theirs_ref, 1 - feat)):
                at = pl.multiple_of(base + owner * group, group)
                table[pl.ds(at, group), cols] = (0.5 * dot(source[...], weight[rows, :])).astype(BF16)
    gain = gain_ref[...].astype(F32).reshape(1, width)
    for at in range(0, share, block):
        part = slice(at, at + block)
        some = slice(at // 128, (at + block) // 128)
        receivers = recv_ref[some, :]
        columns = [index_columns(send_ref[some, :]), index_columns(receivers)]
        picks = jnp.concatenate([one_hot_rows(column, layout.local_slots, 2 * group) for column in columns], axis=1)
        hidden = silu_of_double(pre_ref[part, :] + dot(picks, table[...])).astype(BF16)
        pre = dot(hidden[:, :half], va_ref[...]) + dot(hidden[:, half:], vb_ref[...])
        live = jnp.concatenate([column[:, :1] for column in columns[1]], axis=0) != DEAD
        fresh = (latent_ref[part, :].astype(F32) + layer_norm(pre, gain, live)).astype(BF16)
        low, high = fresh[:, : width // 2], fresh[:, width // 2 :]
        out_mine_ref[part, :] = jnp.where(feat == 0, low, high)
        out_other_ref[part, :] = jnp.where(feat == 0, high, low)
        added = dot(one_hot_columns(flat_row(receivers), layout.local_slots, 2 * group), fresh)
        sums[...] = added if at == 0 else sums[...] + added
    group_mine_ref[...] = sums[pl.ds(pl.multiple_of(feat * group, group), group), :]
    group_other_ref[...] = sums[pl.ds(pl.multiple_of((1 - feat) * group, group), group), :].astype(BF16)


def merge_kernel(mine_ref, theirs_ref, *out_refs):
    at = 0
    for out_ref in out_refs:
        rows = out_ref.shape[0]
        part = slice(at, at + rows)
        out_ref[...] = (mine_ref[part, :] + theirs_ref[part, :].astype(F32)).astype(BF16)
        at += rows


def local_sums_kernel(mine_ref, other_ref, recv_ref, node_ref, wa_ref, wb_ref, sums_ref, pre_ref, block):
    width = node_ref.shape[1]
    share, half = mine_ref.shape
    used = sums_ref.shape[0]
    feat = lax.axis_index("feat")
    mine = other = None
    for at in range(0, share, block):
        part = slice(at, at + block)
        picks = one_hot_columns(flat_row(recv_ref[at // 128 : (at + block) // 128, :]), 0, used)
        new_mine, new_other = dot(picks, mine_ref[part, :]), dot(picks, other_ref[part, :])
        mine = new_mine if mine is None else mine + new_mine
        other = new_other if other is None else other + new_other
    sums_ref[:, :half] = jnp.where(feat == 0, mine, other)
    sums_ref[:, half:] = jnp.where(feat == 0, other, mine)
    pre_ref[:, :half] = dot(node_ref[...], wa_ref[:width, :])
    pre_ref[:, half:] = dot(node_ref[...], wb_ref[:width, :])


def receive_kernel(sums_ref, halo_ref, coarse_ref, *refs):
    *parts, own_ref, rounded_ref = refs
    node_count = own_ref.shape[0]
    coarse = coarse_ref.shape[0]
    coarse_row = coarse_ref[...].reshape(1, coarse)
    index_row = jnp.concatenate([lent_list(halo_ref[...])] + [coarse_row] * (len(parts) + 1), axis=1)
    returned = jnp.concatenate([part[...] for part in parts] + [sums_ref[node_count:, :].astype(BF16)], axis=0)
    own = sums_ref[:node_count, :] + dot(one_hot_columns(index_row, 0, node_count), returned)
    own_ref[...] = own
    rounded_ref[...] = own.astype(BF16)


def node_kernel(
    node_ref,
    own_ref,
    partner_ref,
    pre_ref,
    wa_ref,
    wb_ref,
    va_ref,
    vb_ref,
    gain_ref,
    mine_ref,
    theirs_ref,
    out_ref,
    edges_ref,
    sems,
):
    node_count, width = node_ref.shape
    half = wa_ref.shape[1]
    share = mine_ref.shape[0]
    feat = lax.axis_index("feat")
    placed = copies(
        [
            (source, edges_ref.at[pl.ds(pl.multiple_of(owner * share, share), share), :])
            for source, owner in ((mine_ref, feat), (theirs_ref, 1 - feat))
        ],
        sems,
    )
    received = (own_ref[...] + partner_ref[...].astype(F32)).astype(BF16)
    total = None
    for weight, second, col in ((wa_ref, va_ref, 0), (wb_ref, vb_ref, half)):
        pre = pre_ref[:, col : col + half] + dot(received, weight[width:, :])
        part = dot(silu_of_double(0.5 * pre).astype(BF16), second[...])
        total = part if total is None else total + part
    update = layer_norm(total, gain_ref[...].astype(F32).reshape(1, width))
    fresh = (node_ref[...].astype(F32) + update).astype(BF16)
    out_ref[...] = jnp.where(feat == 0, fresh[:, : width // 2], fresh[:, width // 2 :])
    for copy in placed:
        copy.wait()


def in_hbm(array):
    return pltpu.with_memory_space_constraint(array, pltpu.HBM)


VMEM_SPEC = pl.BlockSpec(memory_space=pltpu.VMEM)
ANY_SPEC = pl.BlockSpec(memory_space=pl.ANY)


def call(kernel, operands, in_specs, outputs, out_specs, flops, limit, scratch=()):
    return pl.pallas_call(
        kernel,
        in_specs=in_specs,
        out_specs=out_specs,
        out_shape=outputs,
        scratch_shapes=list(scratch),
        cost_estimate=pl.CostEstimate(flops=flops, bytes_accessed=4 * MIB, transcendentals=0),
        compiler_params=pltpu.CompilerParams(vmem_limit_bytes=limit * MIB),
    )(*operands)


def exchange_pairs(count):
    across = [(p + 1 if p % 2 else p - 1) % count for p in range(count)]
    rounds = [([p ^ 1 for p in range(count)], across)]
    for distance in range(2, count, 2):
        rounds.append(([p ^ distance for p in range(count)], [p ^ (distance + 1) for p in range(count)]))
    return [
        [(2 * p + feat, 2 * targets[p] + feat) for p in range(count) for feat, targets in enumerate(some)]
        for some in rounds
    ]


def on_device(
    node_latent,
    edge_latent,
    edge_senders,
    edge_receivers,
    halo_rows,
    coarse_rows,
    edge_counts,
    edge_w1,
    edge_w2,
    edge_gain,
    node_w1,
    node_w2,
    node_gain,
):
    node_count, width = node_latent.shape
    half = width // 2
    edge_count = edge_latent.shape[0]
    halo, coarse = halo_rows.shape[1], coarse_rows.shape[0]
    patches = lax.axis_size("patch")
    both = ("patch", "feat")
    layout = Layout(patches, node_count, halo, coarse)
    group, used, local_slots = layout.group, layout.used, layout.local_slots
    share = edge_count // 2
    block = 512
    dma = pltpu.SemaphoreType.DMA

    def shape(rows, columns, kind=BF16):
        return jax.ShapeDtypeStruct((rows, columns), kind)

    def like(array):
        return jax.ShapeDtypeStruct(array.shape, array.dtype)

    def swap(values):
        return lax.ppermute(values, "feat", FEAT_SWAP)

    edge_w1_b, edge_w2_b = swap(edge_w1), swap(edge_w2)

    lent, node, halo_lists, coarse_list = call(
        lend_kernel,
        [in_hbm(array) for array in (node_latent, halo_rows, coarse_rows)],
        [ANY_SPEC] * 3,
        [shape(halo + coarse, width), like(node_latent), like(halo_rows), like(coarse_rows)],
        [VMEM_SPEC] * 4,
        2 * node_count * (halo + coarse) * width,
        8,
        scratch=[dma((3,))],
    )
    pairs = exchange_pairs(patches)
    arrived = [lax.ppermute(lent, both, pairs[0])]
    for some in pairs[1:]:
        arrived.append(lax.ppermute(lent[halo:], both, some))

    index_rows = (edge_count // 128, 128)
    more = (edge_w2, edge_gain, node_w1, node_w2, node_gain)
    pre, latent, send, recv, w1, w2, e_gain, n_w1, n_w2, n_gain = call(
        functools.partial(local_kernel, layout=layout, block=block),
        [node, lent, edge_w1_b, edge_counts]
        + [
            in_hbm(array)
            for array in (
                edge_latent,
                edge_senders.reshape(index_rows),
                edge_receivers.reshape(index_rows),
                edge_w1,
                *more,
            )
        ],
        [VMEM_SPEC] * 3 + [pl.BlockSpec(memory_space=pltpu.SMEM)] + [ANY_SPEC] * (4 + len(more)),
        [
            shape(share, width, F32),
            shape(share, width),
            shape(share // 128, 128, jnp.int32),
            shape(share // 128, 128, jnp.int32),
            like(edge_w1),
        ]
        + [like(array) for array in more],
        [VMEM_SPEC] * (5 + len(more)),
        2 * width * width * share + 4 * used * width * width + 4 * share * local_slots * width,
        LIMIT,
        scratch=[
            pltpu.VMEM((2 * local_slots, width), BF16),
            dma((3 + len(more),)),
            dma((share // block,)),
        ],
    )
    *arrived, pre = lax.optimization_barrier((*arrived, pre))
    table_mine = jnp.concatenate(arrived, axis=0)
    table_theirs = swap(table_mine)
    node_w1_b, node_w2_b = swap(n_w1), swap(n_w2)

    mine, other, group_mine, group_other = call(
        functools.partial(edge_kernel, layout=layout, block=block),
        (pre, latent, send, recv, table_mine, table_theirs, w1, edge_w1_b, w2, edge_w2_b, e_gain),
        [VMEM_SPEC] * 11,
        [shape(share, half), shape(share, half), shape(group, width, F32), shape(group, width)],
        [VMEM_SPEC] * 4,
        2 * share * width * (width + 6 * group) + 8 * group * width * width,
        LIMIT,
        scratch=[pltpu.VMEM((4 * group, width), BF16), pltpu.VMEM((2 * group, width), F32)],
    )

    group_theirs = swap(group_other)
    sizes = [halo + coarse] + [coarse] * (len(pairs) - 1)
    outgoing = call(
        merge_kernel,
        (group_mine, group_theirs),
        [VMEM_SPEC] * 2,
        [shape(rows, width) for rows in sizes],
        [VMEM_SPEC] * len(sizes),
        group * width,
        8,
    )
    *outgoing, mine, other = lax.optimization_barrier((*outgoing, mine, other))
    back = [lax.ppermute(part, both, some) for part, some in zip(outgoing, pairs)]
    edges_theirs = swap(other)
    local_sums, node_pre = call(
        functools.partial(local_sums_kernel, block=block),
        (mine, other, recv, node, n_w1, node_w1_b),
        [VMEM_SPEC] * 6,
        [shape(used, width, F32), shape(node_count, width, F32)],
        [VMEM_SPEC] * 2,
        2 * share * width * used + 2 * node_count * width * width,
        16,
    )
    own, rounded = call(
        receive_kernel,
        (local_sums, halo_lists, coarse_list, *back),
        [VMEM_SPEC] * (3 + len(sizes)),
        [shape(node_count, width, F32), shape(node_count, width)],
        [VMEM_SPEC] * 2,
        2 * node_count * width * (group + coarse),
        16,
    )
    partner = swap(rounded)
    nodes_out, edges_out = call(
        node_kernel,
        (node, own, partner, node_pre, n_w1, node_w1_b, n_w2, node_w2_b, n_gain, mine, edges_theirs),
        [VMEM_SPEC] * 9 + [ANY_SPEC] * 2,
        [shape(node_count, half), shape(edge_count, half)],
        [VMEM_SPEC, ANY_SPEC],
        4 * node_count * width * width,
        16,
        scratch=[dma((2,))],
    )
    return nodes_out, edges_out


def solution(mesh):
    placed = (
        P(("member", "patch"), None),
        P(("member", "patch"), None),
        P(("member", "patch")),
        P(("member", "patch")),
        P(("member", "patch"), None),
        P(("member", "patch")),
        P(("member", "patch")),
        P(None, "feat"),
        P("feat", None),
        P(),
        P(None, "feat"),
        P("feat", None),
        P(),
    )
    return jax.shard_map(
        on_device,
        mesh=mesh,
        in_specs=placed,
        out_specs=(P(("member", "patch"), "feat"), P(("member", "patch"), "feat")),
        check_vma=False,
    )
```

```python
import functools

import jax
import jax.numpy as jnp
from jax import lax
from jax.experimental import pallas as pl
from jax.experimental.pallas import tpu as pltpu
from jax.sharding import PartitionSpec as P

EPSILON = 1e-05
F32 = jnp.float32
BF16 = jnp.bfloat16
MIB = 1024 * 1024
LIMIT = 30
BESIDE = 10
DEAD = -1
NOWHERE = -2
FEAT_SWAP = [(0, 1), (1, 0)]


def silu_of_double(half_v):
    return half_v + half_v * jnp.tanh(half_v)


def dot(a, b):
    return jnp.dot(a, b, preferred_element_type=F32)


def layer_norm(pre, gain, keep=None):
    width = pre.shape[1]
    center = jnp.sum(pre, axis=1, keepdims=True) * (1.0 / width)
    square = jnp.sum(pre * pre, axis=1, keepdims=True) * (1.0 / width)
    scale = lax.rsqrt(square - center * center + EPSILON)
    if keep is not None:
        scale = jnp.where(keep, scale, 0.0)
    return (pre - center) * scale * gain


def index_columns(index):
    return [
        jnp.transpose(jnp.broadcast_to(index[j : j + 1, :], (128, 128))) for j in range(index.shape[0])
    ]


def one_hot_rows(columns, first, count):
    lanes = lax.broadcasted_iota(jnp.int32, (128, 128), 1) + first
    return jnp.concatenate(
        [
            jnp.concatenate(
                [(column == lanes + at).astype(F32).astype(BF16) for at in range(0, count, 128)], axis=1
            )
            for column in columns
        ],
        axis=0,
    )


def one_hot_columns(index_row, first, count):
    entries = index_row.shape[1]
    rows = lax.broadcasted_iota(jnp.int32, (count, entries), 0) + first
    return (rows == jnp.broadcast_to(index_row, (count, entries))).astype(F32).astype(BF16)


def flat_row(index):
    return jnp.concatenate([index[j : j + 1, :] for j in range(index.shape[0])], axis=1)


def copies(pairs, sems):
    made = [pltpu.make_async_copy(source, target, sems.at[i]) for i, (source, target) in enumerate(pairs)]
    for copy in made:
        copy.start()
    return made


class Layout:
    def __init__(self, patches, node_count, halo, coarse):
        self.patches, self.node_count, self.halo, self.coarse = patches, node_count, halo, coarse
        self.group = halo + coarse * (patches // 2)
        self.used = node_count + coarse
        self.local_slots = -(-self.used // 256) * 256

    def slots(self, rows, patch, feat):
        node_count, halo, coarse, group = self.node_count, self.halo, self.coarse, self.group
        at = rows - (node_count + 2 * halo)
        owner, entry = lax.shift_right_arithmetic(at, coarse.bit_length() - 1), at & (coarse - 1)
        distance = patch ^ owner
        even = 1 - (patch & 1)
        core0 = self.local_slots + feat * group
        place = self.local_slots + ((distance & 1) ^ feat) * group + halo
        place = place + coarse * lax.shift_right_arithmetic(distance, 1)
        place = jnp.where(distance == 0, node_count, place)
        place = jnp.where(distance == 1, core0 + halo, place) + entry
        lower = self.local_slots + (even ^ feat) * group - node_count + rows
        upper = self.local_slots + (1 - (even ^ feat)) * group - (node_count + halo) + rows
        lower = jnp.where(patch == 0, NOWHERE, lower)
        upper = jnp.where(patch == self.patches - 1, NOWHERE, upper)
        place = jnp.where(rows < node_count + 2 * halo, upper, place)
        place = jnp.where(rows < node_count + halo, lower, place)
        return jnp.where(rows < node_count, rows, place)


def lent_list(lists):
    which = (lax.axis_index("feat") + lax.axis_index("patch")) & 1
    return jnp.where(which == 0, lists[0:1], lists[1:2])


def lend_kernel(*refs, share):
    (node_hbm, halo_hbm, coarse_hbm, wa_hbm, send_hbm, recv_hbm), refs = refs[:6], refs[6:]
    lent_ref, node, halo, coarse, wa, send, recv, sems = refs
    rows128 = share // 128
    mine = pl.ds(pl.multiple_of(lax.axis_index("feat") * rows128, rows128), rows128)
    loads = copies(
        (
            (halo_hbm, halo),
            (coarse_hbm, coarse),
            (node_hbm, node),
            (wa_hbm, wa),
            (send_hbm.at[mine, :], send),
            (recv_hbm.at[mine, :], recv),
        ),
        sems,
    )
    for copy in loads[:3]:
        copy.wait()
    index_row = jnp.concatenate([lent_list(halo[...]), coarse[...].reshape(1, -1)], axis=1)
    lent_ref[...] = lax.dot_general(
        one_hot_columns(index_row, 0, node.shape[0]),
        node[...],
        (((0,), (0,)), ((), ())),
        preferred_element_type=F32,
    ).astype(BF16)
    for copy in loads[3:]:
        copy.wait()


def local_part(at, block, latent, send, recv, wa, wb, table):
    part, some = slice(at, at + block), slice(at // 128, (at + block) // 128)
    half = wa.shape[1]
    width = latent.shape[1]
    slots = table.shape[0] // 2
    picks = jnp.concatenate(
        [one_hot_rows(index_columns(index[some, :]), 0, slots) for index in (send, recv)], axis=1
    )
    return jnp.concatenate(
        [
            0.5 * (dot(latent[part, :], weight[:width, :]) + dot(picks, table[:, col : col + half]))
            for weight, col in ((wa, 0), (wb, half))
        ],
        axis=1,
    )


def local_kernel(node, lent_ref, wa, wb, send_in, recv_in, limit, latent_hbm, *refs, layout, block):
    count = (len(refs) - 7) // 2
    more_hbm, refs = refs[:count], refs[count:]
    pre_ref, latent, send, recv, table, *more = refs[: 5 + count]
    sems, block_sems = refs[5 + count :]
    share, width = latent.shape
    half = wa.shape[1]
    feat, patch = lax.axis_index("feat"), lax.axis_index("patch")
    local_slots, used = layout.local_slots, layout.used
    blocks = copies(
        [
            (
                latent_hbm.at[pl.ds(pl.multiple_of(feat * share + at, block), block), :],
                latent.at[pl.ds(at, block), :],
            )
            for at in range(0, share, block)
        ],
        block_sems,
    )
    rest = copies(list(zip(more_hbm, more)), sems)
    rows_in = jnp.concatenate([node[...], lent_ref[lent_ref.shape[0] - layout.coarse :, :]], axis=0)
    for side in range(2):
        base = side * local_slots
        rows = slice((side + 1) * width, (side + 2) * width)
        for weight, col in ((wa, 0), (wb, half)):
            table[base : base + used, col : col + half] = dot(rows_in, weight[rows, :]).astype(BF16)
        table[base + used : base + local_slots, :] = jnp.zeros((local_slots - used, 2 * half), BF16)
    shape = send.shape
    edge = lax.broadcasted_iota(jnp.int32, shape, 0) * 128 + lax.broadcasted_iota(jnp.int32, shape, 1) + feat * share
    live = edge < limit[0]
    for index_in, index in ((send_in, send), (recv_in, recv)):
        index[...] = jnp.where(live, layout.slots(index_in[...], patch, feat), DEAD)
    for i, copy in enumerate(blocks):
        copy.wait()
        at = i * block
        if at < pre_ref.shape[0]:
            pre_ref[at : at + block, :] = local_part(at, block, latent, send, recv, wa, wb, table)
    for copy in rest:
        copy.wait()


def second_kernel(latent, send, recv, wa, wb, table, mine, pre_ref, projected, block):
    share, width = latent.shape
    half = wa.shape[1]
    done = share - pre_ref.shape[0]
    group = mine.shape[0]
    for at in range(done, share, block):
        pre_ref[at - done : at - done + block, :] = local_part(at, block, latent, send, recv, wa, wb, table)
    project(mine, wa, wb, projected)


def project(rows, wa, wb, out):
    group, width = rows.shape
    half = wa.shape[1]
    for side in range(2):
        part = slice((side + 1) * width, (side + 2) * width)
        for weight, col in ((wa, 0), (wb, half)):
            out[side * group : (side + 1) * group, col : col + half] = (
                0.5 * dot(rows[...], weight[part, :])
            ).astype(BF16)


def edge_kernel(
    pre_ref,
    pre2_ref,
    latent_ref,
    send_ref,
    recv_ref,
    mine_table,
    theirs_ref,
    wa_ref,
    wb_ref,
    va_ref,
    vb_ref,
    gain_ref,
    out_mine_ref,
    out_other_ref,
    group_mine_ref,
    group_other_ref,
    theirs_table,
    sums,
    layout,
    block,
):
    share, width = latent_ref.shape
    half = wa_ref.shape[1]
    group = layout.group
    feat = lax.axis_index("feat")
    project(theirs_ref, wa_ref, wb_ref, theirs_table)
    gain = gain_ref[...].astype(F32).reshape(1, width)
    for at in range(0, share, block):
        part = slice(at, at + block)
        some = slice(at // 128, (at + block) // 128)
        receivers = recv_ref[some, :]
        columns = [index_columns(send_ref[some, :]), index_columns(receivers)]
        first = pre_ref.shape[0]
        pre = pre_ref[part, :] if at < first else pre2_ref[at - first : at - first + block, :]
        for base, table in ((layout.local_slots, mine_table), (layout.local_slots + group, theirs_table)):
            picks = jnp.concatenate([one_hot_rows(column, base, group) for column in columns], axis=1)
            pre = pre + dot(picks, table[...])
        hidden = silu_of_double(pre).astype(BF16)
        pre = dot(hidden[:, :half], va_ref[...]) + dot(hidden[:, half:], vb_ref[...])
        live = jnp.concatenate([column[:, :1] for column in columns[1]], axis=0) != DEAD
        fresh = (latent_ref[part, :].astype(F32) + layer_norm(pre, gain, live)).astype(BF16)
        low, high = fresh[:, : width // 2], fresh[:, width // 2 :]
        out_mine_ref[part, :] = jnp.where(feat == 0, low, high)
        out_other_ref[part, :] = jnp.where(feat == 0, high, low)
        added = dot(one_hot_columns(flat_row(receivers), layout.local_slots, 2 * group), fresh)
        sums[...] = added if at == 0 else sums[...] + added
    group_mine_ref[...] = sums[:group, :]
    group_other_ref[...] = sums[group:, :].astype(BF16)


def merge_kernel(mine_ref, theirs_ref, *out_refs):
    at = 0
    for out_ref in out_refs:
        rows = out_ref.shape[0]
        part = slice(at, at + rows)
        out_ref[...] = (mine_ref[part, :] + theirs_ref[part, :].astype(F32)).astype(BF16)
        at += rows


def local_sums_kernel(mine_ref, other_ref, recv_ref, node_ref, wa_ref, wb_ref, sums_ref, pre_ref, block):
    width = node_ref.shape[1]
    share, half = mine_ref.shape
    used = sums_ref.shape[0]
    feat = lax.axis_index("feat")
    mine = other = None
    for at in range(0, share, block):
        part = slice(at, at + block)
        picks = one_hot_columns(flat_row(recv_ref[at // 128 : (at + block) // 128, :]), 0, used)
        new_mine, new_other = dot(picks, mine_ref[part, :]), dot(picks, other_ref[part, :])
        mine = new_mine if mine is None else mine + new_mine
        other = new_other if other is None else other + new_other
    sums_ref[:, :half] = jnp.where(feat == 0, mine, other)
    sums_ref[:, half:] = jnp.where(feat == 0, other, mine)
    pre_ref[:, :half] = dot(node_ref[...], wa_ref[:width, :])
    pre_ref[:, half:] = dot(node_ref[...], wb_ref[:width, :])


def receive_kernel(sums_ref, halo_ref, coarse_ref, *refs):
    *parts, own_ref, rounded_ref = refs
    node_count = own_ref.shape[0]
    coarse = coarse_ref.shape[0]
    coarse_row = coarse_ref[...].reshape(1, coarse)
    index_row = jnp.concatenate([lent_list(halo_ref[...])] + [coarse_row] * (len(parts) + 1), axis=1)
    returned = jnp.concatenate([part[...] for part in parts] + [sums_ref[node_count:, :].astype(BF16)], axis=0)
    own = sums_ref[:node_count, :] + dot(one_hot_columns(index_row, 0, node_count), returned)
    own_ref[...] = own
    rounded_ref[...] = own.astype(BF16)


def node_kernel(
    node_ref,
    own_ref,
    partner_ref,
    pre_ref,
    wa_ref,
    wb_ref,
    va_ref,
    vb_ref,
    gain_ref,
    mine_ref,
    theirs_ref,
    out_ref,
    edges_ref,
    sems,
):
    node_count, width = node_ref.shape
    half = wa_ref.shape[1]
    share = mine_ref.shape[0]
    feat = lax.axis_index("feat")
    placed = copies(
        [
            (source, edges_ref.at[pl.ds(pl.multiple_of(owner * share, share), share), :])
            for source, owner in ((mine_ref, feat), (theirs_ref, 1 - feat))
        ],
        sems,
    )
    received = (own_ref[...] + partner_ref[...].astype(F32)).astype(BF16)
    total = None
    for weight, second, col in ((wa_ref, va_ref, 0), (wb_ref, vb_ref, half)):
        pre = pre_ref[:, col : col + half] + dot(received, weight[width:, :])
        part = dot(silu_of_double(0.5 * pre).astype(BF16), second[...])
        total = part if total is None else total + part
    update = layer_norm(total, gain_ref[...].astype(F32).reshape(1, width))
    fresh = (node_ref[...].astype(F32) + update).astype(BF16)
    out_ref[...] = jnp.where(feat == 0, fresh[:, : width // 2], fresh[:, width // 2 :])
    for copy in placed:
        copy.wait()


def in_hbm(array):
    return pltpu.with_memory_space_constraint(array, pltpu.HBM)


VMEM_SPEC = pl.BlockSpec(memory_space=pltpu.VMEM)
ANY_SPEC = pl.BlockSpec(memory_space=pl.ANY)


def call(kernel, operands, in_specs, outputs, out_specs, flops, limit, scratch=()):
    return pl.pallas_call(
        kernel,
        in_specs=in_specs,
        out_specs=out_specs,
        out_shape=outputs,
        scratch_shapes=list(scratch),
        cost_estimate=pl.CostEstimate(flops=flops, bytes_accessed=MIB // 4, transcendentals=0),
        compiler_params=pltpu.CompilerParams(vmem_limit_bytes=limit * MIB),
    )(*operands)


def exchange_pairs(count):
    across = [(p + 1 if p % 2 else p - 1) % count for p in range(count)]
    rounds = [([p ^ 1 for p in range(count)], across)]
    for distance in range(2, count, 2):
        rounds.append(([p ^ distance for p in range(count)], [p ^ (distance + 1) for p in range(count)]))
    return [
        [(2 * p + feat, 2 * targets[p] + feat) for p in range(count) for feat, targets in enumerate(some)]
        for some in rounds
    ]


def on_device(
    node_latent,
    edge_latent,
    edge_senders,
    edge_receivers,
    halo_rows,
    coarse_rows,
    edge_counts,
    edge_w1,
    edge_w2,
    edge_gain,
    node_w1,
    node_w2,
    node_gain,
):
    node_count, width = node_latent.shape
    half = width // 2
    edge_count = edge_latent.shape[0]
    halo, coarse = halo_rows.shape[1], coarse_rows.shape[0]
    patches = lax.axis_size("patch")
    both = ("patch", "feat")
    layout = Layout(patches, node_count, halo, coarse)
    group, used, local_slots = layout.group, layout.used, layout.local_slots
    share = edge_count // 2
    block = 512
    dma = pltpu.SemaphoreType.DMA

    def shape(rows, columns, kind=BF16):
        return jax.ShapeDtypeStruct((rows, columns), kind)

    def like(array):
        return jax.ShapeDtypeStruct(array.shape, array.dtype)

    def swap(values):
        return lax.ppermute(values, "feat", FEAT_SWAP)

    edge_w1_b = swap(edge_w1)

    index_rows = (edge_count // 128, 128)
    core_rows = jax.ShapeDtypeStruct((share // 128, 128), jnp.int32)
    lent, node, halo_lists, coarse_list, w1, send, recv = call(
        functools.partial(lend_kernel, share=share),
        [
            in_hbm(array)
            for array in (
                node_latent,
                halo_rows,
                coarse_rows,
                edge_w1,
                edge_senders.reshape(index_rows),
                edge_receivers.reshape(index_rows),
            )
        ],
        [ANY_SPEC] * 6,
        [shape(halo + coarse, width)]
        + [like(array) for array in (node_latent, halo_rows, coarse_rows, edge_w1)]
        + [core_rows] * 2,
        [VMEM_SPEC] * 7,
        2 * node_count * (halo + coarse) * width,
        8,
        scratch=[dma((6,))],
    )
    pairs = exchange_pairs(patches)
    arrived = [
        lax.ppermute(lent[halo:] if i else lent, both, pairs[i]) for i in reversed(range(len(pairs)))
    ][::-1]

    more = (edge_w2, edge_gain, node_w1, node_w2, node_gain)
    first = share // 2
    pre, latent, send, recv, table, w2, e_gain, n_w1, n_w2, n_gain = call(
        functools.partial(local_kernel, layout=layout, block=block),
        [node, lent, w1, edge_w1_b, send, recv, edge_counts] + [in_hbm(array) for array in (edge_latent, *more)],
        [VMEM_SPEC] * 6 + [pl.BlockSpec(memory_space=pltpu.SMEM)] + [ANY_SPEC] * (1 + len(more)),
        [
            shape(first, width, F32),
            shape(share, width),
            core_rows,
            core_rows,
            shape(2 * local_slots, width),
        ]
        + [like(array) for array in more],
        [VMEM_SPEC] * (5 + len(more)),
        (2 * width * width * first + 4 * used * width * width + 4 * first * local_slots * width) // BESIDE,
        LIMIT,
        scratch=[dma((len(more),)), dma((share // block,))],
    )
    pre, *arrived = lax.optimization_barrier((pre, *arrived))
    table_mine = jnp.concatenate(arrived, axis=0)
    table_theirs = swap(table_mine)
    edge_w2_b = swap(w2)
    pre2, projected = call(
        functools.partial(second_kernel, block=block),
        (latent, send, recv, w1, edge_w1_b, table, table_mine),
        [VMEM_SPEC] * 7,
        [shape(share - first, width, F32), shape(2 * group, width)],
        [VMEM_SPEC] * 2,
        2 * width * width * (share - first) + 4 * (share - first) * local_slots * width + 4 * group * width * width,
        LIMIT,
    )
    n_w1_b, n_w2_b = lax.optimization_barrier((n_w1, n_w2, pre2))[:2]
    node_w1_b, node_w2_b = swap(n_w1_b), swap(n_w2_b)

    mine, other, group_mine, group_other = call(
        functools.partial(edge_kernel, layout=layout, block=block),
        (pre, pre2, latent, send, recv, projected, table_theirs, w1, edge_w1_b, w2, edge_w2_b, e_gain),
        [VMEM_SPEC] * 12,
        [shape(share, half), shape(share, half), shape(group, width, F32), shape(group, width)],
        [VMEM_SPEC] * 4,
        2 * share * width * (width + 6 * group) + 4 * group * width * width,
        LIMIT,
        scratch=[pltpu.VMEM((2 * group, width), BF16), pltpu.VMEM((2 * group, width), F32)],
    )
    node_w1_b, node_w2_b, mine, other, group_mine, group_other = lax.optimization_barrier(
        (node_w1_b, node_w2_b, mine, other, group_mine, group_other)
    )

    group_theirs = swap(group_other)
    sizes = [halo + coarse] + [coarse] * (len(pairs) - 1)
    outgoing = call(
        merge_kernel,
        (group_mine, group_theirs),
        [VMEM_SPEC] * 2,
        [shape(rows, width) for rows in sizes],
        [VMEM_SPEC] * len(sizes),
        group * width,
        8,
    )
    *outgoing, mine, other = lax.optimization_barrier((*outgoing, mine, other))
    back = [lax.ppermute(outgoing[i], both, pairs[i]) for i in reversed(range(len(pairs)))][::-1]
    local_sums, node_pre = call(
        functools.partial(local_sums_kernel, block=block),
        (mine, other, recv, node, n_w1, node_w1_b),
        [VMEM_SPEC] * 6,
        [shape(used, width, F32), shape(node_count, width, F32)],
        [VMEM_SPEC] * 2,
        (2 * share * width * used + 2 * node_count * width * width) // BESIDE,
        16,
    )
    edges_theirs = swap(other)
    local_sums, *back = lax.optimization_barrier((local_sums, *back[::-1]))
    back = back[::-1]
    own, rounded = call(
        receive_kernel,
        (local_sums, halo_lists, coarse_list, *back),
        [VMEM_SPEC] * (3 + len(sizes)),
        [shape(node_count, width, F32), shape(node_count, width)],
        [VMEM_SPEC] * 2,
        2 * node_count * width * (group + coarse),
        16,
    )
    partner = swap(rounded)
    nodes_out, edges_out = call(
        node_kernel,
        (node, own, partner, node_pre, n_w1, node_w1_b, n_w2, node_w2_b, n_gain, mine, edges_theirs),
        [VMEM_SPEC] * 9 + [ANY_SPEC] * 2,
        [shape(node_count, half), shape(edge_count, half)],
        [VMEM_SPEC, ANY_SPEC],
        4 * node_count * width * width,
        16,
        scratch=[dma((2,))],
    )
    return nodes_out, edges_out


def solution(mesh):
    placed = (
        P(("member", "patch"), None),
        P(("member", "patch"), None),
        P(("member", "patch")),
        P(("member", "patch")),
        P(("member", "patch"), None),
        P(("member", "patch")),
        P(("member", "patch")),
        P(None, "feat"),
        P("feat", None),
        P(),
        P(None, "feat"),
        P("feat", None),
        P(),
    )
    return jax.shard_map(
        on_device,
        mesh=mesh,
        in_specs=placed,
        out_specs=(P(("member", "patch"), "feat"), P(("member", "patch"), "feat")),
        check_vma=False,
    )
```

```python
import functools

import jax
import jax.numpy as jnp
from jax import lax
from jax.experimental import pallas as pl
from jax.experimental.pallas import tpu as pltpu
from jax.sharding import PartitionSpec as P

EPSILON = 1e-05
F32 = jnp.float32
BF16 = jnp.bfloat16
MIB = 1024 * 1024
LIMIT = 30
BESIDE = 10
DEAD = -1
NOWHERE = -2
FEAT_SWAP = [(0, 1), (1, 0)]


def silu_of_double(half_v):
    return half_v + half_v * jnp.tanh(half_v)


def dot(a, b):
    return jnp.dot(a, b, preferred_element_type=F32)


def lane_sums(x):
    high = x.astype(BF16)
    low = (x - high.astype(F32)).astype(BF16)
    ones = jnp.ones((128, 128), BF16)
    return dot(high, ones) + dot(low, ones)


def layer_norm(pre, gain, keep=None):
    width = pre.shape[1]
    parts = [pre[:, at : at + 128] for at in range(0, width, 128)]
    center = jnp.sum(sum(parts), axis=1, keepdims=True) * (1.0 / width)
    square = jnp.sum(sum(part * part for part in parts), axis=1, keepdims=True) * (1.0 / width)
    scale = lax.rsqrt(square - center * center + EPSILON)
    if keep is not None:
        scale = jnp.where(keep, scale, 0.0)
    shift = -center * scale
    return jnp.concatenate(
        [(part * scale + shift) * gain[:, at * 128 : at * 128 + 128] for at, part in enumerate(parts)], axis=1
    )


def index_columns(index):
    return [
        jnp.transpose(jnp.broadcast_to(index[j : j + 1, :], (128, 128))) for j in range(index.shape[0])
    ]


def one_hot_rows(columns, first, count):
    lanes = lax.broadcasted_iota(jnp.int32, (128, 128), 1) + first
    return jnp.concatenate(
        [
            jnp.concatenate(
                [(column == lanes + at).astype(F32).astype(BF16) for at in range(0, count, 128)], axis=1
            )
            for column in columns
        ],
        axis=0,
    )


def one_hot_columns(index_row, first, count):
    entries = index_row.shape[1]
    rows = lax.broadcasted_iota(jnp.int32, (count, entries), 0) + first
    return (rows == jnp.broadcast_to(index_row, (count, entries))).astype(F32).astype(BF16)


def flat_row(index):
    return jnp.concatenate([index[j : j + 1, :] for j in range(index.shape[0])], axis=1)


def copies(pairs, sems):
    made = [pltpu.make_async_copy(source, target, sems.at[i]) for i, (source, target) in enumerate(pairs)]
    for copy in made:
        copy.start()
    return made


class Layout:
    def __init__(self, rounds, node_count, halo, coarse):
        self.patches = len(rounds[0][0])
        self.node_count, self.halo, self.coarse = node_count, halo, coarse
        self.group = halo + coarse * len(rounds)
        self.used = node_count + coarse
        self.local_slots = -(-self.used // 256) * 256
        self.code = [[0] * self.patches for _ in range(self.patches)]
        for i, some in reversed(list(enumerate(rounds))):
            for core, targets in enumerate(some):
                for patch, owner in enumerate(targets):
                    self.code[patch][owner] = (core << 16) + halo + coarse * i

    def slots(self, rows, patch, feat):
        node_count, halo, coarse, group = self.node_count, self.halo, self.coarse, self.group
        at = rows - (node_count + 2 * halo)
        owner, entry = lax.shift_right_arithmetic(at, coarse.bit_length() - 1), at & (coarse - 1)
        place = jnp.zeros_like(rows)
        for q in range(self.patches):
            code = jnp.int32(0)
            for p in range(self.patches):
                code = jnp.where(patch == p, self.code[p][q], code)
            remote = self.local_slots + (lax.shift_right_arithmetic(code, 16) ^ feat) * group + (code & 0xFFFF)
            place = jnp.where(owner == q, jnp.where(patch == q, node_count, remote), place)
        place = place + entry
        even = 1 - (patch & 1)
        lower = self.local_slots + (even ^ feat) * group - node_count + rows
        upper = self.local_slots + (1 - (even ^ feat)) * group - (node_count + halo) + rows
        lower = jnp.where(patch == 0, NOWHERE, lower)
        upper = jnp.where(patch == self.patches - 1, NOWHERE, upper)
        place = jnp.where(rows < node_count + 2 * halo, upper, place)
        place = jnp.where(rows < node_count + halo, lower, place)
        return jnp.where(rows < node_count, rows, place)


def lent_list(lists):
    which = (lax.axis_index("feat") + lax.axis_index("patch")) & 1
    return jnp.where(which == 0, lists[0:1], lists[1:2])


def lend_kernel(*refs, share, layout):
    (node_hbm, halo_hbm, coarse_hbm, wa_hbm, send_hbm, recv_hbm), refs = refs[:6], refs[6:]
    lent_ref, node, halo, coarse, wa, send, recv, sems = refs
    rows128 = share // 128
    feat, patch = lax.axis_index("feat"), lax.axis_index("patch")
    mine = pl.ds(pl.multiple_of(feat * rows128, rows128), rows128)
    loads = copies(
        (
            (halo_hbm, halo),
            (coarse_hbm, coarse),
            (node_hbm, node),
            (send_hbm.at[mine, :], send),
            (recv_hbm.at[mine, :], recv),
            (wa_hbm, wa),
        ),
        sems,
    )
    for copy in loads[:3]:
        copy.wait()
    index_row = jnp.concatenate([lent_list(halo[...]), coarse[...].reshape(1, -1)], axis=1)
    lent_ref[...] = lax.dot_general(
        one_hot_columns(index_row, 0, node.shape[0]),
        node[...],
        (((0,), (0,)), ((), ())),
        preferred_element_type=F32,
    ).astype(BF16)
    for copy in loads[3:5]:
        copy.wait()
    for index in (send, recv):
        index[...] = layout.slots(index[...], patch, feat)
    loads[5].wait()


def local_part(at, block, latent, send, recv, wa, wb, table, before=None):
    part, some = slice(at, at + block), slice(at // 128, (at + block) // 128)
    half = wa.shape[1]
    width = latent.shape[1]
    slots = table.shape[0] // 2
    picks = jnp.concatenate(
        [one_hot_rows(index_columns(index[some, :]), 0, slots) for index in (send, recv)], axis=1
    )
    picked = [dot(picks, table[:, col : col + half]) for col in (0, half)]
    if before is not None:
        before.wait()
    rows = latent[part, :]
    return jnp.concatenate(
        [0.5 * (some + dot(rows, weight[:width, :])) for some, weight in zip(picked, (wa, wb))], axis=1
    )


def local_kernel(node, lent_ref, wa, wb, send, recv, latent_hbm, *refs, layout, block):
    count = (len(refs) - 5) // 2
    more_hbm, refs = refs[:count], refs[count:]
    pre_ref, latent, table, *more = refs[: 3 + count]
    sems, block_sems = refs[3 + count :]
    share, width = latent.shape
    half = wa.shape[1]
    feat = lax.axis_index("feat")
    local_slots, used = layout.local_slots, layout.used
    first = pre_ref.shape[0]
    blocks = [
        (latent_hbm.at[pl.ds(pl.multiple_of(feat * share + at, block), block), :], latent.at[pl.ds(at, block), :])
        for at in range(0, share, block)
    ]
    early = copies(blocks[: first // block], block_sems)
    rows_in = jnp.concatenate([node[...], lent_ref[lent_ref.shape[0] - layout.coarse :, :]], axis=0)
    for side in range(2):
        base = side * local_slots
        rows = slice((side + 1) * width, (side + 2) * width)
        for weight, col in ((wa, 0), (wb, half)):
            table[base : base + used, col : col + half] = dot(rows_in, weight[rows, :]).astype(BF16)
        table[base + used : base + local_slots, :] = jnp.zeros((local_slots - used, 2 * half), BF16)
    rest = copies(blocks[first // block :] + list(zip(more_hbm, more)), sems)
    for i, copy in enumerate(early):
        at = i * block
        pre_ref[at : at + block, :] = local_part(at, block, latent, send, recv, wa, wb, table, copy)
    for copy in rest:
        copy.wait()


def second_kernel(latent, send, recv, wa, wb, table, mine, pre_ref, projected, block):
    share, width = latent.shape
    half = wa.shape[1]
    done = share - pre_ref.shape[0]
    group = mine.shape[0]
    for at in range(done, share, block):
        pre_ref[at - done : at - done + block, :] = local_part(at, block, latent, send, recv, wa, wb, table)
    project(mine, wa, wb, projected)


def project(rows, wa, wb, out):
    group, width = rows.shape
    half = wa.shape[1]
    for side in range(2):
        part = slice((side + 1) * width, (side + 2) * width)
        for weight, col in ((wa, 0), (wb, half)):
            out[side * group : (side + 1) * group, col : col + half] = (
                0.5 * dot(rows[...], weight[part, :])
            ).astype(BF16)


def edge_kernel(
    limit_ref,
    pre_ref,
    pre2_ref,
    latent_ref,
    send_ref,
    recv_ref,
    mine_table,
    theirs_ref,
    wa_ref,
    wb_ref,
    va_ref,
    vb_ref,
    gain_ref,
    out_mine_ref,
    out_other_ref,
    fresh_all,
    group_other_ref,
    live_recv_ref,
    theirs_table,
    layout,
    block,
):
    share, width = latent_ref.shape
    half = wa_ref.shape[1]
    group = layout.group
    feat = lax.axis_index("feat")
    project(theirs_ref, wa_ref, wb_ref, theirs_table)
    shape = recv_ref.shape
    edge = lax.broadcasted_iota(jnp.int32, shape, 0) * 128 + lax.broadcasted_iota(jnp.int32, shape, 1) + feat * share
    live_recv_ref[...] = jnp.where(edge < limit_ref[0], recv_ref[...], DEAD)
    gain = gain_ref[...].astype(F32).reshape(1, width)
    for at in range(0, share, block):
        part = slice(at, at + block)
        some = slice(at // 128, (at + block) // 128)
        receivers = live_recv_ref[some, :]
        columns = [index_columns(send_ref[some, :]), index_columns(receivers)]
        first = pre_ref.shape[0]
        pre = pre_ref[part, :] if at < first else pre2_ref[at - first : at - first + block, :]
        for base, table in ((layout.local_slots, mine_table), (layout.local_slots + group, theirs_table)):
            picks = jnp.concatenate([one_hot_rows(column, base, group) for column in columns], axis=1)
            pre = pre + dot(picks, table[...])
        hidden = silu_of_double(pre).astype(BF16)
        pre = dot(hidden[:, :half], va_ref[...]) + dot(hidden[:, half:], vb_ref[...])
        live = jnp.concatenate(columns[1], axis=0) != DEAD
        fresh = (latent_ref[part, :].astype(F32) + layer_norm(pre, gain, live)).astype(BF16)
        low, high = fresh[:, : width // 2], fresh[:, width // 2 :]
        out_mine_ref[part, :] = jnp.where(feat == 0, low, high)
        out_other_ref[part, :] = jnp.where(feat == 0, high, low)
        fresh_all[part, :] = fresh
    receivers = flat_row(live_recv_ref[...])
    group_other_ref[...] = dot(one_hot_columns(receivers, layout.local_slots + group, group), fresh_all[...]).astype(BF16)


def group_sums_kernel(fresh_ref, recv_ref, sums_ref, first):
    sums_ref[...] = dot(one_hot_columns(flat_row(recv_ref[...]), first, sums_ref.shape[0]), fresh_ref[...])


def merge_kernel(mine_ref, theirs_ref, *out_refs):
    at = 0
    for out_ref in out_refs:
        rows = out_ref.shape[0]
        part = slice(at, at + rows)
        out_ref[...] = (mine_ref[part, :] + theirs_ref[part, :].astype(F32)).astype(BF16)
        at += rows


def local_sums_kernel(fresh_ref, recv_ref, node_ref, wa_ref, wb_ref, sums_ref, pre_ref):
    width = node_ref.shape[1]
    half = wa_ref.shape[1]
    sums_ref[...] = dot(one_hot_columns(flat_row(recv_ref[...]), 0, sums_ref.shape[0]), fresh_ref[...])
    pre_ref[:, :half] = dot(node_ref[...], wa_ref[:width, :])
    pre_ref[:, half:] = dot(node_ref[...], wb_ref[:width, :])


def receive_kernel(sums_ref, halo_ref, coarse_ref, *refs):
    *parts, own_ref, rounded_ref = refs
    node_count = own_ref.shape[0]
    coarse = coarse_ref.shape[0]
    coarse_row = coarse_ref[...].reshape(1, coarse)
    index_row = jnp.concatenate([lent_list(halo_ref[...])] + [coarse_row] * (len(parts) + 1), axis=1)
    returned = jnp.concatenate([part[...] for part in parts] + [sums_ref[node_count:, :].astype(BF16)], axis=0)
    own = sums_ref[:node_count, :] + dot(one_hot_columns(index_row, 0, node_count), returned)
    own_ref[...] = own
    rounded_ref[...] = own.astype(BF16)


def node_kernel(
    node_ref,
    own_ref,
    partner_ref,
    pre_ref,
    wa_ref,
    wb_ref,
    va_ref,
    vb_ref,
    gain_ref,
    mine_ref,
    theirs_ref,
    out_ref,
    edges_ref,
    sems,
):
    node_count, width = node_ref.shape
    half = wa_ref.shape[1]
    share = mine_ref.shape[0]
    feat = lax.axis_index("feat")
    placed = copies(
        [
            (source, edges_ref.at[pl.ds(pl.multiple_of(owner * share, share), share), :])
            for source, owner in ((mine_ref, feat), (theirs_ref, 1 - feat))
        ],
        sems,
    )
    received = (own_ref[...] + partner_ref[...].astype(F32)).astype(BF16)
    total = None
    for weight, second, col in ((wa_ref, va_ref, 0), (wb_ref, vb_ref, half)):
        pre = pre_ref[:, col : col + half] + dot(received, weight[width:, :])
        part = dot(silu_of_double(0.5 * pre).astype(BF16), second[...])
        total = part if total is None else total + part
    update = layer_norm(total, gain_ref[...].astype(F32).reshape(1, width))
    fresh = (node_ref[...].astype(F32) + update).astype(BF16)
    out_ref[...] = jnp.where(feat == 0, fresh[:, : width // 2], fresh[:, width // 2 :])
    for copy in placed:
        copy.wait()


def in_hbm(array):
    return pltpu.with_memory_space_constraint(array, pltpu.HBM)


VMEM_SPEC = pl.BlockSpec(memory_space=pltpu.VMEM)
ANY_SPEC = pl.BlockSpec(memory_space=pl.ANY)


def call(kernel, operands, in_specs, outputs, out_specs, flops, limit, scratch=()):
    return pl.pallas_call(
        kernel,
        in_specs=in_specs,
        out_specs=out_specs,
        out_shape=outputs,
        scratch_shapes=list(scratch),
        cost_estimate=pl.CostEstimate(flops=flops, bytes_accessed=MIB // 4, transcendentals=0),
        compiler_params=pltpu.CompilerParams(vmem_limit_bytes=limit * MIB),
    )(*operands)


def pairing(count, pairs):
    targets = [None] * count
    for p, q in pairs:
        targets[p], targets[q] = q, p
    return targets


def exchange_rounds(count):
    across = [(p + 1 if p % 2 else p - 1) % count for p in range(count)]
    apart = lambda distance: [p ^ distance for p in range(count)]
    rounds = [(apart(1), across)]
    if count == 8:
        mixed = pairing(count, [(0, 3), (4, 7), (1, 6), (2, 5)])
        return rounds + [(apart(4), apart(5)), (apart(2), apart(2)), (apart(6), mixed)]
    return rounds + [(apart(distance), apart(distance + 1)) for distance in range(2, count, 2)]


def exchange_pairs(rounds):
    count = len(rounds[0][0])
    return [
        [(2 * p + feat, 2 * targets[p] + feat) for p in range(count) for feat, targets in enumerate(some)]
        for some in rounds
    ]


def on_device(
    node_latent,
    edge_latent,
    edge_senders,
    edge_receivers,
    halo_rows,
    coarse_rows,
    edge_counts,
    edge_w1,
    edge_w2,
    edge_gain,
    node_w1,
    node_w2,
    node_gain,
):
    node_count, width = node_latent.shape
    half = width // 2
    edge_count = edge_latent.shape[0]
    halo, coarse = halo_rows.shape[1], coarse_rows.shape[0]
    patches = lax.axis_size("patch")
    both = ("patch", "feat")
    rounds = exchange_rounds(patches)
    layout = Layout(rounds, node_count, halo, coarse)
    group, used, local_slots = layout.group, layout.used, layout.local_slots
    share = edge_count // 2
    block = 512
    dma = pltpu.SemaphoreType.DMA

    def shape(rows, columns, kind=BF16):
        return jax.ShapeDtypeStruct((rows, columns), kind)

    def like(array):
        return jax.ShapeDtypeStruct(array.shape, array.dtype)

    def swap(values):
        return lax.ppermute(values, "feat", FEAT_SWAP)

    edge_w1_b = swap(edge_w1)

    index_rows = (edge_count // 128, 128)
    core_rows = jax.ShapeDtypeStruct((share // 128, 128), jnp.int32)
    lent, node, halo_lists, coarse_list, w1, send, recv = call(
        functools.partial(lend_kernel, share=share, layout=layout),
        [
            in_hbm(array)
            for array in (
                node_latent,
                halo_rows,
                coarse_rows,
                edge_w1,
                edge_senders.reshape(index_rows),
                edge_receivers.reshape(index_rows),
            )
        ],
        [ANY_SPEC] * 6,
        [shape(halo + coarse, width)]
        + [like(array) for array in (node_latent, halo_rows, coarse_rows, edge_w1)]
        + [core_rows] * 2,
        [VMEM_SPEC] * 7,
        2 * node_count * (halo + coarse) * width,
        8,
        scratch=[dma((6,))],
    )
    pairs = exchange_pairs(rounds)
    arrived = [
        lax.ppermute(lent[halo:] if i else lent, both, pairs[i]) for i in reversed(range(len(pairs)))
    ][::-1]

    more = (edge_w2, edge_gain, node_w1, node_w2, node_gain)
    first = share // 2
    pre, latent, table, w2, e_gain, n_w1, n_w2, n_gain = call(
        functools.partial(local_kernel, layout=layout, block=block),
        [node, lent, w1, edge_w1_b, send, recv] + [in_hbm(array) for array in (edge_latent, *more)],
        [VMEM_SPEC] * 6 + [ANY_SPEC] * (1 + len(more)),
        [
            shape(first, width, F32),
            shape(share, width),
            shape(2 * local_slots, width),
        ]
        + [like(array) for array in more],
        [VMEM_SPEC] * (3 + len(more)),
        (2 * width * width * first + 4 * used * width * width + 4 * first * local_slots * width) // BESIDE,
        LIMIT,
        scratch=[dma((len(more) + (share - first) // block,)), dma((first // block,))],
    )
    pre, *arrived = lax.optimization_barrier((pre, *arrived))
    table_mine = jnp.concatenate(arrived, axis=0)
    table_theirs = swap(table_mine)
    edge_w2_b = swap(w2)
    pre2, projected = call(
        functools.partial(second_kernel, block=block),
        (latent, send, recv, w1, edge_w1_b, table, table_mine),
        [VMEM_SPEC] * 7,
        [shape(share - first, width, F32), shape(2 * group, width)],
        [VMEM_SPEC] * 2,
        2 * width * width * (share - first) + 4 * (share - first) * local_slots * width + 4 * group * width * width,
        LIMIT,
    )
    n_w1_b, n_w2_b = lax.optimization_barrier((n_w1, n_w2, pre2))[:2]
    node_w1_b, node_w2_b = swap(n_w1_b), swap(n_w2_b)

    mine, other, fresh, group_other, live_recv = call(
        functools.partial(edge_kernel, layout=layout, block=block),
        (edge_counts, pre, pre2, latent, send, recv, projected, table_theirs, w1, edge_w1_b, w2, edge_w2_b, e_gain),
        [pl.BlockSpec(memory_space=pltpu.SMEM)] + [VMEM_SPEC] * 12,
        [shape(share, half), shape(share, half), shape(share, width), shape(group, width), core_rows],
        [VMEM_SPEC] * 5,
        2 * share * width * (width + 6 * group) + 4 * group * width * width,
        LIMIT,
        scratch=[pltpu.VMEM((2 * group, width), BF16)],
    )
    node_w1_b, node_w2_b, mine, other, fresh, group_other = lax.optimization_barrier(
        (node_w1_b, node_w2_b, mine, other, fresh, group_other)
    )

    group_theirs = swap(group_other)
    group_mine = call(
        functools.partial(group_sums_kernel, first=local_slots),
        (fresh, live_recv),
        [VMEM_SPEC] * 2,
        shape(group, width, F32),
        VMEM_SPEC,
        2 * share * width * group,
        16,
    )
    sizes = [halo + coarse] + [coarse] * (len(pairs) - 1)
    outgoing = call(
        merge_kernel,
        (group_mine, group_theirs),
        [VMEM_SPEC] * 2,
        [shape(rows, width) for rows in sizes],
        [VMEM_SPEC] * len(sizes),
        group * width,
        8,
    )
    *outgoing, mine, other, fresh = lax.optimization_barrier((*outgoing, mine, other, fresh))
    back = [lax.ppermute(outgoing[i], both, pairs[i]) for i in reversed(range(len(pairs)))][::-1]
    local_sums, node_pre = call(
        local_sums_kernel,
        (fresh, live_recv, node, n_w1, node_w1_b),
        [VMEM_SPEC] * 5,
        [shape(used, width, F32), shape(node_count, width, F32)],
        [VMEM_SPEC] * 2,
        (2 * share * width * used + 2 * node_count * width * width) // BESIDE,
        16,
    )
    edges_theirs = swap(other)
    local_sums, *back = lax.optimization_barrier((local_sums, *back[::-1]))
    back = back[::-1]
    own, rounded = call(
        receive_kernel,
        (local_sums, halo_lists, coarse_list, *back),
        [VMEM_SPEC] * (3 + len(sizes)),
        [shape(node_count, width, F32), shape(node_count, width)],
        [VMEM_SPEC] * 2,
        2 * node_count * width * (group + coarse),
        16,
    )
    partner = swap(rounded)
    nodes_out, edges_out = call(
        node_kernel,
        (node, own, partner, node_pre, n_w1, node_w1_b, n_w2, node_w2_b, n_gain, mine, edges_theirs),
        [VMEM_SPEC] * 9 + [ANY_SPEC] * 2,
        [shape(node_count, half), shape(edge_count, half)],
        [VMEM_SPEC, ANY_SPEC],
        4 * node_count * width * width,
        16,
        scratch=[dma((2,))],
    )
    return nodes_out, edges_out


def solution(mesh):
    placed = (
        P(("member", "patch"), None),
        P(("member", "patch"), None),
        P(("member", "patch")),
        P(("member", "patch")),
        P(("member", "patch"), None),
        P(("member", "patch")),
        P(("member", "patch")),
        P(None, "feat"),
        P("feat", None),
        P(),
        P(None, "feat"),
        P("feat", None),
        P(),
    )
    return jax.shard_map(
        on_device,
        mesh=mesh,
        in_specs=placed,
        out_specs=(P(("member", "patch"), "feat"), P(("member", "patch"), "feat")),
        check_vma=False,
    )
```

```python
import functools

import jax
import jax.numpy as jnp
from jax import lax
from jax.experimental import pallas as pl
from jax.experimental.pallas import tpu as pltpu
from jax.sharding import PartitionSpec as P

EPSILON = 1e-05
F32 = jnp.float32
BF16 = jnp.bfloat16
MIB = 1024 * 1024
LIMIT = 30
BESIDE = 10
DEAD = -1
NOWHERE = -2
FEAT_SWAP = [(0, 1), (1, 0)]


def silu_of_double(half_v):
    return half_v + half_v * jnp.tanh(half_v)


def dot(a, b):
    return jnp.dot(a, b, preferred_element_type=F32)


def lane_sums(x):
    high = x.astype(BF16)
    low = (x - high.astype(F32)).astype(BF16)
    ones = jnp.ones((128, 128), BF16)
    return dot(high, ones) + dot(low, ones)


def layer_norm(pre, gain, keep=None):
    width = pre.shape[1]
    parts = [pre[:, at : at + 128] for at in range(0, width, 128)]
    center = jnp.sum(sum(parts), axis=1, keepdims=True) * (1.0 / width)
    square = jnp.sum(sum(part * part for part in parts), axis=1, keepdims=True) * (1.0 / width)
    scale = lax.rsqrt(square - center * center + EPSILON)
    if keep is not None:
        scale = jnp.where(keep, scale, 0.0)
    shift = -center * scale
    return jnp.concatenate(
        [(part * scale + shift) * gain[:, at * 128 : at * 128 + 128] for at, part in enumerate(parts)], axis=1
    )


def index_columns(index):
    return [
        jnp.transpose(jnp.broadcast_to(index[j : j + 1, :], (128, 128))) for j in range(index.shape[0])
    ]


def one_hot_rows(columns, first, count):
    lanes = lax.broadcasted_iota(jnp.int32, (128, 128), 1) + first
    return jnp.concatenate(
        [
            jnp.concatenate(
                [(column == lanes + at).astype(F32).astype(BF16) for at in range(0, count, 128)], axis=1
            )
            for column in columns
        ],
        axis=0,
    )


def one_hot_columns(index_row, first, count):
    entries = index_row.shape[1]
    rows = lax.broadcasted_iota(jnp.int32, (count, entries), 0) + first
    return (rows == jnp.broadcast_to(index_row, (count, entries))).astype(F32).astype(BF16)


def flat_row(index):
    return jnp.concatenate([index[j : j + 1, :] for j in range(index.shape[0])], axis=1)


def copies(pairs, sems):
    made = [pltpu.make_async_copy(source, target, sems.at[i]) for i, (source, target) in enumerate(pairs)]
    for copy in made:
        copy.start()
    return made


class Layout:
    def __init__(self, rounds, node_count, halo, coarse):
        self.patches = len(rounds[0][0])
        self.node_count, self.halo, self.coarse = node_count, halo, coarse
        self.group = halo + coarse * len(rounds)
        self.local_slots = -(-node_count // 128) * 128
        self.code = [[0] * self.patches for _ in range(self.patches)]
        for i, some in reversed(list(enumerate(rounds))):
            for core, targets in enumerate(some):
                for patch, owner in enumerate(targets):
                    self.code[patch][owner] = (core << 16) + halo + coarse * i

    def slots(self, rows, patch, feat, own):
        node_count, halo, coarse, group = self.node_count, self.halo, self.coarse, self.group
        at = rows - (node_count + 2 * halo)
        owner, entry = lax.shift_right_arithmetic(at, coarse.bit_length() - 1), at & (coarse - 1)
        place = jnp.zeros_like(rows)
        for q in range(self.patches):
            code = jnp.int32(0)
            for p in range(self.patches):
                code = jnp.where(patch == p, self.code[p][q], code)
            remote = self.local_slots + (lax.shift_right_arithmetic(code, 16) ^ feat) * group + (code & 0xFFFF)
            place = jnp.where(owner == q, remote, place)
        place = place + entry
        for i in range(coarse):
            place = jnp.where((owner == patch) & (entry == i), own[i], place)
        even = 1 - (patch & 1)
        lower = self.local_slots + (even ^ feat) * group - node_count + rows
        upper = self.local_slots + (1 - (even ^ feat)) * group - (node_count + halo) + rows
        lower = jnp.where(patch == 0, NOWHERE, lower)
        upper = jnp.where(patch == self.patches - 1, NOWHERE, upper)
        place = jnp.where(rows < node_count + 2 * halo, upper, place)
        place = jnp.where(rows < node_count + halo, lower, place)
        return jnp.where(rows < node_count, rows, place)


def lent_list(lists):
    which = (lax.axis_index("feat") + lax.axis_index("patch")) & 1
    return jnp.where(which == 0, lists[0:1], lists[1:2])


def lend_kernel(*refs, share, layout):
    (node_hbm, halo_hbm, coarse_hbm, wa_hbm, send_hbm, recv_hbm, latent_hbm), refs = refs[:7], refs[7:]
    lent_ref, node, halo, coarse, wa, send, recv, latent, own, sems = refs
    rows128 = share // 128
    feat, patch = lax.axis_index("feat"), lax.axis_index("patch")
    mine = pl.ds(pl.multiple_of(feat * rows128, rows128), rows128)
    loads = copies(
        (
            (halo_hbm, halo),
            (coarse_hbm, coarse),
            (node_hbm, node),
            (send_hbm.at[mine, :], send),
            (recv_hbm.at[mine, :], recv),
            (coarse_hbm, own),
            (wa_hbm, wa),
            (latent_hbm.at[pl.ds(pl.multiple_of(feat * share, share), latent.shape[0]), :], latent),
        ),
        sems,
    )
    for copy in loads[:3]:
        copy.wait()
    index_row = jnp.concatenate([lent_list(halo[...]), coarse[...].reshape(1, -1)], axis=1)
    lent_ref[...] = lax.dot_general(
        one_hot_columns(index_row, 0, node.shape[0]),
        node[...],
        (((0,), (0,)), ((), ())),
        preferred_element_type=F32,
    ).astype(BF16)
    for copy in loads[3:6]:
        copy.wait()
    for index in (send, recv):
        index[...] = layout.slots(index[...], patch, feat, own)
    for copy in loads[6:]:
        copy.wait()


def local_part(at, block, latent, send, recv, wa, wb, table, before=None):
    part, some = slice(at, at + block), slice(at // 128, (at + block) // 128)
    half = wa.shape[1]
    width = latent.shape[1]
    slots = table.shape[0] // 2
    picks = jnp.concatenate(
        [one_hot_rows(index_columns(index[some, :]), 0, slots) for index in (send, recv)], axis=1
    )
    picked = [dot(picks, table[:, col : col + half]) for col in (0, half)]
    if before is not None:
        before.wait()
    rows = latent[part, :]
    return jnp.concatenate(
        [0.5 * (some + dot(rows, weight[:width, :])) for some, weight in zip(picked, (wa, wb))], axis=1
    )


def local_kernel(node, wa, wb, send, recv, early_latent, latent_hbm, *refs, layout, block):
    count = (len(refs) - 5) // 2
    more_hbm, refs = refs[:count], refs[count:]
    pre_ref, latent, table, *more = refs[: 3 + count]
    sems, block_sems = refs[3 + count :]
    share, width = latent.shape
    half = wa.shape[1]
    feat = lax.axis_index("feat")
    local_slots, used = layout.local_slots, layout.node_count
    first = pre_ref.shape[0]
    blocks = [
        (latent_hbm.at[pl.ds(pl.multiple_of(feat * share + at, block), block), :], latent.at[pl.ds(at, block), :])
        for at in range(block, share, block)
    ]
    wanted = first // block - 1
    early = copies(blocks[:wanted], block_sems)
    latent[:block, :] = early_latent[...]
    for side in range(2):
        base = side * local_slots
        rows = slice((side + 1) * width, (side + 2) * width)
        for weight, col in ((wa, 0), (wb, half)):
            table[base : base + used, col : col + half] = dot(node[...], weight[rows, :]).astype(BF16)
        if used < local_slots:
            table[base + used : base + local_slots, :] = jnp.zeros((local_slots - used, 2 * half), BF16)
    rest = copies(blocks[wanted:] + list(zip(more_hbm, more)), sems)
    for i, copy in enumerate([None] + early):
        at = i * block
        pre_ref[at : at + block, :] = local_part(at, block, latent, send, recv, wa, wb, table, copy)
    for copy in rest:
        copy.wait()


def second_kernel(latent, send, recv, wa, wb, table, mine, *refs, block):
    count = (len(refs) - 3) // 2
    more_hbm, pre_ref, projected, more, sems = refs[:count], refs[count], refs[count + 1], refs[count + 2 : -1], refs[-1]
    rest = copies(list(zip(more_hbm, more)), sems)
    share, width = latent.shape
    half = wa.shape[1]
    done = share - pre_ref.shape[0]
    group = mine.shape[0]
    for at in range(done, share, block):
        pre_ref[at - done : at - done + block, :] = local_part(at, block, latent, send, recv, wa, wb, table)
    project(mine, wa, wb, projected)
    for copy in rest:
        copy.wait()


def project(rows, wa, wb, out, at=0):
    group, width = rows.shape
    half = wa.shape[1]
    for side in range(2):
        part = slice((side + 1) * width, (side + 2) * width)
        for weight, col in ((wa, 0), (wb, half)):
            out[at + side * group : at + (side + 1) * group, col : col + half] = (
                0.5 * dot(rows[...], weight[part, :])
            ).astype(BF16)


def edge_kernel(
    limit_ref,
    pre_ref,
    pre2_ref,
    latent_ref,
    send_ref,
    recv_ref,
    mine_table,
    theirs_ref,
    wa_ref,
    wb_ref,
    va_ref,
    vb_ref,
    gain_ref,
    out_mine_ref,
    out_other_ref,
    fresh_all,
    group_other_ref,
    live_recv_ref,
    table,
    layout,
    block,
):
    share, width = latent_ref.shape
    half = wa_ref.shape[1]
    group = layout.group
    feat = lax.axis_index("feat")
    table[: 2 * group, :] = mine_table[...]
    project(theirs_ref, wa_ref, wb_ref, table, 2 * group)
    shape = recv_ref.shape
    edge = lax.broadcasted_iota(jnp.int32, shape, 0) * 128 + lax.broadcasted_iota(jnp.int32, shape, 1) + feat * share
    live_recv_ref[...] = jnp.where(edge < limit_ref[...], recv_ref[...], DEAD)
    gain = gain_ref[...].astype(F32).reshape(1, width)
    for at in range(0, share, block):
        part = slice(at, at + block)
        some = slice(at // 128, (at + block) // 128)
        receivers = live_recv_ref[some, :]
        columns = [index_columns(send_ref[some, :]), index_columns(receivers)]
        first = pre_ref.shape[0]
        pre = pre_ref[part, :] if at < first else pre2_ref[at - first : at - first + block, :]
        picks = jnp.concatenate(
            [
                one_hot_rows(column, base, group)
                for base in (layout.local_slots, layout.local_slots + group)
                for column in columns
            ],
            axis=1,
        )
        hidden = silu_of_double(pre + dot(picks, table[...])).astype(BF16)
        pre = dot(hidden[:, :half], va_ref[...]) + dot(hidden[:, half:], vb_ref[...])
        live = jnp.concatenate(columns[1], axis=0) != DEAD
        fresh = (latent_ref[part, :].astype(F32) + layer_norm(pre, gain, live)).astype(BF16)
        low, high = fresh[:, : width // 2], fresh[:, width // 2 :]
        out_mine_ref[part, :] = jnp.where(feat == 0, low, high)
        out_other_ref[part, :] = jnp.where(feat == 0, high, low)
        fresh_all[part, :] = fresh
    receivers = flat_row(live_recv_ref[...])
    group_other_ref[...] = dot(one_hot_columns(receivers, layout.local_slots + group, group), fresh_all[...]).astype(BF16)


def group_sums_kernel(fresh_ref, recv_ref, sums_ref, first):
    sums_ref[...] = dot(one_hot_columns(flat_row(recv_ref[...]), first, sums_ref.shape[0]), fresh_ref[...])


def merge_kernel(mine_ref, theirs_ref, *out_refs):
    at = 0
    for out_ref in out_refs:
        rows = out_ref.shape[0]
        part = slice(at, at + rows)
        out_ref[...] = (mine_ref[part, :] + theirs_ref[part, :].astype(F32)).astype(BF16)
        at += rows


def local_sums_kernel(fresh_ref, recv_ref, sums_ref):
    sums_ref[...] = dot(one_hot_columns(flat_row(recv_ref[...]), 0, sums_ref.shape[0]), fresh_ref[...])


def beside_kernel(node_ref, wa_ref, wb_ref, mine_ref, theirs_ref, pre_ref, edges_ref, sems):
    width = node_ref.shape[1]
    half = wa_ref.shape[1]
    share = mine_ref.shape[0]
    feat = lax.axis_index("feat")
    placed = copies(
        [
            (source, edges_ref.at[pl.ds(pl.multiple_of(owner * share, share), share), :])
            for source, owner in ((mine_ref, feat), (theirs_ref, 1 - feat))
        ],
        sems,
    )
    for weight, col in ((wa_ref, 0), (wb_ref, half)):
        pre_ref[:, col : col + half] = 0.5 * dot(node_ref[...], weight[:width, :])
    for copy in placed:
        copy.wait()


def receive_kernel(sums_ref, halo_ref, coarse_ref, *refs):
    *parts, own_ref, rounded_ref = refs
    coarse = coarse_ref.shape[0]
    coarse_row = coarse_ref[...].reshape(1, coarse)
    index_row = jnp.concatenate([lent_list(halo_ref[...])] + [coarse_row] * len(parts), axis=1)
    returned = jnp.concatenate([part[...] for part in parts], axis=0)
    own = sums_ref[...] + dot(one_hot_columns(index_row, 0, own_ref.shape[0]), returned)
    own_ref[...] = own
    rounded_ref[...] = own.astype(BF16)


def node_kernel(node_ref, own_ref, partner_ref, pre_ref, wa_ref, wb_ref, va_ref, vb_ref, gain_ref, out_ref):
    width = node_ref.shape[1]
    half = wa_ref.shape[1]
    feat = lax.axis_index("feat")
    received = (own_ref[...] + partner_ref[...].astype(F32)).astype(BF16)
    total = None
    for weight, second, col in ((wa_ref, va_ref, 0), (wb_ref, vb_ref, half)):
        pre = pre_ref[:, col : col + half] + 0.5 * dot(received, weight[width:, :])
        part = dot(silu_of_double(pre).astype(BF16), second[...])
        total = part if total is None else total + part
    update = layer_norm(total, gain_ref[...].astype(F32).reshape(1, width))
    fresh = (node_ref[...].astype(F32) + update).astype(BF16)
    out_ref[...] = jnp.where(feat == 0, fresh[:, : width // 2], fresh[:, width // 2 :])


def in_hbm(array):
    return pltpu.with_memory_space_constraint(array, pltpu.HBM)


VMEM_SPEC = pl.BlockSpec(memory_space=pltpu.VMEM)
ANY_SPEC = pl.BlockSpec(memory_space=pl.ANY)


def call(kernel, operands, in_specs, outputs, out_specs, flops, limit, scratch=()):
    return pl.pallas_call(
        kernel,
        in_specs=in_specs,
        out_specs=out_specs,
        out_shape=outputs,
        scratch_shapes=list(scratch),
        cost_estimate=pl.CostEstimate(flops=flops, bytes_accessed=MIB // 4, transcendentals=0),
        compiler_params=pltpu.CompilerParams(vmem_limit_bytes=limit * MIB),
    )(*operands)


def pairing(count, pairs):
    targets = [None] * count
    for p, q in pairs:
        targets[p], targets[q] = q, p
    return targets


def exchange_rounds(count):
    across = [(p + 1 if p % 2 else p - 1) % count for p in range(count)]
    apart = lambda distance: [p ^ distance for p in range(count)]
    rounds = [(apart(1), across)]
    if count == 8:
        mixed = pairing(count, [(0, 3), (4, 7), (1, 6), (2, 5)])
        return rounds + [(apart(4), apart(5)), (apart(2), apart(2)), (apart(6), mixed)]
    return rounds + [(apart(distance), apart(distance + 1)) for distance in range(2, count, 2)]


def exchange_pairs(rounds):
    count = len(rounds[0][0])
    return [
        [(2 * p + feat, 2 * targets[p] + feat) for p in range(count) for feat, targets in enumerate(some)]
        for some in rounds
    ]


def on_device(
    node_latent,
    edge_latent,
    edge_senders,
    edge_receivers,
    halo_rows,
    coarse_rows,
    edge_counts,
    edge_w1,
    edge_w2,
    edge_gain,
    node_w1,
    node_w2,
    node_gain,
):
    node_count, width = node_latent.shape
    half = width // 2
    edge_count = edge_latent.shape[0]
    halo, coarse = halo_rows.shape[1], coarse_rows.shape[0]
    patches = lax.axis_size("patch")
    both = ("patch", "feat")
    rounds = exchange_rounds(patches)
    layout = Layout(rounds, node_count, halo, coarse)
    group, local_slots = layout.group, layout.local_slots
    share = edge_count // 2
    block = 512
    dma = pltpu.SemaphoreType.DMA

    def shape(rows, columns, kind=BF16):
        return jax.ShapeDtypeStruct((rows, columns), kind)

    def like(array):
        return jax.ShapeDtypeStruct(array.shape, array.dtype)

    def swap(values):
        return lax.ppermute(values, "feat", FEAT_SWAP)

    edge_w1_b = swap(edge_w1)

    index_rows = (edge_count // 128, 128)
    core_rows = jax.ShapeDtypeStruct((share // 128, 128), jnp.int32)
    lent, node, halo_lists, coarse_list, w1, send, recv, early_latent = call(
        functools.partial(lend_kernel, share=share, layout=layout),
        [
            in_hbm(array)
            for array in (
                node_latent,
                halo_rows,
                coarse_rows,
                edge_w1,
                edge_senders.reshape(index_rows),
                edge_receivers.reshape(index_rows),
                edge_latent,
            )
        ],
        [ANY_SPEC] * 7,
        [shape(halo + coarse, width)]
        + [like(array) for array in (node_latent, halo_rows, coarse_rows, edge_w1)]
        + [core_rows] * 2
        + [shape(block, width)],
        [VMEM_SPEC] * 8,
        2 * node_count * (halo + coarse) * width,
        8,
        scratch=[pltpu.SMEM((coarse,), jnp.int32), dma((8,))],
    )
    pairs = exchange_pairs(rounds)
    arrived = [
        lax.ppermute(lent[halo:] if i else lent, both, pairs[i]) for i in reversed(range(len(pairs)))
    ][::-1]

    more = (edge_w2, edge_gain)
    later = (node_w1, node_w2, node_gain)
    first = share * 3 // 4
    pre, latent, table, w2, e_gain = call(
        functools.partial(local_kernel, layout=layout, block=block),
        [node, w1, edge_w1_b, send, recv, early_latent] + [in_hbm(array) for array in (edge_latent, *more)],
        [VMEM_SPEC] * 6 + [ANY_SPEC] * (1 + len(more)),
        [
            shape(first, width, F32),
            shape(share, width),
            shape(2 * local_slots, width),
        ]
        + [like(array) for array in more],
        [VMEM_SPEC] * (3 + len(more)),
        (2 * width * width * first + 4 * node_count * width * width + 4 * first * local_slots * width) // BESIDE,
        LIMIT,
        scratch=[dma((len(more) + (share - first) // block,)), dma((first // block,))],
    )
    pre, *arrived = lax.optimization_barrier((pre, *arrived))
    table_mine = jnp.concatenate(arrived, axis=0)
    table_theirs = swap(table_mine)
    edge_w2_b = swap(w2)
    pre2, projected, n_w1, n_w2, n_gain = call(
        functools.partial(second_kernel, block=block),
        [latent, send, recv, w1, edge_w1_b, table, table_mine] + [in_hbm(array) for array in later],
        [VMEM_SPEC] * 7 + [ANY_SPEC] * len(later),
        [shape(share - first, width, F32), shape(2 * group, width)] + [like(array) for array in later],
        [VMEM_SPEC] * (2 + len(later)),
        2 * width * width * (share - first) + 4 * (share - first) * local_slots * width + 4 * group * width * width,
        LIMIT,
        scratch=[dma((len(later),))],
    )
    n_w1_b, n_w2_b = lax.optimization_barrier((n_w1, n_w2, pre2))[:2]
    node_w1_b, node_w2_b = swap(n_w1_b), swap(n_w2_b)

    mine, other, fresh, group_other, live_recv = call(
        functools.partial(edge_kernel, layout=layout, block=block),
        (edge_counts.reshape(1, 1), pre, pre2, latent, send, recv, projected, table_theirs, w1, edge_w1_b, w2, edge_w2_b, e_gain),
        [VMEM_SPEC] * 13,
        [shape(share, half), shape(share, half), shape(share, width), shape(group, width), core_rows],
        [VMEM_SPEC] * 5,
        2 * share * width * (width + 6 * group) + 4 * group * width * width,
        LIMIT,
        scratch=[pltpu.VMEM((4 * group, width), BF16)],
    )
    node_w1_b, node_w2_b, mine, other, fresh, group_other = lax.optimization_barrier(
        (node_w1_b, node_w2_b, mine, other, fresh, group_other)
    )

    group_theirs = swap(group_other)
    group_mine = call(
        functools.partial(group_sums_kernel, first=local_slots),
        (fresh, live_recv),
        [VMEM_SPEC] * 2,
        shape(group, width, F32),
        VMEM_SPEC,
        2 * share * width * group,
        16,
    )
    sizes = [halo + coarse] + [coarse] * (len(pairs) - 1)
    outgoing = call(
        merge_kernel,
        (group_mine, group_theirs),
        [VMEM_SPEC] * 2,
        [shape(rows, width) for rows in sizes],
        [VMEM_SPEC] * len(sizes),
        group * width,
        8,
    )
    *outgoing, mine, other, fresh = lax.optimization_barrier((*outgoing, mine, other, fresh))
    back = [lax.ppermute(outgoing[i], both, pairs[i]) for i in reversed(range(len(pairs)))][::-1]
    local_sums = call(
        local_sums_kernel,
        (fresh, live_recv),
        [VMEM_SPEC] * 2,
        shape(node_count, width, F32),
        VMEM_SPEC,
        2 * share * width * node_count // BESIDE,
        16,
    )
    edges_theirs = swap(other)
    local_sums, *back = lax.optimization_barrier((local_sums, *back[::-1]))
    back = back[::-1]
    own, rounded = call(
        receive_kernel,
        (local_sums, halo_lists, coarse_list, *back),
        [VMEM_SPEC] * (3 + len(sizes)),
        [shape(node_count, width, F32), shape(node_count, width)],
        [VMEM_SPEC] * 2,
        2 * node_count * width * group,
        16,
    )
    partner = swap(rounded)
    mine, edges_theirs, node = lax.optimization_barrier((mine, edges_theirs, node, rounded))[:3]
    node_pre, edges_out = call(
        beside_kernel,
        (node, n_w1, node_w1_b, mine, edges_theirs),
        [VMEM_SPEC] * 3 + [ANY_SPEC] * 2,
        [shape(node_count, width, F32), shape(edge_count, half)],
        [VMEM_SPEC, ANY_SPEC],
        2 * node_count * width * width,
        16,
        scratch=[dma((2,))],
    )
    nodes_out = call(
        node_kernel,
        (node, own, partner, node_pre, n_w1, node_w1_b, n_w2, node_w2_b, n_gain),
        [VMEM_SPEC] * 9,
        shape(node_count, half),
        VMEM_SPEC,
        4 * node_count * width * width,
        16,
    )
    return nodes_out, edges_out


def solution(mesh):
    placed = (
        P(("member", "patch"), None),
        P(("member", "patch"), None),
        P(("member", "patch")),
        P(("member", "patch")),
        P(("member", "patch"), None),
        P(("member", "patch")),
        P(("member", "patch")),
        P(None, "feat"),
        P("feat", None),
        P(),
        P(None, "feat"),
        P("feat", None),
        P(),
    )
    return jax.shard_map(
        on_device,
        mesh=mesh,
        in_specs=placed,
        out_specs=(P(("member", "patch"), "feat"), P(("member", "patch"), "feat")),
        check_vma=False,
    )
```

```python
import functools

import jax
import jax.numpy as jnp
from jax import lax
from jax.experimental import pallas as pl
from jax.experimental.pallas import tpu as pltpu
from jax.sharding import PartitionSpec as P

EPSILON = 1e-05
F32 = jnp.float32
BF16 = jnp.bfloat16
MIB = 1024 * 1024
LIMIT = 30
BESIDE = 10
DEAD = -1
NOWHERE = -2
FEAT_SWAP = [(0, 1), (1, 0)]


def silu_of_double(half_v):
    return half_v + half_v * jnp.tanh(half_v)


def dot(a, b):
    return jnp.dot(a, b, preferred_element_type=F32)


def lane_sums(x):
    high = x.astype(BF16)
    low = (x - high.astype(F32)).astype(BF16)
    ones = jnp.ones((128, 128), BF16)
    return dot(high, ones) + dot(low, ones)


def layer_norm(pre, gain, keep=None):
    width = pre.shape[1]
    parts = [pre[:, at : at + 128] for at in range(0, width, 128)]
    center = jnp.sum(sum(parts), axis=1, keepdims=True) * (1.0 / width)
    square = jnp.sum(sum(part * part for part in parts), axis=1, keepdims=True) * (1.0 / width)
    scale = lax.rsqrt(square - center * center + EPSILON)
    if keep is not None:
        scale = jnp.where(keep, scale, 0.0)
    shift = -center * scale
    return jnp.concatenate(
        [(part * scale + shift) * gain[:, at * 128 : at * 128 + 128] for at, part in enumerate(parts)], axis=1
    )


def index_columns(index):
    return [
        jnp.transpose(jnp.broadcast_to(index[j : j + 1, :], (128, 128))) for j in range(index.shape[0])
    ]


def one_hot_rows(columns, first, count):
    lanes = lax.broadcasted_iota(jnp.int32, (128, 128), 1) + first
    return jnp.concatenate(
        [
            jnp.concatenate(
                [(column == lanes + at).astype(F32).astype(BF16) for at in range(0, count, 128)], axis=1
            )
            for column in columns
        ],
        axis=0,
    )


def one_hot_columns(index_row, first, count):
    entries = index_row.shape[1]
    rows = lax.broadcasted_iota(jnp.int32, (count, entries), 0) + first
    return (rows == jnp.broadcast_to(index_row, (count, entries))).astype(F32).astype(BF16)


def flat_row(index):
    return jnp.concatenate([index[j : j + 1, :] for j in range(index.shape[0])], axis=1)


def copies(pairs, sems):
    made = [pltpu.make_async_copy(source, target, sems.at[i]) for i, (source, target) in enumerate(pairs)]
    for copy in made:
        copy.start()
    return made


class Layout:
    def __init__(self, rounds, node_count, halo, coarse):
        self.patches = len(rounds[0][0])
        self.node_count, self.halo, self.coarse = node_count, halo, coarse
        self.group = halo + coarse * len(rounds)
        self.local_slots = -(-node_count // 128) * 128
        self.code = [[0] * self.patches for _ in range(self.patches)]
        for i, some in reversed(list(enumerate(rounds))):
            for core, targets in enumerate(some):
                for patch, owner in enumerate(targets):
                    self.code[patch][owner] = (core << 16) + halo + coarse * i

    def slots(self, rows, patch, feat, own):
        node_count, halo, coarse, group = self.node_count, self.halo, self.coarse, self.group
        at = rows - (node_count + 2 * halo)
        owner, entry = lax.shift_right_arithmetic(at, coarse.bit_length() - 1), at & (coarse - 1)
        place = jnp.zeros_like(rows)
        for q in range(self.patches):
            code = jnp.int32(0)
            for p in range(self.patches):
                code = jnp.where(patch == p, self.code[p][q], code)
            remote = self.local_slots + (lax.shift_right_arithmetic(code, 16) ^ feat) * group + (code & 0xFFFF)
            place = jnp.where(owner == q, remote, place)
        place = place + entry
        for i in range(coarse):
            place = jnp.where((owner == patch) & (entry == i), own[i], place)
        even = 1 - (patch & 1)
        lower = self.local_slots + (even ^ feat) * group - node_count + rows
        upper = self.local_slots + (1 - (even ^ feat)) * group - (node_count + halo) + rows
        lower = jnp.where(patch == 0, NOWHERE, lower)
        upper = jnp.where(patch == self.patches - 1, NOWHERE, upper)
        place = jnp.where(rows < node_count + 2 * halo, upper, place)
        place = jnp.where(rows < node_count + halo, lower, place)
        return jnp.where(rows < node_count, rows, place)


def lent_list(lists):
    which = (lax.axis_index("feat") + lax.axis_index("patch")) & 1
    return jnp.where(which == 0, lists[0:1], lists[1:2])


def lend_kernel(*refs, share, layout):
    (node_hbm, halo_hbm, coarse_hbm, wa_hbm, send_hbm, recv_hbm, latent_hbm), refs = refs[:7], refs[7:]
    lent_ref, node, halo, coarse, wa, send, recv, latent, own, sems = refs
    rows128 = share // 128
    feat, patch = lax.axis_index("feat"), lax.axis_index("patch")
    mine = pl.ds(pl.multiple_of(feat * rows128, rows128), rows128)
    loads = copies(
        (
            (halo_hbm, halo),
            (coarse_hbm, coarse),
            (node_hbm, node),
            (send_hbm.at[mine, :], send),
            (recv_hbm.at[mine, :], recv),
            (coarse_hbm, own),
            (wa_hbm, wa),
            (latent_hbm.at[pl.ds(pl.multiple_of(feat * share, share), latent.shape[0]), :], latent),
        ),
        sems,
    )
    for copy in loads[:3]:
        copy.wait()
    index_row = jnp.concatenate([lent_list(halo[...]), coarse[...].reshape(1, -1)], axis=1)
    lent_ref[...] = lax.dot_general(
        one_hot_columns(index_row, 0, node.shape[0]),
        node[...],
        (((0,), (0,)), ((), ())),
        preferred_element_type=F32,
    ).astype(BF16)
    for copy in loads[3:6]:
        copy.wait()
    for index in (send, recv):
        index[...] = layout.slots(index[...], patch, feat, own)
    for copy in loads[6:]:
        copy.wait()


def local_part(at, block, latent, send, recv, wa, wb, table, before=None):
    part, some = slice(at, at + block), slice(at // 128, (at + block) // 128)
    half = wa.shape[1]
    width = latent.shape[1]
    slots = table.shape[0] // 2
    picks = jnp.concatenate(
        [one_hot_rows(index_columns(index[some, :]), 0, slots) for index in (send, recv)], axis=1
    )
    picked = [dot(picks, table[:, col : col + half]) for col in (0, half)]
    if before is not None:
        before.wait()
    rows = latent[part, :]
    return jnp.concatenate(
        [0.5 * (some + dot(rows, weight[:width, :])) for some, weight in zip(picked, (wa, wb))], axis=1
    )


def local_kernel(limit_ref, node, wa, wb, send, recv, early_latent, latent_hbm, *refs, layout, block):
    count = (len(refs) - 6) // 2
    more_hbm, refs = refs[:count], refs[count:]
    pre_ref, latent, table, live_ref, *more = refs[: 4 + count]
    sems, block_sems = refs[4 + count :]
    share, width = latent.shape
    half = wa.shape[1]
    feat = lax.axis_index("feat")
    local_slots, used = layout.local_slots, layout.node_count
    first = pre_ref.shape[0]
    blocks = [
        (latent_hbm.at[pl.ds(pl.multiple_of(feat * share + at, block), block), :], latent.at[pl.ds(at, block), :])
        for at in range(block, share, block)
    ]
    wanted = first // block - 1
    early = copies(blocks[:wanted], block_sems)
    latent[:block, :] = early_latent[...]
    for side in range(2):
        base = side * local_slots
        rows = slice((side + 1) * width, (side + 2) * width)
        for weight, col in ((wa, 0), (wb, half)):
            table[base : base + used, col : col + half] = dot(node[...], weight[rows, :]).astype(BF16)
        if used < local_slots:
            table[base + used : base + local_slots, :] = jnp.zeros((local_slots - used, 2 * half), BF16)
    shape = recv.shape
    edge = lax.broadcasted_iota(jnp.int32, shape, 0) * 128 + lax.broadcasted_iota(jnp.int32, shape, 1) + feat * share
    live_ref[...] = jnp.where(edge < limit_ref[...], recv[...], DEAD)
    rest = copies(blocks[wanted:] + list(zip(more_hbm, more)), sems)
    for i, copy in enumerate([None] + early):
        at = i * block
        pre_ref[at : at + block, :] = local_part(at, block, latent, send, recv, wa, wb, table, copy)
    for copy in rest:
        copy.wait()


def second_kernel(latent, send, recv, wa, wb, table, mine, pre_ref, projected, block):
    share, width = latent.shape
    half = wa.shape[1]
    done = share - pre_ref.shape[0]
    group = mine.shape[0]
    for at in range(done, share, block):
        pre_ref[at - done : at - done + block, :] = local_part(at, block, latent, send, recv, wa, wb, table)
    project(mine, wa, wb, projected)


def project(rows, wa, wb, out, at=0):
    group, width = rows.shape
    half = wa.shape[1]
    for side in range(2):
        part = slice((side + 1) * width, (side + 2) * width)
        for weight, col in ((wa, 0), (wb, half)):
            out[at + side * group : at + (side + 1) * group, col : col + half] = (
                0.5 * dot(rows[...], weight[part, :])
            ).astype(BF16)


def edge_kernel(
    live_ref,
    pre_ref,
    pre2_ref,
    latent_ref,
    send_ref,
    recv_ref,
    mine_table,
    theirs_ref,
    wa_ref,
    wb_ref,
    va_ref,
    vb_ref,
    gain_ref,
    out_mine_ref,
    out_other_ref,
    fresh_all,
    group_other_ref,
    live_recv_ref,
    table,
    layout,
    block,
):
    share, width = latent_ref.shape
    half = wa_ref.shape[1]
    group = layout.group
    feat = lax.axis_index("feat")
    table[: 2 * group, :] = mine_table[...]
    project(theirs_ref, wa_ref, wb_ref, table, 2 * group)
    live_recv_ref[...] = live_ref[...]
    gain = gain_ref[...].astype(F32).reshape(1, width)
    for at in range(0, share, block):
        part = slice(at, at + block)
        some = slice(at // 128, (at + block) // 128)
        receivers = live_recv_ref[some, :]
        columns = [index_columns(send_ref[some, :]), index_columns(receivers)]
        first = pre_ref.shape[0]
        pre = pre_ref[part, :] if at < first else pre2_ref[at - first : at - first + block, :]
        picks = jnp.concatenate(
            [
                one_hot_rows(column, base, group)
                for base in (layout.local_slots, layout.local_slots + group)
                for column in columns
            ],
            axis=1,
        )
        hidden = silu_of_double(pre + dot(picks, table[...])).astype(BF16)
        pre = dot(hidden[:, :half], va_ref[...]) + dot(hidden[:, half:], vb_ref[...])
        live = jnp.concatenate(columns[1], axis=0) != DEAD
        fresh = (latent_ref[part, :].astype(F32) + layer_norm(pre, gain, live)).astype(BF16)
        low, high = fresh[:, : width // 2], fresh[:, width // 2 :]
        out_mine_ref[part, :] = jnp.where(feat == 0, low, high)
        out_other_ref[part, :] = jnp.where(feat == 0, high, low)
        fresh_all[part, :] = fresh
    receivers = flat_row(live_recv_ref[...])
    group_other_ref[...] = dot(one_hot_columns(receivers, layout.local_slots + group, group), fresh_all[...]).astype(BF16)


def group_sums_kernel(fresh_ref, recv_ref, sums_ref, first):
    sums_ref[...] = dot(one_hot_columns(flat_row(recv_ref[...]), first, sums_ref.shape[0]), fresh_ref[...])


def merge_kernel(mine_ref, theirs_ref, *out_refs):
    at = 0
    for out_ref in out_refs:
        rows = out_ref.shape[0]
        part = slice(at, at + rows)
        out_ref[...] = (mine_ref[part, :] + theirs_ref[part, :].astype(F32)).astype(BF16)
        at += rows


def core_rows_of(edges, core):
    share = edges.shape[0] // 2
    return edges.at[pl.ds(pl.multiple_of(core * share, share), share), :]


def local_sums_kernel(fresh_ref, recv_ref, node_ref, wa_ref, wb_ref, mine_ref, sums_ref, pre_ref, edges_ref, sems):
    placed = copies([(mine_ref, core_rows_of(edges_ref, lax.axis_index("feat")))], sems)
    width = node_ref.shape[1]
    half = wa_ref.shape[1]
    sums_ref[...] = dot(one_hot_columns(flat_row(recv_ref[...]), 0, sums_ref.shape[0]), fresh_ref[...])
    for weight, col in ((wa_ref, 0), (wb_ref, half)):
        pre_ref[:, col : col + half] = 0.5 * dot(node_ref[...], weight[:width, :])
    for copy in placed:
        copy.wait()


def beside_kernel(theirs_ref, edges_in_ref, edges_ref, sems):
    for copy in copies([(theirs_ref, core_rows_of(edges_ref, 1 - lax.axis_index("feat")))], sems):
        copy.wait()


def receive_kernel(sums_ref, halo_ref, coarse_ref, *refs):
    *parts, own_ref, rounded_ref = refs
    coarse = coarse_ref.shape[0]
    coarse_row = coarse_ref[...].reshape(1, coarse)
    index_row = jnp.concatenate([lent_list(halo_ref[...])] + [coarse_row] * len(parts), axis=1)
    returned = jnp.concatenate([part[...] for part in parts], axis=0)
    own = sums_ref[...] + dot(one_hot_columns(index_row, 0, own_ref.shape[0]), returned)
    own_ref[...] = own
    rounded_ref[...] = own.astype(BF16)


def node_kernel(node_ref, own_ref, partner_ref, pre_ref, wa_ref, wb_ref, va_ref, vb_ref, gain_ref, out_ref):
    width = node_ref.shape[1]
    half = wa_ref.shape[1]
    feat = lax.axis_index("feat")
    received = (own_ref[...] + partner_ref[...].astype(F32)).astype(BF16)
    total = None
    for weight, second, col in ((wa_ref, va_ref, 0), (wb_ref, vb_ref, half)):
        pre = pre_ref[:, col : col + half] + 0.5 * dot(received, weight[width:, :])
        part = dot(silu_of_double(pre).astype(BF16), second[...])
        total = part if total is None else total + part
    update = layer_norm(total, gain_ref[...].astype(F32).reshape(1, width))
    fresh = (node_ref[...].astype(F32) + update).astype(BF16)
    out_ref[...] = jnp.where(feat == 0, fresh[:, : width // 2], fresh[:, width // 2 :])


def in_hbm(array):
    return pltpu.with_memory_space_constraint(array, pltpu.HBM)


VMEM_SPEC = pl.BlockSpec(memory_space=pltpu.VMEM)
ANY_SPEC = pl.BlockSpec(memory_space=pl.ANY)


def call(kernel, operands, in_specs, outputs, out_specs, flops, limit, scratch=(), aliases=None):
    return pl.pallas_call(
        kernel,
        in_specs=in_specs,
        out_specs=out_specs,
        out_shape=outputs,
        scratch_shapes=list(scratch),
        input_output_aliases=aliases or {},
        cost_estimate=pl.CostEstimate(flops=flops, bytes_accessed=MIB // 4, transcendentals=0),
        compiler_params=pltpu.CompilerParams(vmem_limit_bytes=limit * MIB),
    )(*operands)


def pairing(count, pairs):
    targets = [None] * count
    for p, q in pairs:
        targets[p], targets[q] = q, p
    return targets


def exchange_rounds(count):
    across = [(p + 1 if p % 2 else p - 1) % count for p in range(count)]
    apart = lambda distance: [p ^ distance for p in range(count)]
    rounds = [(apart(1), across)]
    if count == 8:
        mixed = pairing(count, [(0, 3), (4, 7), (1, 6), (2, 5)])
        return rounds + [(apart(4), apart(5)), (apart(2), apart(2)), (apart(6), mixed)]
    return rounds + [(apart(distance), apart(distance + 1)) for distance in range(2, count, 2)]


def exchange_pairs(rounds):
    count = len(rounds[0][0])
    return [
        [(2 * p + feat, 2 * targets[p] + feat) for p in range(count) for feat, targets in enumerate(some)]
        for some in rounds
    ]


def on_device(
    node_latent,
    edge_latent,
    edge_senders,
    edge_receivers,
    halo_rows,
    coarse_rows,
    edge_counts,
    edge_w1,
    edge_w2,
    edge_gain,
    node_w1,
    node_w2,
    node_gain,
):
    node_count, width = node_latent.shape
    half = width // 2
    edge_count = edge_latent.shape[0]
    halo, coarse = halo_rows.shape[1], coarse_rows.shape[0]
    patches = lax.axis_size("patch")
    both = ("patch", "feat")
    rounds = exchange_rounds(patches)
    layout = Layout(rounds, node_count, halo, coarse)
    group, local_slots = layout.group, layout.local_slots
    share = edge_count // 2
    block = 512
    dma = pltpu.SemaphoreType.DMA

    def shape(rows, columns, kind=BF16):
        return jax.ShapeDtypeStruct((rows, columns), kind)

    def like(array):
        return jax.ShapeDtypeStruct(array.shape, array.dtype)

    def swap(values):
        return lax.ppermute(values, "feat", FEAT_SWAP)

    edge_w1_b = swap(edge_w1)

    index_rows = (edge_count // 128, 128)
    core_rows = jax.ShapeDtypeStruct((share // 128, 128), jnp.int32)
    lent, node, halo_lists, coarse_list, w1, send, recv, early_latent = call(
        functools.partial(lend_kernel, share=share, layout=layout),
        [
            in_hbm(array)
            for array in (
                node_latent,
                halo_rows,
                coarse_rows,
                edge_w1,
                edge_senders.reshape(index_rows),
                edge_receivers.reshape(index_rows),
                edge_latent,
            )
        ],
        [ANY_SPEC] * 7,
        [shape(halo + coarse, width)]
        + [like(array) for array in (node_latent, halo_rows, coarse_rows, edge_w1)]
        + [core_rows] * 2
        + [shape(block, width)],
        [VMEM_SPEC] * 8,
        2 * node_count * (halo + coarse) * width,
        8,
        scratch=[pltpu.SMEM((coarse,), jnp.int32), dma((8,))],
    )
    pairs = exchange_pairs(rounds)
    arrived = [
        lax.ppermute(lent[halo:] if i else lent, both, pairs[i]) for i in reversed(range(len(pairs)))
    ][::-1]

    more = (edge_w2, edge_gain, node_w1, node_w2, node_gain)
    first = share // 2
    pre, latent, table, live, w2, e_gain, n_w1, n_w2, n_gain = call(
        functools.partial(local_kernel, layout=layout, block=block),
        [edge_counts.reshape(1, 1), node, w1, edge_w1_b, send, recv, early_latent] + [in_hbm(array) for array in (edge_latent, *more)],
        [VMEM_SPEC] * 7 + [ANY_SPEC] * (1 + len(more)),
        [
            shape(first, width, F32),
            shape(share, width),
            shape(2 * local_slots, width),
            core_rows,
        ]
        + [like(array) for array in more],
        [VMEM_SPEC] * (4 + len(more)),
        (2 * width * width * first + 4 * node_count * width * width + 4 * first * local_slots * width) // BESIDE,
        LIMIT,
        scratch=[dma((len(more) + (share - first) // block,)), dma((first // block,))],
    )
    pre, *arrived = lax.optimization_barrier((pre, *arrived))
    table_mine = jnp.concatenate(arrived, axis=0)
    table_theirs = swap(table_mine)
    edge_w2_b = swap(w2)
    pre2, projected = call(
        functools.partial(second_kernel, block=block),
        [latent, send, recv, w1, edge_w1_b, table, table_mine],
        [VMEM_SPEC] * 7,
        [shape(share - first, width, F32), shape(2 * group, width)],
        [VMEM_SPEC] * 2,
        2 * width * width * (share - first) + 4 * (share - first) * local_slots * width + 4 * group * width * width,
        LIMIT,
    )
    node_w1_b, node_w2_b = swap(n_w1), swap(n_w2)

    mine, other, fresh, group_other, live_recv = call(
        functools.partial(edge_kernel, layout=layout, block=block),
        (live, pre, pre2, latent, send, recv, projected, table_theirs, w1, edge_w1_b, w2, edge_w2_b, e_gain),
        [VMEM_SPEC] * 13,
        [shape(share, half), shape(share, half), shape(share, width), shape(group, width), core_rows],
        [VMEM_SPEC] * 5,
        2 * share * width * (width + 6 * group) + 4 * group * width * width,
        LIMIT,
        scratch=[pltpu.VMEM((4 * group, width), BF16)],
    )
    node_w1_b, node_w2_b, mine, other, fresh, group_other = lax.optimization_barrier(
        (node_w1_b, node_w2_b, mine, other, fresh, group_other)
    )

    group_theirs = swap(group_other)
    group_mine = call(
        functools.partial(group_sums_kernel, first=local_slots),
        (fresh, live_recv),
        [VMEM_SPEC] * 2,
        shape(group, width, F32),
        VMEM_SPEC,
        2 * share * width * group,
        16,
    )
    group_mine, other = lax.optimization_barrier((group_mine, other))
    edges_theirs = swap(other)
    sizes = [halo + coarse] + [coarse] * (len(pairs) - 1)
    outgoing = call(
        merge_kernel,
        (group_mine, group_theirs),
        [VMEM_SPEC] * 2,
        [shape(rows, width) for rows in sizes],
        [VMEM_SPEC] * len(sizes),
        group * width,
        8,
    )
    *outgoing, fresh = lax.optimization_barrier((*outgoing, fresh))
    back = [lax.ppermute(outgoing[i], both, pairs[i]) for i in reversed(range(len(pairs)))][::-1]
    local_sums, node_pre, edges = call(
        local_sums_kernel,
        (fresh, live_recv, node, n_w1, node_w1_b, mine),
        [VMEM_SPEC] * 5 + [ANY_SPEC],
        [shape(node_count, width, F32), shape(node_count, width, F32), shape(edge_count, half)],
        [VMEM_SPEC] * 2 + [ANY_SPEC],
        2 * share * width * node_count // BESIDE,
        16,
        scratch=[dma((1,))],
    )
    local_sums, *back = lax.optimization_barrier((local_sums, *back[::-1]))
    back = back[::-1]
    own, rounded = call(
        receive_kernel,
        (local_sums, halo_lists, coarse_list, *back),
        [VMEM_SPEC] * (3 + len(sizes)),
        [shape(node_count, width, F32), shape(node_count, width)],
        [VMEM_SPEC] * 2,
        2 * node_count * width * group,
        16,
    )
    partner = swap(rounded)
    edges_theirs = lax.optimization_barrier((edges_theirs, rounded))[0]
    edges_out = call(
        beside_kernel,
        (edges_theirs, edges),
        [ANY_SPEC] * 2,
        shape(edge_count, half),
        ANY_SPEC,
        2 * node_count * width * width,
        8,
        scratch=[dma((1,))],
        aliases={1: 0},
    )
    nodes_out = call(
        node_kernel,
        (node, own, partner, node_pre, n_w1, node_w1_b, n_w2, node_w2_b, n_gain),
        [VMEM_SPEC] * 9,
        shape(node_count, half),
        VMEM_SPEC,
        4 * node_count * width * width,
        16,
    )
    return nodes_out, edges_out


def solution(mesh):
    placed = (
        P(("member", "patch"), None),
        P(("member", "patch"), None),
        P(("member", "patch")),
        P(("member", "patch")),
        P(("member", "patch"), None),
        P(("member", "patch")),
        P(("member", "patch")),
        P(None, "feat"),
        P("feat", None),
        P(),
        P(None, "feat"),
        P("feat", None),
        P(),
    )
    return jax.shard_map(
        on_device,
        mesh=mesh,
        in_specs=placed,
        out_specs=(P(("member", "patch"), "feat"), P(("member", "patch"), "feat")),
        check_vma=False,
    )
```

```python
import functools

import jax
import jax.numpy as jnp
from jax import lax
from jax.experimental import pallas as pl
from jax.experimental.pallas import tpu as pltpu
from jax.sharding import PartitionSpec as P

EPSILON = 1e-05
F32 = jnp.float32
BF16 = jnp.bfloat16
MIB = 1024 * 1024
LIMIT = 30
BESIDE = 10
DEAD = -1
NOWHERE = -2
FEAT_SWAP = [(0, 1), (1, 0)]


def silu_of_double(half_v):
    return half_v + half_v * jnp.tanh(half_v)


def dot(a, b):
    return jnp.dot(a, b, preferred_element_type=F32)


def lane_sums(x):
    high = x.astype(BF16)
    low = (x - high.astype(F32)).astype(BF16)
    ones = jnp.ones((128, 128), BF16)
    return dot(high, ones) + dot(low, ones)


def layer_norm(pre, gain, keep=None):
    width = pre.shape[1]
    parts = [pre[:, at : at + 128] for at in range(0, width, 128)]
    center = jnp.sum(sum(parts), axis=1, keepdims=True) * (1.0 / width)
    square = jnp.sum(sum(part * part for part in parts), axis=1, keepdims=True) * (1.0 / width)
    scale = lax.rsqrt(square - center * center + EPSILON)
    if keep is not None:
        scale = jnp.where(keep, scale, 0.0)
    shift = -center * scale
    return jnp.concatenate(
        [(part * scale + shift) * gain[:, at * 128 : at * 128 + 128] for at, part in enumerate(parts)], axis=1
    )


def index_columns(index):
    return [
        jnp.transpose(jnp.broadcast_to(index[j : j + 1, :], (128, 128))) for j in range(index.shape[0])
    ]


def one_hot_rows(columns, first, count):
    lanes = lax.broadcasted_iota(jnp.int32, (128, 128), 1) + first
    return jnp.concatenate(
        [
            jnp.concatenate(
                [(column == lanes + at).astype(F32).astype(BF16) for at in range(0, count, 128)], axis=1
            )
            for column in columns
        ],
        axis=0,
    )


def one_hot_columns(index_row, first, count):
    entries = index_row.shape[1]
    rows = lax.broadcasted_iota(jnp.int32, (count, entries), 0) + first
    return (rows == jnp.broadcast_to(index_row, (count, entries))).astype(F32).astype(BF16)


def flat_row(index):
    return jnp.concatenate([index[j : j + 1, :] for j in range(index.shape[0])], axis=1)


def copies(pairs, sems):
    made = [pltpu.make_async_copy(source, target, sems.at[i]) for i, (source, target) in enumerate(pairs)]
    for copy in made:
        copy.start()
    return made


class Layout:
    def __init__(self, rounds, node_count, halo, coarse):
        self.patches = len(rounds[0][0])
        self.node_count, self.halo, self.coarse = node_count, halo, coarse
        self.group = halo + coarse * len(rounds)
        self.local_slots = -(-node_count // 128) * 128
        self.code = [[0] * self.patches for _ in range(self.patches)]
        for i, some in reversed(list(enumerate(rounds))):
            for core, targets in enumerate(some):
                for patch, owner in enumerate(targets):
                    self.code[patch][owner] = (core << 16) + halo + coarse * i

    def slots(self, rows, patch, feat, own):
        node_count, halo, coarse, group = self.node_count, self.halo, self.coarse, self.group
        at = rows - (node_count + 2 * halo)
        owner, entry = lax.shift_right_arithmetic(at, coarse.bit_length() - 1), at & (coarse - 1)
        place = jnp.zeros_like(rows)
        for q in range(self.patches):
            code = jnp.int32(0)
            for p in range(self.patches):
                code = jnp.where(patch == p, self.code[p][q], code)
            remote = self.local_slots + (lax.shift_right_arithmetic(code, 16) ^ feat) * group + (code & 0xFFFF)
            place = jnp.where(owner == q, remote, place)
        place = place + entry
        for i in range(coarse):
            place = jnp.where((owner == patch) & (entry == i), own[i], place)
        even = 1 - (patch & 1)
        lower = self.local_slots + (even ^ feat) * group - node_count + rows
        upper = self.local_slots + (1 - (even ^ feat)) * group - (node_count + halo) + rows
        lower = jnp.where(patch == 0, NOWHERE, lower)
        upper = jnp.where(patch == self.patches - 1, NOWHERE, upper)
        place = jnp.where(rows < node_count + 2 * halo, upper, place)
        place = jnp.where(rows < node_count + halo, lower, place)
        return jnp.where(rows < node_count, rows, place)


def lent_list(lists):
    which = (lax.axis_index("feat") + lax.axis_index("patch")) & 1
    return jnp.where(which == 0, lists[0:1], lists[1:2])


def lend_kernel(*refs, share, layout):
    (node_hbm, halo_hbm, coarse_hbm, wa_hbm, send_hbm, recv_hbm, latent_hbm), refs = refs[:7], refs[7:]
    lent_ref, node, halo, coarse, wa, send, recv, latent, own, sems = refs
    rows128 = share // 128
    feat, patch = lax.axis_index("feat"), lax.axis_index("patch")
    mine = pl.ds(pl.multiple_of(feat * rows128, rows128), rows128)
    loads = copies(
        (
            (halo_hbm, halo),
            (coarse_hbm, coarse),
            (node_hbm, node),
            (send_hbm.at[mine, :], send),
            (recv_hbm.at[mine, :], recv),
            (coarse_hbm, own),
            (wa_hbm, wa),
            (latent_hbm.at[pl.ds(pl.multiple_of(feat * share, share), latent.shape[0]), :], latent),
        ),
        sems,
    )
    for copy in loads[:3]:
        copy.wait()
    index_row = jnp.concatenate([lent_list(halo[...]), coarse[...].reshape(1, -1)], axis=1)
    lent_ref[...] = lax.dot_general(
        one_hot_columns(index_row, 0, node.shape[0]),
        node[...],
        (((0,), (0,)), ((), ())),
        preferred_element_type=F32,
    ).astype(BF16)
    for copy in loads[3:6]:
        copy.wait()
    for index in (send, recv):
        index[...] = layout.slots(index[...], patch, feat, own)
    for copy in loads[6:]:
        copy.wait()


def local_part(at, block, latent, send, recv, wa, wb, table, before=None):
    part, some = slice(at, at + block), slice(at // 128, (at + block) // 128)
    half = wa.shape[1]
    width = latent.shape[1]
    slots = table.shape[0] // 2
    picks = jnp.concatenate(
        [one_hot_rows(index_columns(index[some, :]), 0, slots) for index in (send, recv)], axis=1
    )
    picked = [dot(picks, table[:, col : col + half]) for col in (0, half)]
    if before is not None:
        before.wait()
    rows = latent[part, :]
    return jnp.concatenate(
        [0.5 * (some + dot(rows, weight[:width, :])) for some, weight in zip(picked, (wa, wb))], axis=1
    )


def local_kernel(limit_ref, node, wa, wb, send, recv, early_latent, latent_hbm, *refs, layout, block):
    count = (len(refs) - 6) // 2
    more_hbm, refs = refs[:count], refs[count:]
    pre_ref, latent, table, live_ref, *more = refs[: 4 + count]
    sems, block_sems = refs[4 + count :]
    share, width = latent.shape
    half = wa.shape[1]
    feat = lax.axis_index("feat")
    local_slots, used = layout.local_slots, layout.node_count
    first = pre_ref.shape[0]
    blocks = [
        (latent_hbm.at[pl.ds(pl.multiple_of(feat * share + at, block), block), :], latent.at[pl.ds(at, block), :])
        for at in range(block, share, block)
    ]
    wanted = first // block - 1
    early = copies(blocks[:wanted], block_sems)
    latent[:block, :] = early_latent[...]
    for side in range(2):
        base = side * local_slots
        rows = slice((side + 1) * width, (side + 2) * width)
        for weight, col in ((wa, 0), (wb, half)):
            table[base : base + used, col : col + half] = dot(node[...], weight[rows, :]).astype(BF16)
        if used < local_slots:
            table[base + used : base + local_slots, :] = jnp.zeros((local_slots - used, 2 * half), BF16)
    shape = recv.shape
    edge = lax.broadcasted_iota(jnp.int32, shape, 0) * 128 + lax.broadcasted_iota(jnp.int32, shape, 1) + feat * share
    live_ref[...] = jnp.where(edge < limit_ref[...], recv[...], DEAD)
    rest = copies(blocks[wanted:] + list(zip(more_hbm, more)), sems)
    for i, copy in enumerate([None] + early):
        at = i * block
        pre_ref[at : at + block, :] = local_part(at, block, latent, send, recv, wa, wb, table, copy)
    for copy in rest:
        copy.wait()


def second_kernel(latent, send, recv, wa, wb, table, mine, pre_ref, projected, block):
    share, width = latent.shape
    half = wa.shape[1]
    done = share - pre_ref.shape[0]
    group = mine.shape[0]
    for at in range(done, share, block):
        pre_ref[at - done : at - done + block, :] = local_part(at, block, latent, send, recv, wa, wb, table)
    project(mine, wa, wb, projected)


def project(rows, wa, wb, out, at=0):
    group, width = rows.shape
    half = wa.shape[1]
    for side in range(2):
        part = slice((side + 1) * width, (side + 2) * width)
        for weight, col in ((wa, 0), (wb, half)):
            out[at + side * group : at + (side + 1) * group, col : col + half] = (
                0.5 * dot(rows[...], weight[part, :])
            ).astype(BF16)


def edge_kernel(
    live_ref,
    pre_ref,
    pre2_ref,
    latent_ref,
    send_ref,
    recv_ref,
    mine_table,
    theirs_ref,
    wa_ref,
    wb_ref,
    va_ref,
    vb_ref,
    gain_ref,
    out_other_ref,
    fresh_all,
    group_other_ref,
    live_recv_ref,
    table,
    layout,
    block,
):
    share, width = latent_ref.shape
    half = wa_ref.shape[1]
    group = layout.group
    feat = lax.axis_index("feat")
    table[: 2 * group, :] = mine_table[...]
    project(theirs_ref, wa_ref, wb_ref, table, 2 * group)
    live_recv_ref[...] = live_ref[...]
    gain = gain_ref[...].astype(F32).reshape(1, width)
    for at in range(0, share, block):
        part = slice(at, at + block)
        some = slice(at // 128, (at + block) // 128)
        receivers = live_recv_ref[some, :]
        columns = [index_columns(send_ref[some, :]), index_columns(receivers)]
        first = pre_ref.shape[0]
        pre = pre_ref[part, :] if at < first else pre2_ref[at - first : at - first + block, :]
        picks = jnp.concatenate(
            [
                one_hot_rows(column, base, group)
                for base in (layout.local_slots, layout.local_slots + group)
                for column in columns
            ],
            axis=1,
        )
        hidden = silu_of_double(pre + dot(picks, table[...])).astype(BF16)
        pre = dot(hidden[:, :half], va_ref[...]) + dot(hidden[:, half:], vb_ref[...])
        live = jnp.concatenate(columns[1], axis=0) != DEAD
        fresh = (latent_ref[part, :].astype(F32) + layer_norm(pre, gain, live)).astype(BF16)
        low, high = fresh[:, : width // 2], fresh[:, width // 2 :]
        out_other_ref[part, :] = jnp.where(feat == 0, high, low)
        fresh_all[part, :] = fresh
    receivers = flat_row(live_recv_ref[...])
    group_other_ref[...] = dot(one_hot_columns(receivers, layout.local_slots + group, group), fresh_all[...]).astype(BF16)


def group_sums_kernel(fresh_ref, recv_ref, sums_ref, first):
    sums_ref[...] = dot(one_hot_columns(flat_row(recv_ref[...]), first, sums_ref.shape[0]), fresh_ref[...])


def merge_kernel(mine_ref, theirs_ref, *out_refs):
    at = 0
    for out_ref in out_refs:
        rows = out_ref.shape[0]
        part = slice(at, at + rows)
        out_ref[...] = (mine_ref[part, :] + theirs_ref[part, :].astype(F32)).astype(BF16)
        at += rows


def core_rows_of(edges, core):
    share = edges.shape[0] // 2
    return edges.at[pl.ds(pl.multiple_of(core * share, share), share), :]


def local_sums_kernel(fresh_ref, recv_ref, node_ref, wa_ref, wb_ref, sums_ref, pre_ref, edges_ref, sems):
    width = node_ref.shape[1]
    half = wa_ref.shape[1]
    feat = lax.axis_index("feat")
    columns = pl.ds(pl.multiple_of(feat * half, half), half)
    placed = copies([(fresh_ref.at[:, columns], core_rows_of(edges_ref, feat))], sems)
    sums_ref[...] = dot(one_hot_columns(flat_row(recv_ref[...]), 0, sums_ref.shape[0]), fresh_ref[...])
    for weight, col in ((wa_ref, 0), (wb_ref, half)):
        pre_ref[:, col : col + half] = 0.5 * dot(node_ref[...], weight[:width, :])
    for copy in placed:
        copy.wait()


def beside_kernel(theirs_ref, edges_in_ref, edges_ref, sems):
    for copy in copies([(theirs_ref, core_rows_of(edges_ref, 1 - lax.axis_index("feat")))], sems):
        copy.wait()


def receive_kernel(sums_ref, halo_ref, coarse_ref, *refs):
    *parts, own_ref, rounded_ref = refs
    coarse = coarse_ref.shape[0]
    coarse_row = coarse_ref[...].reshape(1, coarse)
    index_row = jnp.concatenate([lent_list(halo_ref[...])] + [coarse_row] * len(parts), axis=1)
    returned = jnp.concatenate([part[...] for part in parts], axis=0)
    own = sums_ref[...] + dot(one_hot_columns(index_row, 0, own_ref.shape[0]), returned)
    own_ref[...] = own
    rounded_ref[...] = own.astype(BF16)


def node_kernel(node_ref, own_ref, partner_ref, pre_ref, wa_ref, wb_ref, va_ref, vb_ref, gain_ref, out_ref):
    width = node_ref.shape[1]
    half = wa_ref.shape[1]
    feat = lax.axis_index("feat")
    received = (own_ref[...] + partner_ref[...].astype(F32)).astype(BF16)
    total = None
    for weight, second, col in ((wa_ref, va_ref, 0), (wb_ref, vb_ref, half)):
        pre = pre_ref[:, col : col + half] + 0.5 * dot(received, weight[width:, :])
        part = dot(silu_of_double(pre).astype(BF16), second[...])
        total = part if total is None else total + part
    update = layer_norm(total, gain_ref[...].astype(F32).reshape(1, width))
    fresh = (node_ref[...].astype(F32) + update).astype(BF16)
    out_ref[...] = jnp.where(feat == 0, fresh[:, : width // 2], fresh[:, width // 2 :])


def in_hbm(array):
    return pltpu.with_memory_space_constraint(array, pltpu.HBM)


VMEM_SPEC = pl.BlockSpec(memory_space=pltpu.VMEM)
ANY_SPEC = pl.BlockSpec(memory_space=pl.ANY)


def call(kernel, operands, in_specs, outputs, out_specs, flops, limit, scratch=(), aliases=None):
    return pl.pallas_call(
        kernel,
        in_specs=in_specs,
        out_specs=out_specs,
        out_shape=outputs,
        scratch_shapes=list(scratch),
        input_output_aliases=aliases or {},
        cost_estimate=pl.CostEstimate(flops=flops, bytes_accessed=MIB // 4, transcendentals=0),
        compiler_params=pltpu.CompilerParams(vmem_limit_bytes=limit * MIB),
    )(*operands)


def pairing(count, pairs):
    targets = [None] * count
    for p, q in pairs:
        targets[p], targets[q] = q, p
    return targets


def exchange_rounds(count):
    across = [(p + 1 if p % 2 else p - 1) % count for p in range(count)]
    apart = lambda distance: [p ^ distance for p in range(count)]
    rounds = [(apart(1), across)]
    if count == 8:
        mixed = pairing(count, [(0, 3), (4, 7), (1, 6), (2, 5)])
        return rounds + [(apart(4), apart(5)), (apart(2), apart(2)), (apart(6), mixed)]
    return rounds + [(apart(distance), apart(distance + 1)) for distance in range(2, count, 2)]


def exchange_pairs(rounds):
    count = len(rounds[0][0])
    return [
        [(2 * p + feat, 2 * targets[p] + feat) for p in range(count) for feat, targets in enumerate(some)]
        for some in rounds
    ]


def on_device(
    node_latent,
    edge_latent,
    edge_senders,
    edge_receivers,
    halo_rows,
    coarse_rows,
    edge_counts,
    edge_w1,
    edge_w2,
    edge_gain,
    node_w1,
    node_w2,
    node_gain,
):
    node_count, width = node_latent.shape
    half = width // 2
    edge_count = edge_latent.shape[0]
    halo, coarse = halo_rows.shape[1], coarse_rows.shape[0]
    patches = lax.axis_size("patch")
    both = ("patch", "feat")
    rounds = exchange_rounds(patches)
    layout = Layout(rounds, node_count, halo, coarse)
    group, local_slots = layout.group, layout.local_slots
    share = edge_count // 2
    block = 512
    dma = pltpu.SemaphoreType.DMA

    def shape(rows, columns, kind=BF16):
        return jax.ShapeDtypeStruct((rows, columns), kind)

    def like(array):
        return jax.ShapeDtypeStruct(array.shape, array.dtype)

    def swap(values):
        return lax.ppermute(values, "feat", FEAT_SWAP)

    edge_w1_b = swap(edge_w1)

    index_rows = (edge_count // 128, 128)
    core_rows = jax.ShapeDtypeStruct((share // 128, 128), jnp.int32)
    lent, node, halo_lists, coarse_list, w1, send, recv, early_latent = call(
        functools.partial(lend_kernel, share=share, layout=layout),
        [
            in_hbm(array)
            for array in (
                node_latent,
                halo_rows,
                coarse_rows,
                edge_w1,
                edge_senders.reshape(index_rows),
                edge_receivers.reshape(index_rows),
                edge_latent,
            )
        ],
        [ANY_SPEC] * 7,
        [shape(halo + coarse, width)]
        + [like(array) for array in (node_latent, halo_rows, coarse_rows, edge_w1)]
        + [core_rows] * 2
        + [shape(block, width)],
        [VMEM_SPEC] * 8,
        2 * node_count * (halo + coarse) * width,
        8,
        scratch=[pltpu.SMEM((coarse,), jnp.int32), dma((8,))],
    )
    pairs = exchange_pairs(rounds)
    arrived = [
        lax.ppermute(lent[halo:] if i else lent, both, pairs[i]) for i in reversed(range(len(pairs)))
    ][::-1]

    more = (edge_w2, edge_gain, node_w1, node_w2, node_gain)
    first = share // 2
    pre, latent, table, live, w2, e_gain, n_w1, n_w2, n_gain = call(
        functools.partial(local_kernel, layout=layout, block=block),
        [edge_counts.reshape(1, 1), node, w1, edge_w1_b, send, recv, early_latent] + [in_hbm(array) for array in (edge_latent, *more)],
        [VMEM_SPEC] * 7 + [ANY_SPEC] * (1 + len(more)),
        [
            shape(first, width, F32),
            shape(share, width),
            shape(2 * local_slots, width),
            core_rows,
        ]
        + [like(array) for array in more],
        [VMEM_SPEC] * (4 + len(more)),
        (2 * width * width * first + 4 * node_count * width * width + 4 * first * local_slots * width) // BESIDE,
        LIMIT,
        scratch=[dma((len(more) + (share - first) // block,)), dma((first // block,))],
    )
    pre, *arrived = lax.optimization_barrier((pre, *arrived))
    table_mine = jnp.concatenate(arrived, axis=0)
    table_theirs = swap(table_mine)
    edge_w2_b = swap(w2)
    pre2, projected = call(
        functools.partial(second_kernel, block=block),
        [latent, send, recv, w1, edge_w1_b, table, table_mine],
        [VMEM_SPEC] * 7,
        [shape(share - first, width, F32), shape(2 * group, width)],
        [VMEM_SPEC] * 2,
        2 * width * width * (share - first) + 4 * (share - first) * local_slots * width + 4 * group * width * width,
        LIMIT,
    )
    node_w1_b, node_w2_b = swap(n_w1), swap(n_w2)

    other, fresh, group_other, live_recv = call(
        functools.partial(edge_kernel, layout=layout, block=block),
        (live, pre, pre2, latent, send, recv, projected, table_theirs, w1, edge_w1_b, w2, edge_w2_b, e_gain),
        [VMEM_SPEC] * 13,
        [shape(share, half), shape(share, width), shape(group, width), core_rows],
        [VMEM_SPEC] * 4,
        2 * share * width * (width + 6 * group) + 4 * group * width * width,
        LIMIT,
        scratch=[pltpu.VMEM((4 * group, width), BF16)],
    )
    node_w1_b, node_w2_b, other, fresh, group_other = lax.optimization_barrier(
        (node_w1_b, node_w2_b, other, fresh, group_other)
    )

    group_theirs = swap(group_other)
    group_mine = call(
        functools.partial(group_sums_kernel, first=local_slots),
        (fresh, live_recv),
        [VMEM_SPEC] * 2,
        shape(group, width, F32),
        VMEM_SPEC,
        2 * share * width * group,
        16,
    )
    group_mine, other = lax.optimization_barrier((group_mine, other))
    edges_theirs = swap(other)
    sizes = [halo + coarse] + [coarse] * (len(pairs) - 1)
    outgoing = call(
        merge_kernel,
        (group_mine, group_theirs),
        [VMEM_SPEC] * 2,
        [shape(rows, width) for rows in sizes],
        [VMEM_SPEC] * len(sizes),
        group * width,
        8,
    )
    *outgoing, fresh = lax.optimization_barrier((*outgoing, fresh))
    back = [lax.ppermute(outgoing[i], both, pairs[i]) for i in reversed(range(len(pairs)))][::-1]
    local_sums, node_pre, edges = call(
        local_sums_kernel,
        (fresh, live_recv, node, n_w1, node_w1_b),
        [VMEM_SPEC] * 5,
        [shape(node_count, width, F32), shape(node_count, width, F32), shape(edge_count, half)],
        [VMEM_SPEC] * 2 + [ANY_SPEC],
        2 * share * width * node_count // BESIDE,
        16,
        scratch=[dma((1,))],
    )
    local_sums, *back = lax.optimization_barrier((local_sums, *back[::-1]))
    back = back[::-1]
    own, rounded = call(
        receive_kernel,
        (local_sums, halo_lists, coarse_list, *back),
        [VMEM_SPEC] * (3 + len(sizes)),
        [shape(node_count, width, F32), shape(node_count, width)],
        [VMEM_SPEC] * 2,
        2 * node_count * width * group,
        16,
    )
    partner = swap(rounded)
    edges_theirs = lax.optimization_barrier((edges_theirs, rounded))[0]
    edges_out = call(
        beside_kernel,
        (edges_theirs, edges),
        [ANY_SPEC] * 2,
        shape(edge_count, half),
        ANY_SPEC,
        2 * node_count * width * width,
        8,
        scratch=[dma((1,))],
        aliases={1: 0},
    )
    nodes_out = call(
        node_kernel,
        (node, own, partner, node_pre, n_w1, node_w1_b, n_w2, node_w2_b, n_gain),
        [VMEM_SPEC] * 9,
        shape(node_count, half),
        VMEM_SPEC,
        4 * node_count * width * width,
        16,
    )
    return nodes_out, edges_out


def solution(mesh):
    placed = (
        P(("member", "patch"), None),
        P(("member", "patch"), None),
        P(("member", "patch")),
        P(("member", "patch")),
        P(("member", "patch"), None),
        P(("member", "patch")),
        P(("member", "patch")),
        P(None, "feat"),
        P("feat", None),
        P(),
        P(None, "feat"),
        P("feat", None),
        P(),
    )
    return jax.shard_map(
        on_device,
        mesh=mesh,
        in_specs=placed,
        out_specs=(P(("member", "patch"), "feat"), P(("member", "patch"), "feat")),
        check_vma=False,
    )
```

```python
import functools

import jax
import jax.numpy as jnp
from jax import lax
from jax.experimental import pallas as pl
from jax.experimental.pallas import tpu as pltpu
from jax.sharding import PartitionSpec as P

EPSILON = 1e-05
F32 = jnp.float32
BF16 = jnp.bfloat16
MIB = 1024 * 1024
LIMIT = 30
BESIDE = 10
DEAD = -1
NOWHERE = -2
FEAT_SWAP = [(0, 1), (1, 0)]


def silu_of_double(half_v):
    return half_v + half_v * jnp.tanh(half_v)


def dot(a, b):
    return jnp.dot(a, b, preferred_element_type=F32)


def lane_sums(x):
    high = x.astype(BF16)
    low = (x - high.astype(F32)).astype(BF16)
    ones = jnp.ones((128, 128), BF16)
    return dot(high, ones) + dot(low, ones)


def layer_norm(pre, gain, keep=None):
    width = pre.shape[1]
    parts = [pre[:, at : at + 128] for at in range(0, width, 128)]
    center = jnp.sum(sum(parts), axis=1, keepdims=True) * (1.0 / width)
    square = jnp.sum(sum(part * part for part in parts), axis=1, keepdims=True) * (1.0 / width)
    scale = lax.rsqrt(square - center * center + EPSILON)
    if keep is not None:
        scale = jnp.where(keep, scale, 0.0)
    shift = -center * scale
    return jnp.concatenate(
        [(part * scale + shift) * gain[:, at * 128 : at * 128 + 128] for at, part in enumerate(parts)], axis=1
    )


def index_columns(index):
    return [
        jnp.transpose(jnp.broadcast_to(index[j : j + 1, :], (128, 128))) for j in range(index.shape[0])
    ]


def one_hot_rows(columns, first, count):
    lanes = lax.broadcasted_iota(jnp.int32, (128, 128), 1) + first
    return jnp.concatenate(
        [
            jnp.concatenate(
                [(column == lanes + at).astype(F32).astype(BF16) for at in range(0, count, 128)], axis=1
            )
            for column in columns
        ],
        axis=0,
    )


def one_hot_columns(index_row, first, count):
    entries = index_row.shape[1]
    rows = lax.broadcasted_iota(jnp.int32, (count, entries), 0) + first
    return (rows == jnp.broadcast_to(index_row, (count, entries))).astype(F32).astype(BF16)


def flat_row(index):
    return jnp.concatenate([index[j : j + 1, :] for j in range(index.shape[0])], axis=1)


def copies(pairs, sems):
    made = [pltpu.make_async_copy(source, target, sems.at[i]) for i, (source, target) in enumerate(pairs)]
    for copy in made:
        copy.start()
    return made


class Layout:
    def __init__(self, rounds, node_count, halo, coarse):
        self.patches = len(rounds[0][0])
        self.node_count, self.halo, self.coarse = node_count, halo, coarse
        self.group = halo + coarse * len(rounds)
        self.local_slots = -(-node_count // 128) * 128
        self.code = [[0] * self.patches for _ in range(self.patches)]
        for i, some in reversed(list(enumerate(rounds))):
            for core, targets in enumerate(some):
                for patch, owner in enumerate(targets):
                    self.code[patch][owner] = (core << 16) + halo + coarse * i

    def slots(self, rows, patch, feat, own):
        node_count, halo, coarse, group = self.node_count, self.halo, self.coarse, self.group
        at = rows - (node_count + 2 * halo)
        owner, entry = lax.shift_right_arithmetic(at, coarse.bit_length() - 1), at & (coarse - 1)
        place = jnp.zeros_like(rows)
        for q in range(self.patches):
            code = jnp.int32(0)
            for p in range(self.patches):
                code = jnp.where(patch == p, self.code[p][q], code)
            remote = self.local_slots + (lax.shift_right_arithmetic(code, 16) ^ feat) * group + (code & 0xFFFF)
            place = jnp.where(owner == q, remote, place)
        place = place + entry
        for i in range(coarse):
            place = jnp.where((owner == patch) & (entry == i), own[i], place)
        even = 1 - (patch & 1)
        lower = self.local_slots + (even ^ feat) * group - node_count + rows
        upper = self.local_slots + (1 - (even ^ feat)) * group - (node_count + halo) + rows
        lower = jnp.where(patch == 0, NOWHERE, lower)
        upper = jnp.where(patch == self.patches - 1, NOWHERE, upper)
        place = jnp.where(rows < node_count + 2 * halo, upper, place)
        place = jnp.where(rows < node_count + halo, lower, place)
        return jnp.where(rows < node_count, rows, place)


def lent_list(lists):
    which = (lax.axis_index("feat") + lax.axis_index("patch")) & 1
    return jnp.where(which == 0, lists[0:1], lists[1:2])


def lend_kernel(*refs, share, layout):
    (node_hbm, halo_hbm, coarse_hbm, wa_hbm, send_hbm, recv_hbm, latent_hbm), refs = refs[:7], refs[7:]
    lent_ref, node, halo, coarse, wa, send, recv, latent, own, sems = refs
    rows128 = share // 128
    feat, patch = lax.axis_index("feat"), lax.axis_index("patch")
    mine = pl.ds(pl.multiple_of(feat * rows128, rows128), rows128)
    loads = copies(
        (
            (halo_hbm, halo),
            (coarse_hbm, coarse),
            (node_hbm, node),
            (send_hbm.at[mine, :], send),
            (recv_hbm.at[mine, :], recv),
            (coarse_hbm, own),
            (wa_hbm, wa),
            (latent_hbm.at[pl.ds(pl.multiple_of(feat * share, share), latent.shape[0]), :], latent),
        ),
        sems,
    )
    for copy in loads[:3]:
        copy.wait()
    index_row = jnp.concatenate([lent_list(halo[...]), coarse[...].reshape(1, -1)], axis=1)
    lent_ref[...] = lax.dot_general(
        one_hot_columns(index_row, 0, node.shape[0]),
        node[...],
        (((0,), (0,)), ((), ())),
        preferred_element_type=F32,
    ).astype(BF16)
    for copy in loads[3:6]:
        copy.wait()
    for index in (send, recv):
        index[...] = layout.slots(index[...], patch, feat, own)
    for copy in loads[6:]:
        copy.wait()


def local_part(at, block, latent, send, recv, wa, wb, table, before=None):
    part, some = slice(at, at + block), slice(at // 128, (at + block) // 128)
    half = wa.shape[1]
    width = latent.shape[1]
    slots = table.shape[0] // 2
    picks = jnp.concatenate(
        [one_hot_rows(index_columns(index[some, :]), 0, slots) for index in (send, recv)], axis=1
    )
    picked = [dot(picks, table[:, col : col + half]) for col in (0, half)]
    if before is not None:
        before.wait()
    rows = latent[part, :]
    return jnp.concatenate(
        [0.5 * (some + dot(rows, weight[:width, :])) for some, weight in zip(picked, (wa, wb))], axis=1
    )


def local_kernel(limit_ref, node, wa, wb, send, recv, early_latent, latent_hbm, *refs, layout, block):
    count = (len(refs) - 6) // 2
    more_hbm, refs = refs[:count], refs[count:]
    pre_ref, latent, table, live_ref, *more = refs[: 4 + count]
    sems, block_sems = refs[4 + count :]
    share, width = latent.shape
    half = wa.shape[1]
    feat = lax.axis_index("feat")
    local_slots, used = layout.local_slots, layout.node_count
    first = pre_ref.shape[0]
    blocks = [
        (latent_hbm.at[pl.ds(pl.multiple_of(feat * share + at, block), block), :], latent.at[pl.ds(at, block), :])
        for at in range(block, share, block)
    ]
    wanted = first // block - 1
    early = copies(blocks[:wanted], block_sems)
    latent[:block, :] = early_latent[...]
    for side in range(2):
        base = side * local_slots
        rows = slice((side + 1) * width, (side + 2) * width)
        for weight, col in ((wa, 0), (wb, half)):
            table[base : base + used, col : col + half] = dot(node[...], weight[rows, :]).astype(BF16)
        if used < local_slots:
            table[base + used : base + local_slots, :] = jnp.zeros((local_slots - used, 2 * half), BF16)
    shape = recv.shape
    edge = lax.broadcasted_iota(jnp.int32, shape, 0) * 128 + lax.broadcasted_iota(jnp.int32, shape, 1) + feat * share
    live_ref[...] = jnp.where(edge < limit_ref[...], recv[...], DEAD)
    rest = copies(blocks[wanted:] + list(zip(more_hbm, more)), sems)
    for i, copy in enumerate([None] + early):
        at = i * block
        pre_ref[at : at + block, :] = local_part(at, block, latent, send, recv, wa, wb, table, copy)
    for copy in rest:
        copy.wait()


def second_kernel(latent, send, recv, wa, wb, table, mine, pre_ref, projected, block):
    share, width = latent.shape
    half = wa.shape[1]
    done = share - pre_ref.shape[0]
    group = mine.shape[0]
    for at in range(done, share, block):
        pre_ref[at - done : at - done + block, :] = local_part(at, block, latent, send, recv, wa, wb, table)
    project(mine, wa, wb, projected)


def project(rows, wa, wb, out, at=0):
    group, width = rows.shape
    half = wa.shape[1]
    for side in range(2):
        part = slice((side + 1) * width, (side + 2) * width)
        for weight, col in ((wa, 0), (wb, half)):
            out[at + side * group : at + (side + 1) * group, col : col + half] = (
                0.5 * dot(rows[...], weight[part, :])
            ).astype(BF16)


def edge_kernel(
    pre_ref,
    pre2_ref,
    latent_ref,
    send_ref,
    live_ref,
    mine_table,
    theirs_ref,
    wa_ref,
    wb_ref,
    va_ref,
    vb_ref,
    gain_ref,
    out_other_ref,
    fresh_all,
    group_other_ref,
    table,
    layout,
    block,
):
    share, width = latent_ref.shape
    half = wa_ref.shape[1]
    group = layout.group
    feat = lax.axis_index("feat")
    table[: 2 * group, :] = mine_table[...]
    project(theirs_ref, wa_ref, wb_ref, table, 2 * group)
    gain = gain_ref[...].astype(F32).reshape(1, width)
    for at in range(0, share, block):
        part = slice(at, at + block)
        some = slice(at // 128, (at + block) // 128)
        receivers = live_ref[some, :]
        columns = [index_columns(send_ref[some, :]), index_columns(receivers)]
        first = pre_ref.shape[0]
        pre = pre_ref[part, :] if at < first else pre2_ref[at - first : at - first + block, :]
        picks = jnp.concatenate(
            [
                one_hot_rows(column, base, group)
                for base in (layout.local_slots, layout.local_slots + group)
                for column in columns
            ],
            axis=1,
        )
        hidden = silu_of_double(pre + dot(picks, table[...])).astype(BF16)
        pre = dot(hidden[:, :half], va_ref[...]) + dot(hidden[:, half:], vb_ref[...])
        live = jnp.concatenate(columns[1], axis=0) != DEAD
        fresh = (latent_ref[part, :].astype(F32) + layer_norm(pre, gain, live)).astype(BF16)
        low, high = fresh[:, : width // 2], fresh[:, width // 2 :]
        out_other_ref[part, :] = jnp.where(feat == 0, high, low)
        fresh_all[part, :] = fresh
    receivers = flat_row(live_ref[...])
    group_other_ref[...] = dot(one_hot_columns(receivers, layout.local_slots + group, group), fresh_all[...]).astype(BF16)


def group_sums_kernel(fresh_ref, recv_ref, sums_ref, first):
    sums_ref[...] = dot(one_hot_columns(flat_row(recv_ref[...]), first, sums_ref.shape[0]), fresh_ref[...])


def merge_kernel(mine_ref, theirs_ref, *out_refs):
    at = 0
    for out_ref in out_refs:
        rows = out_ref.shape[0]
        part = slice(at, at + rows)
        out_ref[...] = (mine_ref[part, :] + theirs_ref[part, :].astype(F32)).astype(BF16)
        at += rows


def core_rows_of(edges, core):
    share = edges.shape[0] // 2
    return edges.at[pl.ds(pl.multiple_of(core * share, share), share), :]


def local_sums_kernel(fresh_ref, recv_ref, node_ref, wa_ref, wb_ref, sums_ref, pre_ref, edges_ref, sems):
    width = node_ref.shape[1]
    half = wa_ref.shape[1]
    feat = lax.axis_index("feat")
    columns = pl.ds(pl.multiple_of(feat * half, half), half)
    placed = copies([(fresh_ref.at[:, columns], core_rows_of(edges_ref, feat))], sems)
    sums_ref[...] = dot(one_hot_columns(flat_row(recv_ref[...]), 0, sums_ref.shape[0]), fresh_ref[...])
    for weight, col in ((wa_ref, 0), (wb_ref, half)):
        pre_ref[:, col : col + half] = 0.5 * dot(node_ref[...], weight[:width, :])
    for copy in placed:
        copy.wait()


def beside_kernel(theirs_ref, edges_in_ref, edges_ref, sems):
    for copy in copies([(theirs_ref, core_rows_of(edges_ref, 1 - lax.axis_index("feat")))], sems):
        copy.wait()


def receive_kernel(sums_ref, halo_ref, coarse_ref, *refs):
    *parts, own_ref, rounded_ref = refs
    coarse = coarse_ref.shape[0]
    coarse_row = coarse_ref[...].reshape(1, coarse)
    index_row = jnp.concatenate([lent_list(halo_ref[...])] + [coarse_row] * len(parts), axis=1)
    returned = jnp.concatenate([part[...] for part in parts], axis=0)
    own = sums_ref[...] + dot(one_hot_columns(index_row, 0, own_ref.shape[0]), returned)
    own_ref[...] = own
    rounded_ref[...] = own.astype(BF16)


def node_kernel(node_ref, own_ref, partner_ref, pre_ref, wa_ref, wb_ref, va_ref, vb_ref, gain_ref, out_ref):
    width = node_ref.shape[1]
    half = wa_ref.shape[1]
    feat = lax.axis_index("feat")
    received = (own_ref[...] + partner_ref[...].astype(F32)).astype(BF16)
    total = None
    for weight, second, col in ((wa_ref, va_ref, 0), (wb_ref, vb_ref, half)):
        pre = pre_ref[:, col : col + half] + 0.5 * dot(received, weight[width:, :])
        part = dot(silu_of_double(pre).astype(BF16), second[...])
        total = part if total is None else total + part
    update = layer_norm(total, gain_ref[...].astype(F32).reshape(1, width))
    fresh = (node_ref[...].astype(F32) + update).astype(BF16)
    out_ref[...] = jnp.where(feat == 0, fresh[:, : width // 2], fresh[:, width // 2 :])


def in_hbm(array):
    return pltpu.with_memory_space_constraint(array, pltpu.HBM)


VMEM_SPEC = pl.BlockSpec(memory_space=pltpu.VMEM)
ANY_SPEC = pl.BlockSpec(memory_space=pl.ANY)


def call(kernel, operands, in_specs, outputs, out_specs, flops, limit, scratch=(), aliases=None):
    return pl.pallas_call(
        kernel,
        in_specs=in_specs,
        out_specs=out_specs,
        out_shape=outputs,
        scratch_shapes=list(scratch),
        input_output_aliases=aliases or {},
        cost_estimate=pl.CostEstimate(flops=flops, bytes_accessed=MIB // 4, transcendentals=0),
        compiler_params=pltpu.CompilerParams(vmem_limit_bytes=limit * MIB),
    )(*operands)


def pairing(count, pairs):
    targets = [None] * count
    for p, q in pairs:
        targets[p], targets[q] = q, p
    return targets


def exchange_rounds(count):
    across = [(p + 1 if p % 2 else p - 1) % count for p in range(count)]
    apart = lambda distance: [p ^ distance for p in range(count)]
    rounds = [(apart(1), across)]
    if count == 8:
        mixed = pairing(count, [(0, 3), (4, 7), (1, 6), (2, 5)])
        return rounds + [(apart(4), apart(5)), (apart(2), apart(2)), (apart(6), mixed)]
    return rounds + [(apart(distance), apart(distance + 1)) for distance in range(2, count, 2)]


def exchange_pairs(rounds):
    count = len(rounds[0][0])
    return [
        [(2 * p + feat, 2 * targets[p] + feat) for p in range(count) for feat, targets in enumerate(some)]
        for some in rounds
    ]


def on_device(
    node_latent,
    edge_latent,
    edge_senders,
    edge_receivers,
    halo_rows,
    coarse_rows,
    edge_counts,
    edge_w1,
    edge_w2,
    edge_gain,
    node_w1,
    node_w2,
    node_gain,
):
    node_count, width = node_latent.shape
    half = width // 2
    edge_count = edge_latent.shape[0]
    halo, coarse = halo_rows.shape[1], coarse_rows.shape[0]
    patches = lax.axis_size("patch")
    both = ("patch", "feat")
    rounds = exchange_rounds(patches)
    layout = Layout(rounds, node_count, halo, coarse)
    group, local_slots = layout.group, layout.local_slots
    share = edge_count // 2
    block = 512
    dma = pltpu.SemaphoreType.DMA

    def shape(rows, columns, kind=BF16):
        return jax.ShapeDtypeStruct((rows, columns), kind)

    def like(array):
        return jax.ShapeDtypeStruct(array.shape, array.dtype)

    def swap(values):
        return lax.ppermute(values, "feat", FEAT_SWAP)

    edge_w1_b = swap(edge_w1)

    index_rows = (edge_count // 128, 128)
    core_rows = jax.ShapeDtypeStruct((share // 128, 128), jnp.int32)
    lent, node, halo_lists, coarse_list, w1, send, recv, early_latent = call(
        functools.partial(lend_kernel, share=share, layout=layout),
        [
            in_hbm(array)
            for array in (
                node_latent,
                halo_rows,
                coarse_rows,
                edge_w1,
                edge_senders.reshape(index_rows),
                edge_receivers.reshape(index_rows),
                edge_latent,
            )
        ],
        [ANY_SPEC] * 7,
        [shape(halo + coarse, width)]
        + [like(array) for array in (node_latent, halo_rows, coarse_rows, edge_w1)]
        + [core_rows] * 2
        + [shape(block, width)],
        [VMEM_SPEC] * 8,
        2 * node_count * (halo + coarse) * width,
        8,
        scratch=[pltpu.SMEM((coarse,), jnp.int32), dma((8,))],
    )
    pairs = exchange_pairs(rounds)
    arrived = [
        lax.ppermute(lent[halo:] if i else lent, both, pairs[i]) for i in reversed(range(len(pairs)))
    ][::-1]

    more = (edge_w2, edge_gain, node_w1, node_w2, node_gain)
    first = share // 2
    pre, latent, table, live, w2, e_gain, n_w1, n_w2, n_gain = call(
        functools.partial(local_kernel, layout=layout, block=block),
        [edge_counts.reshape(1, 1), node, w1, edge_w1_b, send, recv, early_latent] + [in_hbm(array) for array in (edge_latent, *more)],
        [VMEM_SPEC] * 7 + [ANY_SPEC] * (1 + len(more)),
        [
            shape(first, width, F32),
            shape(share, width),
            shape(2 * local_slots, width),
            core_rows,
        ]
        + [like(array) for array in more],
        [VMEM_SPEC] * (4 + len(more)),
        (2 * width * width * first + 4 * node_count * width * width + 4 * first * local_slots * width) // BESIDE,
        LIMIT,
        scratch=[dma((len(more) + (share - first) // block,)), dma((first // block,))],
    )
    pre, *arrived = lax.optimization_barrier((pre, *arrived))
    table_mine = jnp.concatenate(arrived, axis=0)
    table_theirs = swap(table_mine)
    edge_w2_b = swap(w2)
    pre2, projected = call(
        functools.partial(second_kernel, block=block),
        [latent, send, recv, w1, edge_w1_b, table, table_mine],
        [VMEM_SPEC] * 7,
        [shape(share - first, width, F32), shape(2 * group, width)],
        [VMEM_SPEC] * 2,
        2 * width * width * (share - first) + 4 * (share - first) * local_slots * width + 4 * group * width * width,
        LIMIT,
    )
    node_w1_b, node_w2_b = swap(n_w1), swap(n_w2)

    other, fresh, group_other = call(
        functools.partial(edge_kernel, layout=layout, block=block),
        (pre, pre2, latent, send, live, projected, table_theirs, w1, edge_w1_b, w2, edge_w2_b, e_gain),
        [VMEM_SPEC] * 12,
        [shape(share, half), shape(share, width), shape(group, width)],
        [VMEM_SPEC] * 3,
        2 * share * width * (width + 6 * group) + 4 * group * width * width,
        LIMIT,
        scratch=[pltpu.VMEM((4 * group, width), BF16)],
    )
    node_w1_b, node_w2_b, other, fresh, group_other = lax.optimization_barrier(
        (node_w1_b, node_w2_b, other, fresh, group_other)
    )

    group_theirs = swap(group_other)
    group_mine = call(
        functools.partial(group_sums_kernel, first=local_slots),
        (fresh, live),
        [VMEM_SPEC] * 2,
        shape(group, width, F32),
        VMEM_SPEC,
        2 * share * width * group,
        16,
    )
    group_mine, other = lax.optimization_barrier((group_mine, other))
    edges_theirs = swap(other)
    sizes = [halo + coarse] + [coarse] * (len(pairs) - 1)
    outgoing = call(
        merge_kernel,
        (group_mine, group_theirs),
        [VMEM_SPEC] * 2,
        [shape(rows, width) for rows in sizes],
        [VMEM_SPEC] * len(sizes),
        group * width,
        8,
    )
    *outgoing, fresh = lax.optimization_barrier((*outgoing, fresh))
    back = [lax.ppermute(outgoing[i], both, pairs[i]) for i in reversed(range(len(pairs)))][::-1]
    local_sums, node_pre, edges = call(
        local_sums_kernel,
        (fresh, live, node, n_w1, node_w1_b),
        [VMEM_SPEC] * 5,
        [shape(node_count, width, F32), shape(node_count, width, F32), shape(edge_count, half)],
        [VMEM_SPEC] * 2 + [ANY_SPEC],
        2 * share * width * node_count // BESIDE,
        16,
        scratch=[dma((1,))],
    )
    local_sums, *back = lax.optimization_barrier((local_sums, *back[::-1]))
    back = back[::-1]
    own, rounded = call(
        receive_kernel,
        (local_sums, halo_lists, coarse_list, *back),
        [VMEM_SPEC] * (3 + len(sizes)),
        [shape(node_count, width, F32), shape(node_count, width)],
        [VMEM_SPEC] * 2,
        2 * node_count * width * group,
        16,
    )
    partner = swap(rounded)
    edges_theirs = lax.optimization_barrier((edges_theirs, rounded))[0]
    edges_out = call(
        beside_kernel,
        (edges_theirs, edges),
        [ANY_SPEC] * 2,
        shape(edge_count, half),
        ANY_SPEC,
        2 * node_count * width * width,
        8,
        scratch=[dma((1,))],
        aliases={1: 0},
    )
    nodes_out = call(
        node_kernel,
        (node, own, partner, node_pre, n_w1, node_w1_b, n_w2, node_w2_b, n_gain),
        [VMEM_SPEC] * 9,
        shape(node_count, half),
        VMEM_SPEC,
        4 * node_count * width * width,
        16,
    )
    return nodes_out, edges_out


def solution(mesh):
    placed = (
        P(("member", "patch"), None),
        P(("member", "patch"), None),
        P(("member", "patch")),
        P(("member", "patch")),
        P(("member", "patch"), None),
        P(("member", "patch")),
        P(("member", "patch")),
        P(None, "feat"),
        P("feat", None),
        P(),
        P(None, "feat"),
        P("feat", None),
        P(),
    )
    return jax.shard_map(
        on_device,
        mesh=mesh,
        in_specs=placed,
        out_specs=(P(("member", "patch"), "feat"), P(("member", "patch"), "feat")),
        check_vma=False,
    )
```
